32 devices in a mesh: row: 4 (over z), col: 8 (over y, x, core).
Axes of the slice: x: 2, y: 2, z: 4, core: 2. Of those that a mesh axis runs over, the one named last changes fastest.
Arguments:
- images: bfloat16 [32, 3, 64, 96], P(('row', 'col')), may hold values from -1000 to 1000
- weights: bfloat16 [16, 24, 128, 1200], P('row', 'col'), may hold values from -0.1875 to 0.1875
Outputs:
- weight_grad: float32 [16, 24, 128, 1200], P('row', 'col')
The draws below stay inside these ranges and needn't reach their ends.
All inputs are finite; a program needn't handle non-finite values.
Results may differ from the reference program's by a relative error of at most 0.006.
Values may be sent and summed in bfloat16 or wider, within the bound.
No kernel may reach another device: no remote copies, remote signals or barrier semaphores. Data moves between devices by JAX's collectives and lax.ppermute only.
A program may use at most 128 MiB of HBM per device.

```python
import math
import jax
import jax.numpy as jnp
from jax import lax

B = 32
CH = 3
S = 4
FIELD = 20
F = 128
PAD = 8
K = 1200
PROWS = 16
PCOLS = 24
HEIGHT = 64
WIDTH = 96


def draw_images(key, part):
    streams = jax.random.split(key, 5)
    log_scale = jax.random.uniform(streams[0], (B, 1, 1, 1), jnp.float32, 0.0, math.log(10.0))
    shifts = jax.random.uniform(streams[1], (B, CH, 1, 1), jnp.float32, -3.0, 3.0)
    row_scale = jnp.exp(jax.random.uniform(streams[2], (B, 1, HEIGHT, 1), jnp.float32, 0.0, math.log(4.0)))
    col_scale = jnp.exp(jax.random.uniform(streams[3], (B, 1, 1, WIDTH), jnp.float32, 0.0, math.log(4.0)))
    jitter = jnp.clip(jax.random.normal(streams[4], (B, CH, HEIGHT, WIDTH), jnp.float32), -6.0, 6.0)
    return (shifts + jnp.exp(log_scale) * row_scale * col_scale * jitter).astype(jnp.bfloat16)


def steps_of(rng, shape, shards, least, largest):
    def one(position, blocks):
        steps = jax.random.uniform(jax.random.fold_in(jax.random.fold_in(rng, 6), position), (blocks,), jnp.float32, least / len(shards), largest / len(shards))
        return jnp.repeat(jnp.exp(steps), shape[position] // blocks).reshape((-1,) + (1,) * (len(shape) - position - 1))

    factor_of = one(*shards[0])
    for cut in shards[1:]:
        factor_of = factor_of * one(*cut)
    return factor_of


def scatter_about(stream_key, shape, scale, most, cuts=(), held_as=jnp.bfloat16):
    result = jax.random.normal(stream_key, shape, jnp.float32) * scale
    if len(cuts) > 0:
        result = steps_of(stream_key, shape, cuts, -0.22, 0.18) * result
    return jnp.clip(result, min=-most, max=most).astype(held_as)


def setup_inputs(seed: int = 0) -> dict:
    seeds = jax.random.split(jax.random.key(seed), 3)
    return {
        "images": draw_images(jax.random.fold_in(seeds[2], 71), 0),
        "weights": scatter_about(seeds[1], (PROWS, PCOLS, F, K), K ** -0.5, 0.1875, ((0, 4), (1, 8))),
    }


sparsity = 0.5

def field_rows(padded, prow):
    band = lax.dynamic_slice_in_dim(padded, prow * S, FIELD, axis=1)
    table = S * jnp.arange(PCOLS, dtype=jnp.int32)[:, None] + jnp.arange(FIELD, dtype=jnp.int32)[None, :]
    picked = band[:, :, table, :]
    picked = jnp.transpose(picked, (2, 0, 1, 3, 4))
    return picked.reshape(PCOLS, K, picked.shape[-1])

def box_sum(values):
    padded = jnp.pad(values, ((1, 1), (1, 1), (0, 0), (0, 0)))
    total = jnp.zeros(values.shape, jnp.float32)
    for down in range(3):
        for across in range(3):
            total = total + padded[down:down + PROWS, across:across + PCOLS]
    return total

def reference(images, weights):
    pixels = images.astype(jnp.float32)
    center = lax.optimization_barrier(jnp.mean(pixels, axis=(1, 2, 3), keepdims=True))
    variance = lax.optimization_barrier(jnp.mean(jnp.square(pixels - center), axis=(1, 2, 3), keepdims=True))
    normed = ((pixels - center) / jnp.sqrt(variance + 1e-05)).astype(jnp.bfloat16)
    plane = jnp.transpose(normed, (1, 2, 3, 0))
    padded = jnp.pad(plane, ((0, 0), (PAD, PAD), (PAD, PAD), (0, 0)))
    positions = jnp.arange(PROWS, dtype=jnp.int32)

    def encode(prow):
        patches = field_rows(padded, prow).astype(jnp.float32)
        return jnp.einsum('qfk,qkb->qfb', weights[prow].astype(jnp.float32), patches).astype(jnp.bfloat16)
    hidden = lax.map(encode, positions)
    squares = jnp.square(hidden.astype(jnp.float32))
    energy = jnp.sqrt(1.0 + box_sum(squares))
    inverse = (1.0 / energy).astype(jnp.bfloat16)
    spread = box_sum(inverse.astype(jnp.float32))
    table = S * jnp.arange(PCOLS, dtype=jnp.int32)[:, None] + jnp.arange(FIELD, dtype=jnp.int32)[None, :]

    def place(total, prow):
        terms = jnp.einsum('qfk,qfb->qkb', weights[prow].astype(jnp.float32), hidden[prow].astype(jnp.float32))
        terms = terms.reshape(PCOLS, CH, FIELD, FIELD, terms.shape[-1]).transpose(1, 2, 0, 3, 4)
        band = lax.dynamic_slice_in_dim(total, prow * S, FIELD, axis=1)
        band = band.at[:, :, table, :].add(terms)
        return (lax.dynamic_update_slice_in_dim(total, band, prow * S, axis=1), None)
    total, _ = lax.scan(place, jnp.zeros(padded.shape, jnp.float32), positions)
    recon = total[:, PAD:PAD + HEIGHT, PAD:PAD + WIDTH]
    residual = (recon - plane.astype(jnp.float32)).astype(jnp.bfloat16)
    resid_pad = jnp.pad(residual, ((0, 0), (PAD, PAD), (PAD, PAD), (0, 0)))

    def gradient(prow):
        image_patches = field_rows(padded, prow).astype(jnp.float32)
        resid_patches = field_rows(resid_pad, prow).astype(jnp.float32)
        weight_row = weights[prow].astype(jnp.float32)
        hidden_row = hidden[prow].astype(jnp.float32)
        back = sparsity * hidden_row * spread[prow] + jnp.einsum('qfk,qkb->qfb', weight_row, resid_patches)
        back = lax.optimization_barrier(back.astype(jnp.bfloat16)).astype(jnp.float32)
        grad = jnp.einsum('qfb,qkb->qfk', back, image_patches) + jnp.einsum('qfb,qkb->qfk', hidden_row, resid_patches)
        return grad / B
    return lax.map(gradient, positions)
```

```python
import functools

import jax
import jax.numpy as jnp
import numpy as np
from jax import lax
from jax.experimental import pallas as pl
from jax.experimental.pallas import tpu as pltpu
from jax.sharding import PartitionSpec as P

CH = 3
S = 4
FIELD = 20
PAD = 8
K = 1200
GROUP = FIELD // S

sparsity = 0.5
f32 = jnp.float32
bf16 = jnp.bfloat16
NT = (((1,), (1,)), ((), ()))
NN = (((1,), (0,)), ((), ()))
TN = (((0,), (0,)), ((), ()))
MIB = 1024 * 1024


def dot(a, b, dims=NN):
    return lax.dot_general(a, b, dims, preferred_element_type=f32)


class Sizes:
    def __init__(self, images, weights, mesh):
        self.R, self.C = mesh.shape["row"], mesh.shape["col"]
        self.bd = images[0]
        self.height, self.width = images[2], images[3]
        self.rd, self.cd, self.F = weights[0], weights[1], weights[2]
        self.B = self.bd * self.R * self.C
        self.h, self.w = S * self.rd, S * self.cd
        self.ext = self.w + 2 * PAD
        self.stride = -(-self.ext // 32) * 32
        self.lanes = S * self.stride
        self.YB = self.rd + 2 * PAD // S
        self.T = CH * self.YB
        assert self.C % 2 == 0 and self.rd >= 4 and self.cd >= 2 and self.lanes == 128
        assert self.height == self.R * self.h and self.width == self.C * self.w


PIECES = ((0, 0, 512, 0, 256), (1, 384, 512, 256, 256), (2, 768, 256, 512, 128))


def one_hot():
    out = []
    for _, first, depth, start, count in PIECES:
        n = np.arange(start, start + count)
        lane = 32 * (n // FIELD) + n % FIELD
        out.append((np.arange(first, first + depth)[:, None] == lane[None, :]).astype(np.float32))
    return [jnp.asarray(m, bf16) for m in out]


def split_kernel(z, images_ref, out_ref, rows_ref, pad_ref):
    margin = PAD // S
    blocks = z.height // S
    n = lax.broadcasted_iota(jnp.int32, (1, z.C * z.lanes), 1)
    column = n // z.lanes
    inner = n % z.lanes
    lane_row = inner // z.stride
    across = inner % z.stride
    source = jnp.where(across < z.ext, z.w * column - PAD + across, -1)
    pixel = lax.broadcasted_iota(jnp.int32, (128, z.C * z.lanes), 0)
    chunks = rows_ref.shape[1]
    rows_ref[...] = jnp.zeros_like(rows_ref)
    for i in range(z.bd):
        pixels = images_ref[i].astype(f32)
        count = CH * z.height * z.width
        center = jnp.sum(pixels) / count
        moved = pixels - center
        variance = jnp.sum(moved * moved) / count
        normed = (moved / jnp.sqrt(variance + 1e-05)).astype(bf16).astype(f32)
        for k in range(chunks):
            stop = min(128, z.width - 128 * k)
            rows_ref[:, k, :, :stop] = normed[:, :, 128 * k : 128 * k + stop]
        total = jnp.zeros((CH * blocks, z.C * z.lanes), f32)
        for k in range(chunks):
            for j in range(S):
                line = jnp.concatenate(
                    [rows_ref[c, k, pl.ds(j, blocks, stride=S), :] for c in range(CH)], axis=0
                ).astype(bf16)
                wanted = jnp.where(lane_row == j, source - 128 * k, -1)
                total = total + dot(line, (pixel == wanted).astype(f32).astype(bf16))
        pad_ref[...] = jnp.zeros_like(pad_ref)
        for c in range(CH):
            pad_ref[c, margin : margin + blocks, :] = total[c * blocks : (c + 1) * blocks]
        for r in range(z.R):
            for q in range(z.C):
                block = [
                    pad_ref[c, z.rd * r : z.rd * r + z.YB, q * z.lanes : (q + 1) * z.lanes]
                    for c in range(CH)
                ]
                out_ref[r * z.C + q, i] = jnp.concatenate(block, axis=0).astype(bf16)


def split(z, images):
    return pl.pallas_call(
        functools.partial(split_kernel, z),
        out_shape=jax.ShapeDtypeStruct((z.R * z.C, z.bd, z.T, z.lanes), bf16),
        in_specs=[pl.BlockSpec(memory_space=pltpu.VMEM)],
        out_specs=pl.BlockSpec(memory_space=pltpu.VMEM),
        scratch_shapes=[
            pltpu.VMEM((CH, -(-z.width // 128), z.height, 128), f32),
            pltpu.VMEM((CH, z.height // S + 2 * PAD // S, z.C * z.lanes), f32),
        ],
        compiler_params=pltpu.CompilerParams(vmem_limit_bytes=32 * MIB),
    )(images)


def shift_tiles(z, tile_of, rolled_ref):
    for t in range(z.T):
        tile = tile_of(t)
        for q in range(z.cd):
            moved = pltpu.roll(tile, z.lanes - S * q, 1) if q else tile
            rolled_ref[q, t] = moved.astype(bf16)


def field_slab(z, p, rolled_ref, slab_ref):
    for q in range(z.cd):
        for c in range(CH):
            for g in range(GROUP):
                at = (c * GROUP + g) * z.lanes
                slab_ref[q * z.B : (q + 1) * z.B, at : at + z.lanes] = rolled_ref[q, c * z.YB + p + g]


def gather_patches(slab_ref, picks, store):
    for half in range(2):
        for m, first, depth, start, count in PIECES:
            low = 1024 * half + first
            depth = min(depth, CH * GROUP * 128 - low)
            store(640 * half + start, count, dot(slab_ref[:, low : low + depth], picks[m][:depth, :]))


def encode_kernel(
    z, moved_ref, weights_ref, a_ref, b_ref, c_ref,
    patch_ref, window_ref, hidden_ref, contrib_ref, up_ref, down_ref,
    rows_ref, rolled_ref, slab_ref, high_ref, low_ref, spot_ref,
):
    p = pl.program_id(0)
    B = z.B
    picks = (a_ref, b_ref, c_ref)

    @pl.when(p == 0)
    def _():
        rows_ref[...] = moved_ref[...].reshape(B * z.T, z.lanes).astype(f32)
        for t in range(z.T):
            tile = rows_ref[pl.ds(t, B, stride=z.T), :]
            window_ref[t] = tile.astype(bf16)
            for q in range(z.cd):
                turned = pltpu.roll(tile, z.lanes - S * q, 1) if q else tile
                rolled_ref[q, t] = turned.astype(bf16)
        contrib_ref[...] = jnp.zeros_like(contrib_ref)
        high_ref[...] = jnp.zeros_like(high_ref)
        low_ref[...] = jnp.zeros_like(low_ref)

    field_slab(z, p, rolled_ref, slab_ref)

    def store(at, count, value):
        patch_ref[0, :, at : at + count] = value.astype(bf16)

    gather_patches(slab_ref, picks, store)
    for q in range(z.cd):
        weight = weights_ref[0, q]
        hidden = dot(patch_ref[0, q * B : (q + 1) * B, :K], weight, NT).astype(bf16)
        hidden_ref[p, q] = hidden
        terms = dot(hidden, weight)
        high = terms.astype(bf16)
        high_ref[q * B : (q + 1) * B, :K] = high
        low_ref[q * B : (q + 1) * B, :K] = (terms - high.astype(f32)).astype(bf16)
    spot_ref[...] = jnp.zeros_like(spot_ref)
    for half in range(2):
        for m, first, depth, start, count in PIECES:
            low = 1024 * half + first
            depth = min(depth, CH * GROUP * 128 - low)
            pick = picks[m][:depth, :]
            at = 640 * half + start
            value = dot(high_ref[:, at : at + count], pick, NT) + dot(low_ref[:, at : at + count], pick, NT)
            spot_ref[:, low : low + depth] += value
    for c in range(CH):
        for g in range(GROUP):
            at = (c * GROUP + g) * z.lanes
            total = spot_ref[:B, at : at + z.lanes]
            for q in range(1, z.cd):
                total = total + pltpu.roll(spot_ref[q * B : (q + 1) * B, at : at + z.lanes], S * q, 1)
            contrib_ref[c * z.YB + p + g] += total

    @pl.when(p == z.rd - 1)
    def _():
        half = z.YB // 2
        for c in range(CH):
            for y in range(half):
                up_ref[c * half + y] = contrib_ref[c * z.YB + y].astype(bf16)
                down_ref[c * half + y] = contrib_ref[c * z.YB + z.YB - half + y].astype(bf16)
        for i in range(2):
            for q in range(z.cd):
                up_ref[CH * half + i * z.cd + q] = hidden_ref[i, q]
                down_ref[CH * half + i * z.cd + q] = hidden_ref[z.rd - 2 + i, q]


def whole(shape):
    return pl.BlockSpec(shape, lambda p: (0,) * len(shape))


def encode(z, moved, weights, picks):
    B, F, L = z.B, z.F, z.lanes
    sent = CH * (z.YB // 2) + 2 * z.cd
    shapes = [
        ((z.rd, z.cd * B, 1280), bf16),
        ((z.T, B, L), bf16),
        ((z.rd, z.cd, B, F), bf16),
        ((z.T, B, L), f32),
        ((sent, B, L), bf16),
        ((sent, B, L), bf16),
    ]
    return pl.pallas_call(
        functools.partial(encode_kernel, z),
        grid=(z.rd,),
        out_shape=[jax.ShapeDtypeStruct(*s) for s in shapes],
        in_specs=[
            whole(moved.shape),
            pl.BlockSpec((1, z.cd, F, K), lambda p: (p, 0, 0, 0)),
        ] + [whole(m.shape) for m in picks],
        out_specs=[pl.BlockSpec((1, z.cd * B, 1280), lambda p: (p, 0, 0))] + [whole(s[0]) for s in shapes[1:]],
        scratch_shapes=[
            pltpu.VMEM((B * z.T, L), f32),
            pltpu.VMEM((z.cd, z.T, B, L), bf16),
            pltpu.VMEM((z.cd * B, CH * GROUP * L), bf16),
            pltpu.VMEM((z.cd * B, 1280), bf16),
            pltpu.VMEM((z.cd * B, 1280), bf16),
            pltpu.VMEM((z.cd * B, CH * GROUP * L), f32),
        ],
        compiler_params=pltpu.CompilerParams(vmem_limit_bytes=48 * MIB),
    )(moved, weights, *picks)


def vmem_call(kernel, shapes, scratch, *args):
    vmem = pl.BlockSpec(memory_space=pltpu.VMEM)
    return pl.pallas_call(
        kernel,
        out_shape=[jax.ShapeDtypeStruct(*s) for s in shapes],
        in_specs=[vmem] * len(args),
        out_specs=[vmem] * len(shapes),
        scratch_shapes=[pltpu.VMEM(*s) for s in scratch],
        compiler_params=pltpu.CompilerParams(vmem_limit_bytes=32 * MIB),
    )(*args)


def is_even():
    return lax.rem(lax.axis_index("col"), 2) == 0


def from_side(z, value, from_left):
    across = lax.broadcasted_iota(jnp.int32, value.shape, 1) % z.stride
    turned = pltpu.roll(value, jnp.where(from_left, z.lanes - z.w, z.w), 1)
    low = jnp.where(from_left, 0, z.w)
    high = jnp.where(from_left, z.ext - z.w, z.ext)
    return jnp.where((across >= low) & (across < high), turned, 0.0)


def rows_kernel(z, contrib_ref, hidden_ref, above_ref, below_ref, sum_ref, tall_ref, send_ref):
    half = z.YB // 2
    for c in range(CH):
        for y in range(z.YB):
            t = c * z.YB + y
            total = contrib_ref[t]
            if y < half:
                total = total + above_ref[c * half + y].astype(f32)
            if y >= z.YB - half:
                total = total + below_ref[c * half + y - (z.YB - half)].astype(f32)
            sum_ref[t] = total
            send_ref[t] = total.astype(bf16)
    for q in range(z.cd):
        for i in range(2):
            tall_ref[i, q] = above_ref[CH * half + i * z.cd + q]
            tall_ref[z.rd + 2 + i, q] = below_ref[CH * half + i * z.cd + q]
        for i in range(z.rd):
            tall_ref[2 + i, q] = hidden_ref[i, q]
    first = jnp.where(is_even(), z.cd - 2, 0)
    for i in range(z.rd + 4):
        for k in range(2):
            send_ref[z.T + 2 * i + k] = tall_ref[i, first + k]


def near_kernel(z, sum_ref, tall_ref, near_ref, out_ref, send_ref):
    even = is_even()
    for t in range(z.T):
        total = sum_ref[t] + from_side(z, near_ref[t].astype(f32), jnp.logical_not(even))
        out_ref[t] = total
        send_ref[t] = total.astype(bf16)
    first = jnp.where(even, 0, z.cd - 2)
    for i in range(z.rd + 4):
        for k in range(2):
            send_ref[z.T + 2 * i + k] = tall_ref[i, first + k]


def far_kernel(z, sum_ref, far_ref, out_ref, send_ref):
    even = is_even()
    for t in range(z.T):
        came = from_side(z, far_ref[t].astype(f32), even)
        out_ref[t] = sum_ref[t] + came
        send_ref[t] = came.astype(bf16)


def pool_kernel(z, tall_ref, near_ref, far_ref, out_ref, wide_ref, inverse_ref):
    even = is_even()
    row0 = lax.axis_index("row") * z.rd - 1
    col0 = lax.axis_index("col") * z.cd - 1
    near_at = jnp.where(even, z.cd + 2, 0)
    far_at = jnp.where(even, 0, z.cd + 2)
    for i in range(z.rd + 4):
        for k in range(2):
            wide_ref[i, near_at + k] = near_ref[z.T + 2 * i + k]
            wide_ref[i, far_at + k] = far_ref[z.T + 2 * i + k]
        for q in range(z.cd):
            wide_ref[i, 2 + q] = tall_ref[i, q]
    for i in range(z.rd + 2):
        columns = []
        for q in range(z.cd + 4):
            parts = [jnp.square(wide_ref[i + d, q].astype(f32)) for d in range(3)]
            columns.append(parts[0] + parts[1] + parts[2])
        for q in range(z.cd + 2):
            energy = jnp.sqrt(1.0 + (columns[q] + columns[q + 1] + columns[q + 2]))
            inverse = (1.0 / energy).astype(bf16).astype(f32)
            row, col = row0 + i, col0 + q
            inside = (row >= 0) & (row < z.R * z.rd) & (col >= 0) & (col < z.C * z.cd)
            inverse_ref[i, q] = inverse * jnp.where(inside, 1.0, 0.0)
    for i in range(z.rd):
        columns = []
        for q in range(z.cd + 2):
            columns.append(inverse_ref[i, q] + inverse_ref[i + 1, q] + inverse_ref[i + 2, q])
        for q in range(z.cd):
            spread = columns[q] + columns[q + 1] + columns[q + 2]
            out_ref[i, q] = sparsity * tall_ref[2 + i, q].astype(f32) * spread


def grad_kernel(
    z, sum_ref, last_ref, window_ref, patch_ref, hidden_ref, pooled_ref, weights_ref, a_ref, b_ref, c_ref,
    out_ref, rolled_ref, slab_ref, resid_ref,
):
    p = pl.program_id(0)
    B = z.B
    picks = (a_ref, b_ref, c_ref)

    @pl.when(p == 0)
    def _():
        from_left = jnp.logical_not(is_even())
        lane = lax.broadcasted_iota(jnp.int32, (1, z.lanes), 1) % z.stride
        x = lax.axis_index("col") * z.w - PAD + lane
        across = ((x >= 0) & (x < z.width)).astype(f32)
        first = lax.axis_index("row") * z.h - PAD
        for c in range(CH):
            for y in range(z.YB):
                t = c * z.YB + y
                recon = sum_ref[t] + from_side(z, last_ref[t].astype(f32), from_left)
                line = first + S * y
                inside = jnp.where((line >= 0) & (line < z.height), across, 0.0)
                tile = ((recon - window_ref[t].astype(f32)) * inside).astype(bf16).astype(f32)
                for q in range(z.cd):
                    turned = pltpu.roll(tile, z.lanes - S * q, 1) if q else tile
                    rolled_ref[q, t] = turned.astype(bf16)

    field_slab(z, p, rolled_ref, slab_ref)

    def store(at, count, value):
        resid_ref[:, at : at + count] = value.astype(bf16)

    gather_patches(slab_ref, picks, store)
    for q in range(z.cd):
        rows = slice(q * B, (q + 1) * B)
        resid = resid_ref[rows, :K]
        back = (pooled_ref[p, q] + dot(resid, weights_ref[0, q], NT)).astype(bf16)
        left = jnp.concatenate([back, hidden_ref[p, q]], axis=0)
        right = jnp.concatenate([patch_ref[0, rows, :K], resid], axis=0)
        out_ref[0, q] = dot(left, right, TN) * (1.0 / B)


def gradient(z, total, last, window, patch, hidden, pooled, weights, picks):
    B, F, L = z.B, z.F, z.lanes
    return pl.pallas_call(
        functools.partial(grad_kernel, z),
        grid=(z.rd,),
        out_shape=jax.ShapeDtypeStruct((z.rd, z.cd, F, K), f32),
        in_specs=[
            whole(total.shape),
            whole(last.shape),
            whole(window.shape),
            pl.BlockSpec((1, z.cd * B, 1280), lambda p: (p, 0, 0)),
            whole(hidden.shape),
            whole(pooled.shape),
            pl.BlockSpec((1, z.cd, F, K), lambda p: (p, 0, 0, 0)),
        ] + [whole(m.shape) for m in picks],
        out_specs=pl.BlockSpec((1, z.cd, F, K), lambda p: (p, 0, 0, 0)),
        scratch_shapes=[
            pltpu.VMEM((z.cd, z.T, B, L), bf16),
            pltpu.VMEM((z.cd * B, CH * GROUP * L), bf16),
            pltpu.VMEM((z.cd * B, 1280), bf16),
        ],
        compiler_params=pltpu.CompilerParams(vmem_limit_bytes=48 * MIB),
    )(total, last, window, patch, hidden, pooled, weights, *picks)


def body(z, images, weights):
    B, L = z.B, z.lanes
    picks = one_hot()
    blocks = split(z, images)
    moved = lax.all_to_all(
        blocks.reshape(z.R * z.C, z.bd * z.T, L), ("row", "col"), split_axis=0, concat_axis=0, tiled=True
    ).reshape(B, z.T, L)
    patch, window, hidden, contrib, up, down = encode(z, moved, weights, picks)

    below_to = [(r, r + 1) for r in range(z.R - 1)]
    above_to = [(r + 1, r) for r in range(z.R - 1)]
    above = lax.ppermute(down, "row", below_to)
    below = lax.ppermute(up, "row", above_to)
    tall = ((z.rd + 4, z.cd, B, z.F), bf16)
    tiles = ((z.T, B, L), f32)
    sent = ((z.T + 2 * (z.rd + 4), B, L), bf16)
    total, tall, send = vmem_call(
        functools.partial(rows_kernel, z), [tiles, tall, sent], [], contrib, hidden, above, below
    )
    swap = [(c, c ^ 1) for c in range(z.C)]
    cross = [(c, c + 1 if c % 2 else c - 1) for c in range(1, z.C - 1)]
    near = lax.ppermute(send, "col", swap)
    total, send = vmem_call(functools.partial(near_kernel, z), [tiles, sent], [], total, tall, near)
    far = lax.ppermute(send, "col", cross)
    total, send = vmem_call(
        functools.partial(far_kernel, z), [tiles, ((z.T, B, L), bf16)], [], total, far
    )
    last = lax.ppermute(send, "col", swap)
    (pooled,) = vmem_call(
        functools.partial(pool_kernel, z),
        [((z.rd, z.cd, B, z.F), f32)],
        [((z.rd + 4, z.cd + 4, B, z.F), bf16), ((z.rd + 2, z.cd + 2, B, z.F), f32)],
        tall, near, far,
    )
    return gradient(z, total, last, window, patch, hidden, pooled, weights, picks)


def solution(mesh):
    def run(images, weights):
        z = Sizes(
            (images.shape[0] // (mesh.shape["row"] * mesh.shape["col"]),) + images.shape[1:],
            (weights.shape[0] // mesh.shape["row"], weights.shape[1] // mesh.shape["col"]) + weights.shape[2:],
            mesh,
        )
        return jax.shard_map(
            functools.partial(body, z),
            mesh=mesh,
            in_specs=(P(("row", "col"), None, None, None), P("row", "col", None, None)),
            out_specs=P("row", "col", None, None),
            check_vma=False,
        )(images, weights)

    return run
```

```python
import functools

import jax
import jax.numpy as jnp
from jax import lax
from jax.experimental import pallas as pl
from jax.experimental.pallas import tpu as pltpu
from jax.sharding import PartitionSpec as P

CH = 3
S = 4
FIELD = 20
PAD = 8
K = 1200
MARGIN = 16
HELD = 2
GROUP = FIELD // S

sparsity = 0.5
f32 = jnp.float32
bf16 = jnp.bfloat16
NT = (((1,), (1,)), ((), ()))
NN = (((1,), (0,)), ((), ()))
TN = (((0,), (0,)), ((), ()))
MIB = 1024 * 1024


def dot(a, b, dims=NN):
    return lax.dot_general(a, b, dims, preferred_element_type=f32)


class Sizes:
    def __init__(self, images, weights, mesh):
        self.R, self.C = mesh.shape["row"], mesh.shape["col"]
        self.bd = images[0]
        self.height, self.width = images[2], images[3]
        self.rd, self.cd, self.F = weights[0], weights[1], weights[2]
        self.B = self.bd * self.R * self.C
        self.h, self.w = S * self.rd, S * self.cd
        self.ext = self.w + 2 * PAD
        self.stride = -(-self.ext // 32) * 32
        self.lanes = S * self.stride
        self.YB = self.rd + 2 * PAD // S
        self.T = CH * self.YB
        self.KW = CH * FIELD * self.stride
        self.per = 128 // self.B
        self.groups = self.rd // self.per
        assert self.B * self.per == 128 and self.groups * self.per == self.rd and self.F == 128
        assert self.C % 2 == 0 and self.R % 2 == 0 and self.rd >= 4 and self.cd >= 2 and self.lanes == 128
        assert self.height == self.R * self.h and self.width == self.C * self.w


def split_kernel(z, images_ref, out_ref, rows_ref, pad_ref):
    margin = PAD // S
    blocks = z.height // S
    n = lax.broadcasted_iota(jnp.int32, (1, z.C * z.lanes), 1)
    column = n // z.lanes
    inner = n % z.lanes
    lane_row = inner // z.stride
    across = inner % z.stride
    source = jnp.where(across < z.ext, z.w * column - PAD + across, -1)
    pixel = lax.broadcasted_iota(jnp.int32, (128, z.C * z.lanes), 0)
    chunks = rows_ref.shape[1]
    rows_ref[...] = jnp.zeros_like(rows_ref)
    for i in range(z.bd):
        pixels = images_ref[i].astype(f32)
        count = CH * z.height * z.width
        center = jnp.sum(pixels) / count
        moved = pixels - center
        variance = jnp.sum(moved * moved) / count
        normed = (moved / jnp.sqrt(variance + 1e-05)).astype(bf16).astype(f32)
        for k in range(chunks):
            stop = min(128, z.width - 128 * k)
            rows_ref[:, k, :, :stop] = normed[:, :, 128 * k : 128 * k + stop]
        total = jnp.zeros((CH * blocks, z.C * z.lanes), f32)
        for k in range(chunks):
            for j in range(S):
                line = jnp.concatenate(
                    [rows_ref[c, k, pl.ds(j, blocks, stride=S), :] for c in range(CH)], axis=0
                ).astype(bf16)
                wanted = jnp.where(lane_row == j, source - 128 * k, -1)
                total = total + dot(line, (pixel == wanted).astype(f32).astype(bf16))
        pad_ref[...] = jnp.zeros_like(pad_ref)
        for c in range(CH):
            pad_ref[c, margin : margin + blocks, :] = total[c * blocks : (c + 1) * blocks]
        for r in range(z.R):
            for q in range(z.C):
                block = [
                    pad_ref[c, z.rd * r : z.rd * r + z.YB, q * z.lanes : (q + 1) * z.lanes]
                    for c in range(CH)
                ]
                out_ref[r * z.C + q, i] = jnp.concatenate(block, axis=0).astype(bf16)


def split(z, images):
    return pl.pallas_call(
        functools.partial(split_kernel, z),
        out_shape=pltpu.VMEM((z.R * z.C, z.bd, z.T, z.lanes), bf16),
        in_specs=[pl.BlockSpec(memory_space=pltpu.VMEM)],
        out_specs=pl.BlockSpec(memory_space=pltpu.VMEM),
        scratch_shapes=[
            pltpu.VMEM((CH, -(-z.width // 128), z.height, 128), f32),
            pltpu.VMEM((CH, z.height // S + 2 * PAD // S, z.C * z.lanes), f32),
        ],
        compiler_params=pltpu.CompilerParams(vmem_limit_bytes=32 * MIB),
    )(images)


def spread_kernel(z, weights_ref, out_ref, rows_ref):
    row = lax.broadcasted_iota(jnp.int32, (z.stride, z.F), 0)
    for q in range(z.cd):
        rows_ref[MARGIN : MARGIN + K, :] = weights_ref[0, q].astype(f32)
        inside = (row >= S * q) & (row < S * q + FIELD)
        for i in range(CH * FIELD):
            at = MARGIN + FIELD * i - S * q
            value = jnp.where(inside, rows_ref[at : at + z.stride, :], 0.0)
            out_ref[0, z.stride * i : z.stride * (i + 1), q * z.F : (q + 1) * z.F] = value.astype(bf16)


def spread_weights(z, weights, first, count, space):
    return pl.pallas_call(
        functools.partial(spread_kernel, z),
        grid=(count,),
        out_shape=space((count, z.KW, z.cd * z.F), bf16),
        in_specs=[pl.BlockSpec((1, z.cd, K, z.F), lambda p: (p + first, 0, 0, 0))],
        out_specs=pl.BlockSpec((1, z.KW, z.cd * z.F), lambda p: (p, 0, 0)),
        scratch_shapes=[pltpu.VMEM((K + 2 * MARGIN, z.F), f32)],
        compiler_params=pltpu.CompilerParams(vmem_limit_bytes=32 * MIB),
    )(weights)


def field(z, p, tiles_ref):
    return jnp.concatenate(
        [tiles_ref[c * z.YB + p + g] for c in range(CH) for g in range(GROUP)], axis=1
    )


def encode_kernel(
    z, moved_ref, first_ref, wide_hbm, window_ref, hidden_ref, contrib_ref, swap_ref, cross_ref, wide_ref, rows_ref, sems
):
    B = z.B
    copies = [pltpu.make_async_copy(wide_hbm.at[p], wide_ref.at[p], sems.at[p]) for p in range(z.rd - HELD)]
    for copy in copies[:2]:
        copy.start()
    rows_ref[...] = moved_ref[...].reshape(B * z.T, z.lanes).astype(f32)
    for t in range(z.T):
        window_ref[t] = rows_ref[pl.ds(t, B, stride=z.T), :].astype(bf16)
    contrib_ref[...] = jnp.zeros_like(contrib_ref)
    for p in range(z.rd):
        if p >= HELD:
            copies[p - HELD].wait()
            if p - HELD + 2 < len(copies):
                copies[p - HELD + 2].start()
        weight = first_ref.at[p] if p < HELD else wide_ref.at[p - HELD]
        hidden = dot(field(z, p, window_ref), weight[...]).astype(bf16)
        for q in range(z.cd):
            hidden_ref[p, q] = hidden[:, q * z.F : (q + 1) * z.F]
        terms = dot(hidden, weight[...], NT)
        for c in range(CH):
            for g in range(GROUP):
                at = (c * GROUP + g) * z.lanes
                contrib_ref[c * z.YB + p + g] += terms[:, at : at + z.lanes]
    half = z.YB // 2
    even = row_is_even()
    for ref, below in ((swap_ref, even), (cross_ref, jnp.logical_not(even))):
        first = jnp.where(below, z.YB - half, 0)
        row = jnp.where(below, z.rd - 2, 0)
        for c in range(CH):
            for y in range(half):
                ref[c * half + y] = contrib_ref[c * z.YB + first + y].astype(bf16)
        for i in range(2):
            for q in range(z.cd):
                ref[CH * half + i * z.cd + q] = hidden_ref[row + i, q]


def encode(z, moved, first, wide):
    B, L = z.B, z.lanes
    vmem = pl.BlockSpec(memory_space=pltpu.VMEM)
    sent = CH * (z.YB // 2) + 2 * z.cd
    shapes = [
        ((z.T, B, L), bf16),
        ((z.rd, z.cd, B, z.F), bf16),
        ((z.T, B, L), f32),
        ((sent, B, L), bf16),
        ((sent, B, L), bf16),
        ((z.rd - HELD, z.KW, z.cd * z.F), bf16),
    ]
    return pl.pallas_call(
        functools.partial(encode_kernel, z),
        out_shape=[pltpu.VMEM(*s) for s in shapes],
        in_specs=[vmem, vmem, pl.BlockSpec(memory_space=pltpu.HBM)],
        out_specs=[vmem] * len(shapes),
        scratch_shapes=[
            pltpu.VMEM((B * z.T, L), f32),
            pltpu.SemaphoreType.DMA((z.rd - HELD,)),
        ],
        compiler_params=pltpu.CompilerParams(vmem_limit_bytes=32 * MIB),
    )(moved, first, pltpu.with_memory_space_constraint(wide, pltpu.HBM))


def turn_fields(z, tile_of, flat_ref):
    for group in range(z.groups):
        for c in range(CH):
            for g in range(GROUP):
                first = c * z.YB + group * z.per + g
                stack = jnp.concatenate([tile_of(first + p) for p in range(z.per)], axis=0)
                at = (c * GROUP + g) * z.lanes
                flat_ref[group, at : at + z.lanes, :] = stack.astype(f32).T


def place_fields(z, q, flat_ref, dense_ref, out_ref):
    for group in range(z.groups):
        for i in range(CH * FIELD):
            at = z.stride * i + S * q
            dense_ref[FIELD * i : FIELD * (i + 1), :] = flat_ref[group, at : at + FIELD, :]
        out_ref[q, group] = dense_ref[...].astype(bf16)


def patches_kernel(z, window_ref, out_ref, flat_ref, dense_ref):
    turn_fields(z, lambda t: window_ref[t], flat_ref)
    for q in range(z.cd):
        place_fields(z, q, flat_ref, dense_ref, out_ref)


def vmem_call(kernel, shapes, scratch, *args):
    vmem = pl.BlockSpec(memory_space=pltpu.VMEM)
    return pl.pallas_call(
        kernel,
        out_shape=[pltpu.VMEM(*s) for s in shapes],
        in_specs=[vmem] * len(args),
        out_specs=[vmem] * len(shapes),
        scratch_shapes=[pltpu.VMEM(*s) for s in scratch],
        compiler_params=pltpu.CompilerParams(vmem_limit_bytes=32 * MIB),
    )(*args)


def is_even():
    return lax.rem(lax.axis_index("col"), 2) == 0


def row_is_even():
    return lax.rem(lax.axis_index("row"), 2) == 0


def pack_side(z, to_right, first, second):
    wide = 2 * PAD
    across = lax.broadcasted_iota(jnp.int32, first.shape, 1) % z.stride
    low = pltpu.roll(first, jnp.where(to_right, z.lanes - z.w, 0), 1)
    high = pltpu.roll(second, jnp.where(to_right, z.lanes - z.w + wide, wide) % z.lanes, 1)
    return jnp.where(across < wide, low, jnp.where(across < 2 * wide, high, 0.0))


def unpack_side(z, from_left, packed):
    wide = 2 * PAD
    across = lax.broadcasted_iota(jnp.int32, packed.shape, 1) % z.stride
    start = jnp.where(from_left, 0, z.w)
    inside = (across >= start) & (across < start + wide)
    first = pltpu.roll(packed, start, 1)
    second = pltpu.roll(packed, (start + z.lanes - wide) % z.lanes, 1)
    return jnp.where(inside, first, 0.0), jnp.where(inside, second, 0.0)


def rows_kernel(z, contrib_ref, hidden_ref, swap_ref, cross_ref, sum_ref, tall_ref, send_ref):
    half = z.YB // 2
    sum_ref[...] = contrib_ref[...]
    for i in range(z.rd):
        for q in range(z.cd):
            tall_ref[2 + i, q] = hidden_ref[i, q]
    row = lax.axis_index("row")
    even_row = row_is_even()
    for ref, below in ((swap_ref, even_row), (cross_ref, jnp.logical_not(even_row))):
        exists = jnp.where(below, row < z.R - 1, row > 0)
        first = jnp.where(below, z.YB - half, 0)
        at = jnp.where(below, z.rd + 2, 0)
        for c in range(CH):
            for y in range(half):
                sum_ref[c * z.YB + first + y] += jnp.where(exists, ref[c * half + y].astype(f32), 0.0)
        for i in range(2):
            for q in range(z.cd):
                value = ref[CH * half + i * z.cd + q]
                tall_ref[at + i, q] = jnp.where(exists, value, jnp.zeros_like(value))
    even = is_even()
    for t in range(0, z.T, 2):
        send_ref[t // 2] = pack_side(z, even, sum_ref[t], sum_ref[t + 1]).astype(bf16)
    first = jnp.where(even, z.cd - 2, 0)
    for i in range(z.rd + 4):
        for k in range(2):
            send_ref[z.T // 2 + 2 * i + k] = tall_ref[i, first + k]


def near_kernel(z, sum_ref, tall_ref, near_ref, out_ref, send_ref):
    even = is_even()
    for t in range(0, z.T, 2):
        came = unpack_side(z, jnp.logical_not(even), near_ref[t // 2].astype(f32))
        total = [sum_ref[t + k] + came[k] for k in range(2)]
        for k in range(2):
            out_ref[t + k] = total[k]
        send_ref[t // 2] = pack_side(z, jnp.logical_not(even), *total).astype(bf16)
    first = jnp.where(even, 0, z.cd - 2)
    for i in range(z.rd + 4):
        for k in range(2):
            send_ref[z.T // 2 + 2 * i + k] = tall_ref[i, first + k]


def far_kernel(z, sum_ref, far_ref, out_ref, send_ref):
    even = is_even()
    exists = jnp.where(even, lax.axis_index("col") > 0, lax.axis_index("col") < z.C - 1)
    for t in range(0, z.T, 2):
        came = unpack_side(z, even, jnp.where(exists, far_ref[t // 2].astype(f32), 0.0))
        for k in range(2):
            out_ref[t + k] = sum_ref[t + k] + came[k]
        send_ref[t // 2] = pack_side(z, even, *came).astype(bf16)


def pool_kernel(z, tall_ref, near_ref, far_ref, out_ref, wide_ref, inverse_ref):
    even = is_even()
    row0 = lax.axis_index("row") * z.rd - 1
    col0 = lax.axis_index("col") * z.cd - 1
    near_at = jnp.where(even, z.cd + 2, 0)
    far_at = jnp.where(even, 0, z.cd + 2)
    exists = jnp.where(even, lax.axis_index("col") > 0, lax.axis_index("col") < z.C - 1)
    for i in range(z.rd + 4):
        for k in range(2):
            wide_ref[i, near_at + k] = near_ref[z.T // 2 + 2 * i + k]
            far = far_ref[z.T // 2 + 2 * i + k]
            wide_ref[i, far_at + k] = jnp.where(exists, far, jnp.zeros_like(far))
        for q in range(z.cd):
            wide_ref[i, 2 + q] = tall_ref[i, q]
    for i in range(z.rd + 2):
        columns = []
        for q in range(z.cd + 4):
            parts = [jnp.square(wide_ref[i + d, q].astype(f32)) for d in range(3)]
            columns.append(parts[0] + parts[1] + parts[2])
        for q in range(z.cd + 2):
            energy = jnp.sqrt(1.0 + (columns[q] + columns[q + 1] + columns[q + 2]))
            inverse = (1.0 / energy).astype(bf16).astype(f32)
            row, col = row0 + i, col0 + q
            inside = (row >= 0) & (row < z.R * z.rd) & (col >= 0) & (col < z.C * z.cd)
            inverse_ref[i, q] = inverse * jnp.where(inside, 1.0, 0.0)
    for i in range(z.rd):
        columns = []
        for q in range(z.cd + 2):
            columns.append(inverse_ref[i, q] + inverse_ref[i + 1, q] + inverse_ref[i + 2, q])
        for q in range(z.cd):
            spread = columns[q] + columns[q + 1] + columns[q + 2]
            out_ref[i, q] = sparsity * tall_ref[2 + i, q].astype(f32) * spread


CHUNKS = 3


def grad_kernel(
    z, sum_ref, last_ref, window_ref, patch_ref, hidden_ref, pooled_ref, first_ref, wide_ref,
    out_hbm, resid_ref, flat_ref, dense_ref, resid_patch_ref, factor_ref, out_ref, sems,
):
    B, F = z.B, z.F
    from_left = jnp.logical_not(is_even())
    lane = lax.broadcasted_iota(jnp.int32, (1, z.lanes), 1) % z.stride
    x = lax.axis_index("col") * z.w - PAD + lane
    across = ((x >= 0) & (x < z.width)).astype(f32)
    first = lax.axis_index("row") * z.h - PAD
    for t in range(0, z.T, 2):
        came = unpack_side(z, from_left, last_ref[t // 2].astype(f32))
        for n in range(2):
            line = first + S * ((t + n) % z.YB)
            inside = jnp.where((line >= 0) & (line < z.height), across, 0.0)
            recon = sum_ref[t + n] + came[n]
            resid_ref[t + n] = ((recon - window_ref[t + n].astype(f32)) * inside).astype(bf16)

    turn_fields(z, lambda t: resid_ref[t], flat_ref)
    factor_ref[...] = jnp.zeros_like(factor_ref)
    size = K // CHUNKS
    copies = []
    for q in range(z.cd):
        for p in range(z.rd):
            weight = first_ref.at[p] if p < HELD else wide_ref.at[p - HELD]
            back = dot(field(z, p, resid_ref), weight[:, q * F : (q + 1) * F])
            group, inner = p // z.per, p % z.per
            columns = slice(inner * F, (inner + 1) * F)
            at = inner * B
            factor_ref[q, group, at : at + B, columns] = (pooled_ref[p, q] + back).astype(bf16)
            factor_ref[q, group, 128 + at : 128 + at + B, columns] = hidden_ref[p, q]
        place_fields(z, q, flat_ref, dense_ref, resid_patch_ref)
        for k in range(CHUNKS):
            rows = slice(k * size, (k + 1) * size)
            for group in range(z.groups):
                both = jnp.concatenate([patch_ref[q, group, rows, :], resid_patch_ref[q, group, rows, :]], axis=1)
                value = dot(both, factor_ref[q, group]) * (1.0 / B)
                for inner in range(z.per):
                    out_ref[group * z.per + inner, q, rows, :] = value[:, inner * F : (inner + 1) * F]
            copy = pltpu.make_async_copy(out_ref.at[:, q, rows, :], out_hbm.at[:, q, rows, :], sems.at[q, k])
            copy.start()
            copies.append(copy)
    for copy in copies:
        copy.wait()


def gradient(z, *args):
    B, F, L = z.B, z.F, z.lanes
    return pl.pallas_call(
        functools.partial(grad_kernel, z),
        out_shape=pltpu.HBM((z.rd, z.cd, K, F), f32),
        in_specs=[pl.BlockSpec(memory_space=pltpu.VMEM)] * len(args),
        out_specs=pl.BlockSpec(memory_space=pltpu.HBM),
        scratch_shapes=[
            pltpu.VMEM((z.T, B, L), bf16),
            pltpu.VMEM((z.groups, z.KW, 128), f32),
            pltpu.VMEM((K, 128), f32),
            pltpu.VMEM((z.cd, z.groups, K, 128), bf16),
            pltpu.VMEM((z.cd, z.groups, 256, z.per * F), bf16),
            pltpu.VMEM((z.rd, z.cd, K, F), f32),
            pltpu.SemaphoreType.DMA((z.cd, CHUNKS)),
        ],
        compiler_params=pltpu.CompilerParams(vmem_limit_bytes=40 * MIB),
    )(*args)


def exchange(z, value, partner):
    pairs = []
    for r in range(z.R):
        for c in range(z.C):
            to = partner(z, r, c)
            pairs.append((r * z.C + c, to[0] * z.C + to[1]))
    return lax.ppermute(value, ("row", "col"), pairs)


def cross_row(z, r, c):
    to = r + 1 if r % 2 else r - 1
    return (to, c) if 0 <= to < z.R else (r, c ^ 1)


def swap_col(z, r, c):
    return (r, c ^ 1)


def cross_col(z, r, c):
    to = c + 1 if c % 2 else c - 1
    return (r, to) if 0 <= to < z.C else (r ^ 1, c)


def body(z, images, weights):
    B, L = z.B, z.lanes
    tiles = ((z.T, B, L), f32)
    blocks = split(z, images)
    moved = lax.all_to_all(
        blocks.reshape(z.R * z.C, z.bd * z.T, L), ("row", "col"), split_axis=0, concat_axis=0, tiled=True
    ).reshape(B, z.T, L)
    turned = jnp.swapaxes(weights, 2, 3)
    wide_first = spread_weights(z, turned, 0, HELD, pltpu.VMEM)
    wide = spread_weights(z, turned, HELD, z.rd - HELD, pltpu.HBM)
    window, hidden, contrib, to_swap, to_cross, wide = encode(z, moved, wide_first, wide)
    crossed = exchange(z, to_cross, cross_row)
    swapped = exchange(z, to_swap, lambda z, r, c: (r ^ 1, c))
    tall = ((z.rd + 4, z.cd, B, z.F), bf16)
    sent = ((z.T // 2 + 2 * (z.rd + 4), B, L), bf16)
    total, tall, send = vmem_call(
        functools.partial(rows_kernel, z), [tiles, tall, sent], [], contrib, hidden, swapped, crossed
    )
    near = exchange(z, send, swap_col)
    total, send = vmem_call(functools.partial(near_kernel, z), [tiles, sent], [], total, tall, near)
    far = exchange(z, send, cross_col)
    total, send = vmem_call(
        functools.partial(far_kernel, z), [tiles, ((z.T // 2, B, L), bf16)], [], total, far
    )
    last = exchange(z, send, swap_col)
    (pooled,) = vmem_call(
        functools.partial(pool_kernel, z),
        [((z.rd, z.cd, B, z.F), f32)],
        [((z.rd + 4, z.cd + 4, B, z.F), bf16), ((z.rd + 2, z.cd + 2, B, z.F), f32)],
        tall, near, far,
    )
    (patch,) = vmem_call(
        functools.partial(patches_kernel, z),
        [((z.cd, z.groups, K, 128), bf16)],
        [((z.groups, z.KW, 128), f32), ((K, 128), f32)],
        window,
    )
    return jnp.swapaxes(gradient(z, total, last, window, patch, hidden, pooled, wide_first, wide), 2, 3)


def solution(mesh):
    def run(images, weights):
        z = Sizes(
            (images.shape[0] // (mesh.shape["row"] * mesh.shape["col"]),) + images.shape[1:],
            (weights.shape[0] // mesh.shape["row"], weights.shape[1] // mesh.shape["col"]) + weights.shape[2:],
            mesh,
        )
        return jax.shard_map(
            functools.partial(body, z),
            mesh=mesh,
            in_specs=(P(("row", "col"), None, None, None), P("row", "col", None, None)),
            out_specs=P("row", "col", None, None),
            check_vma=False,
        )(images, weights)

    return run
```

```python
import functools

import jax
import jax.numpy as jnp
from jax import lax
from jax.experimental import pallas as pl
from jax.experimental.pallas import tpu as pltpu
from jax.sharding import PartitionSpec as P

CH = 3
S = 4
FIELD = 20
PAD = 8
K = 1200
MARGIN = 16
HELD = 2
GROUP = FIELD // S

sparsity = 0.5
f32 = jnp.float32
bf16 = jnp.bfloat16
NT = (((1,), (1,)), ((), ()))
NN = (((1,), (0,)), ((), ()))
TN = (((0,), (0,)), ((), ()))
MIB = 1024 * 1024


def dot(a, b, dims=NN):
    return lax.dot_general(a, b, dims, preferred_element_type=f32)


class Sizes:
    def __init__(self, images, weights, mesh):
        self.R, self.C = mesh.shape["row"], mesh.shape["col"]
        self.bd = images[0]
        self.height, self.width = images[2], images[3]
        self.rd, self.cd, self.F = weights[0], weights[1], weights[2]
        self.B = self.bd * self.R * self.C
        self.h, self.w = S * self.rd, S * self.cd
        self.ext = self.w + 2 * PAD
        self.stride = -(-self.ext // 32) * 32
        self.lanes = S * self.stride
        self.YB = self.rd + 2 * PAD // S
        self.T = CH * self.YB
        self.KW = CH * FIELD * self.stride
        self.per = 128 // self.B
        self.groups = self.rd // self.per
        assert self.B * self.per == 128 and self.groups * self.per == self.rd and self.F == 128
        assert self.C % 2 == 0 and self.R % 2 == 0 and self.rd >= 4 and self.cd >= 2 and self.lanes == 128
        assert self.height == self.R * self.h and self.width == self.C * self.w


def split_kernel(z, images_hbm, out_hbm, images_ref, rows_ref, pad_ref, pick_ref, out_ref, in_sem, out_sems):
    load = pltpu.make_async_copy(images_hbm, images_ref, in_sem)
    load.start()
    margin = PAD // S
    blocks = z.height // S
    n = lax.broadcasted_iota(jnp.int32, (1, z.C * z.lanes), 1)
    column = n // z.lanes
    inner = n % z.lanes
    lane_row = inner // z.stride
    across = inner % z.stride
    source = jnp.where(across < z.ext, z.w * column - PAD + across, -1)
    pixel = lax.broadcasted_iota(jnp.int32, (128, z.C * z.lanes), 0)
    chunks = rows_ref.shape[1]
    for k in range(chunks):
        for j in range(S):
            wanted = jnp.where(lane_row == j, source - 128 * k, -1)
            pick_ref[k, j] = (pixel == wanted).astype(f32).astype(bf16)
    rows_ref[...] = jnp.zeros_like(rows_ref)
    pad_ref[...] = jnp.zeros_like(pad_ref)
    load.wait()
    for i in range(z.bd):
        pixels = images_ref[i].astype(f32)
        count = CH * z.height * z.width
        center = jnp.sum(pixels) / count
        moved = pixels - center
        variance = jnp.sum(moved * moved) / count
        normed = (moved / jnp.sqrt(variance + 1e-05)).astype(bf16).astype(f32)
        for k in range(chunks):
            stop = min(128, z.width - 128 * k)
            rows_ref[:, k, :, :stop] = normed[:, :, 128 * k : 128 * k + stop]
        total = jnp.zeros((CH * blocks, z.C * z.lanes), f32)
        for k in range(chunks):
            for j in range(S):
                line = jnp.concatenate(
                    [rows_ref[c, k, pl.ds(j, blocks, stride=S), :] for c in range(CH)], axis=0
                ).astype(bf16)
                total = total + dot(line, pick_ref[k, j])
        for c in range(CH):
            pad_ref[c, margin : margin + blocks, :] = total[c * blocks : (c + 1) * blocks]
        for r in range(z.R):
            for q in range(z.C):
                block = [
                    pad_ref[c, z.rd * r : z.rd * r + z.YB, q * z.lanes : (q + 1) * z.lanes]
                    for c in range(CH)
                ]
                out_ref[r * z.C + q, i] = jnp.concatenate(block, axis=0).astype(bf16)
            if i == z.bd - 1:
                part = pl.ds(r * z.C, z.C)
                pltpu.make_async_copy(out_ref.at[part], out_hbm.at[part], out_sems.at[r]).start()
    for r in range(z.R):
        part = pl.ds(r * z.C, z.C)
        pltpu.make_async_copy(out_ref.at[part], out_hbm.at[part], out_sems.at[r]).wait()


def split(z, images):
    shape = (z.R * z.C, z.bd, z.T, z.lanes)
    return pl.pallas_call(
        functools.partial(split_kernel, z),
        out_shape=pltpu.HBM(shape, bf16),
        in_specs=[pl.BlockSpec(memory_space=pltpu.HBM)],
        out_specs=pl.BlockSpec(memory_space=pltpu.HBM),
        scratch_shapes=[
            pltpu.VMEM((z.bd, CH, z.height, z.width), bf16),
            pltpu.VMEM((CH, -(-z.width // 128), z.height, 128), f32),
            pltpu.VMEM((CH, z.height // S + 2 * PAD // S, z.C * z.lanes), f32),
            pltpu.VMEM((-(-z.width // 128), S, 128, z.C * z.lanes), bf16),
            pltpu.VMEM(shape, bf16),
            pltpu.SemaphoreType.DMA,
            pltpu.SemaphoreType.DMA((z.R,)),
        ],
        compiler_params=pltpu.CompilerParams(vmem_limit_bytes=32 * MIB),
    )(pltpu.with_memory_space_constraint(images, pltpu.HBM))


def spread_kernel(z, weights_ref, out_ref, rows_ref):
    row = lax.broadcasted_iota(jnp.int32, (z.stride, z.F), 0)
    for q in range(z.cd):
        rows_ref[MARGIN : MARGIN + K, :] = weights_ref[0, q].astype(f32)
        inside = (row >= S * q) & (row < S * q + FIELD)
        for i in range(CH * FIELD):
            at = MARGIN + FIELD * i - S * q
            value = jnp.where(inside, rows_ref[at : at + z.stride, :], 0.0)
            out_ref[0, z.stride * i : z.stride * (i + 1), q * z.F : (q + 1) * z.F] = value.astype(bf16)


def spread_weights(z, weights, first, count, space):
    return pl.pallas_call(
        functools.partial(spread_kernel, z),
        grid=(count,),
        out_shape=space((count, z.KW, z.cd * z.F), bf16),
        in_specs=[pl.BlockSpec((1, z.cd, K, z.F), lambda p: (p + first, 0, 0, 0))],
        out_specs=pl.BlockSpec((1, z.KW, z.cd * z.F), lambda p: (p, 0, 0)),
        scratch_shapes=[pltpu.VMEM((K + 2 * MARGIN, z.F), f32)],
        compiler_params=pltpu.CompilerParams(vmem_limit_bytes=32 * MIB),
    )(weights)


def field(z, p, tiles_ref):
    return jnp.concatenate(
        [tiles_ref[c * z.YB + p + g] for c in range(CH) for g in range(GROUP)], axis=1
    )


def encode_kernel(
    z, moved_ref, first_ref, wide_hbm, window_ref, hidden_ref, contrib_ref, swap_ref, cross_ref, wide_ref, rows_ref, sems
):
    B = z.B
    copies = [pltpu.make_async_copy(wide_hbm.at[p], wide_ref.at[p], sems.at[p]) for p in range(z.rd - HELD)]
    for copy in copies[:2]:
        copy.start()
    rows_ref[...] = moved_ref[...].reshape(B * z.T, z.lanes).astype(f32)
    for t in range(z.T):
        window_ref[t] = rows_ref[pl.ds(t, B, stride=z.T), :].astype(bf16)
    contrib_ref[...] = jnp.zeros_like(contrib_ref)
    for first in range(0, z.rd, HELD):
        rows = range(first, min(first + HELD, z.rd))
        for p in rows:
            if p >= HELD:
                copies[p - HELD].wait()
                if p - HELD + 2 < len(copies):
                    copies[p - HELD + 2].start()
        weight = [first_ref.at[p] if p < HELD else wide_ref.at[p - HELD] for p in rows]
        hidden = [dot(field(z, p, window_ref), w[...]).astype(bf16) for p, w in zip(rows, weight)]
        terms = [dot(h, w[...], NT) for h, w in zip(hidden, weight)]
        for p, h, value in zip(rows, hidden, terms):
            for q in range(z.cd):
                hidden_ref[p, q] = h[:, q * z.F : (q + 1) * z.F]
            for c in range(CH):
                for g in range(GROUP):
                    at = (c * GROUP + g) * z.lanes
                    contrib_ref[c * z.YB + p + g] += value[:, at : at + z.lanes]
    half = z.YB // 2
    even = row_is_even()
    for ref, below in ((swap_ref, even), (cross_ref, jnp.logical_not(even))):
        first = jnp.where(below, z.YB - half, 0)
        row = jnp.where(below, z.rd - 2, 0)
        for c in range(CH):
            for y in range(half):
                ref[c * half + y] = contrib_ref[c * z.YB + first + y].astype(bf16)
        for i in range(2):
            for q in range(z.cd):
                ref[CH * half + i * z.cd + q] = hidden_ref[row + i, q]


def encode(z, moved, first, wide):
    B, L = z.B, z.lanes
    vmem = pl.BlockSpec(memory_space=pltpu.VMEM)
    sent = CH * (z.YB // 2) + 2 * z.cd
    shapes = [
        ((z.T, B, L), bf16),
        ((z.rd, z.cd, B, z.F), bf16),
        ((z.T, B, L), f32),
        ((sent, B, L), bf16),
        ((sent, B, L), bf16),
        ((z.rd - HELD, z.KW, z.cd * z.F), bf16),
    ]
    return pl.pallas_call(
        functools.partial(encode_kernel, z),
        out_shape=[pltpu.VMEM(*s) for s in shapes],
        in_specs=[vmem, vmem, pl.BlockSpec(memory_space=pltpu.HBM)],
        out_specs=[vmem] * len(shapes),
        scratch_shapes=[
            pltpu.VMEM((B * z.T, L), f32),
            pltpu.SemaphoreType.DMA((z.rd - HELD,)),
        ],
        compiler_params=pltpu.CompilerParams(vmem_limit_bytes=32 * MIB),
    )(moved, first, pltpu.with_memory_space_constraint(wide, pltpu.HBM))


def turn_fields(z, tile_of, flat_ref):
    for group in range(z.groups):
        for c in range(CH):
            for g in range(GROUP):
                first = c * z.YB + group * z.per + g
                stack = jnp.concatenate([tile_of(first + p) for p in range(z.per)], axis=0)
                at = (c * GROUP + g) * z.lanes
                flat_ref[group, at : at + z.lanes, :] = stack.astype(f32).T


def place_fields(z, q, c, flat_ref, dense_ref, out_ref):
    rows = slice(c * FIELD * FIELD, (c + 1) * FIELD * FIELD)
    for group in range(z.groups):
        for i in range(c * FIELD, (c + 1) * FIELD):
            at = z.stride * i + S * q
            dense_ref[FIELD * i : FIELD * (i + 1), :] = flat_ref[group, at : at + FIELD, :]
        out_ref[q, group, rows, :] = dense_ref[rows, :].astype(bf16)


def patches_kernel(z, window_ref, out_ref, flat_ref, dense_ref):
    turn_fields(z, lambda t: window_ref[t], flat_ref)
    for q in range(z.cd):
        for c in range(CH):
            place_fields(z, q, c, flat_ref, dense_ref, out_ref)


def vmem_call(kernel, shapes, scratch, *args):
    vmem = pl.BlockSpec(memory_space=pltpu.VMEM)
    return pl.pallas_call(
        kernel,
        out_shape=[pltpu.VMEM(*s) for s in shapes],
        in_specs=[vmem] * len(args),
        out_specs=[vmem] * len(shapes),
        scratch_shapes=[pltpu.VMEM(*s) for s in scratch],
        compiler_params=pltpu.CompilerParams(vmem_limit_bytes=32 * MIB),
    )(*args)


def is_even():
    return lax.rem(lax.axis_index("col"), 2) == 0


def row_is_even():
    return lax.rem(lax.axis_index("row"), 2) == 0


def pack_side(z, to_right, first, second):
    wide = 2 * PAD
    across = lax.broadcasted_iota(jnp.int32, first.shape, 1) % z.stride
    low = pltpu.roll(first, jnp.where(to_right, z.lanes - z.w, 0), 1)
    high = pltpu.roll(second, jnp.where(to_right, z.lanes - z.w + wide, wide) % z.lanes, 1)
    return jnp.where(across < wide, low, jnp.where(across < 2 * wide, high, 0.0))


def unpack_side(z, from_left, packed):
    wide = 2 * PAD
    across = lax.broadcasted_iota(jnp.int32, packed.shape, 1) % z.stride
    start = jnp.where(from_left, 0, z.w)
    inside = (across >= start) & (across < start + wide)
    first = pltpu.roll(packed, start, 1)
    second = pltpu.roll(packed, (start + z.lanes - wide) % z.lanes, 1)
    return jnp.where(inside, first, 0.0), jnp.where(inside, second, 0.0)


def rows_kernel(z, contrib_ref, hidden_ref, swap_ref, cross_ref, sum_ref, tall_ref, send_ref):
    half = z.YB // 2
    sum_ref[...] = contrib_ref[...]
    row = lax.axis_index("row")
    even_row = row_is_even()
    above_exists, below_exists = row > 0, row < z.R - 1
    for ref, below in ((swap_ref, even_row), (cross_ref, jnp.logical_not(even_row))):
        exists = jnp.where(below, below_exists, above_exists)
        first = jnp.where(below, z.YB - half, 0)
        for c in range(CH):
            for y in range(half):
                sum_ref[c * z.YB + first + y] += jnp.where(exists, ref[c * half + y].astype(f32), 0.0)
    even = is_even()
    for t in range(0, z.T, 2):
        send_ref[t // 2] = pack_side(z, even, sum_ref[t], sum_ref[t + 1]).astype(bf16)
    for q in range(z.cd):
        squares = [jnp.square(hidden_ref[i, q].astype(f32)) for i in range(z.rd)]
        above, below = [], []
        for i in range(2):
            swapped = swap_ref[CH * half + i * z.cd + q].astype(f32)
            crossed = cross_ref[CH * half + i * z.cd + q].astype(f32)
            upper = jnp.where(above_exists, jnp.where(even_row, crossed, swapped), 0.0)
            lower = jnp.where(below_exists, jnp.where(even_row, swapped, crossed), 0.0)
            above.append(jnp.square(upper))
            below.append(jnp.square(lower))
        squares = above + squares + below
        for i in range(z.rd + 2):
            tall_ref[i, q] = squares[i] + squares[i + 1] + squares[i + 2]
    first = jnp.where(even, z.cd - 2, 0)
    for i in range(z.rd + 2):
        for k in range(2):
            send_ref[z.T // 2 + 2 * i + k] = tall_ref[i, first + k].astype(bf16)


def near_kernel(z, sum_ref, tall_ref, near_ref, out_ref, send_ref):
    even = is_even()
    for t in range(0, z.T, 2):
        came = unpack_side(z, jnp.logical_not(even), near_ref[t // 2].astype(f32))
        total = [sum_ref[t + k] + came[k] for k in range(2)]
        for k in range(2):
            out_ref[t + k] = total[k]
        send_ref[t // 2] = pack_side(z, jnp.logical_not(even), *total).astype(bf16)
    first = jnp.where(even, 0, z.cd - 2)
    for i in range(z.rd + 2):
        for k in range(2):
            send_ref[z.T // 2 + 2 * i + k] = tall_ref[i, first + k].astype(bf16)


def far_kernel(z, sum_ref, far_ref, out_ref, send_ref):
    even = is_even()
    exists = jnp.where(even, lax.axis_index("col") > 0, lax.axis_index("col") < z.C - 1)
    for t in range(0, z.T, 2):
        came = unpack_side(z, even, jnp.where(exists, far_ref[t // 2].astype(f32), 0.0))
        for k in range(2):
            out_ref[t + k] = sum_ref[t + k] + came[k]
        send_ref[t // 2] = pack_side(z, even, *came).astype(bf16)


def pool_kernel(z, hidden_ref, tall_ref, near_ref, far_ref, out_ref, wide_ref, inverse_ref):
    even = is_even()
    row0 = lax.axis_index("row") * z.rd - 1
    col0 = lax.axis_index("col") * z.cd - 1
    near_at = jnp.where(even, z.cd + 2, 0)
    far_at = jnp.where(even, 0, z.cd + 2)
    exists = jnp.where(even, lax.axis_index("col") > 0, lax.axis_index("col") < z.C - 1)
    for i in range(z.rd + 2):
        for k in range(2):
            wide_ref[near_at + k] = near_ref[z.T // 2 + 2 * i + k].astype(f32)
            wide_ref[far_at + k] = jnp.where(exists, far_ref[z.T // 2 + 2 * i + k].astype(f32), 0.0)
        for q in range(z.cd):
            wide_ref[2 + q] = tall_ref[i, q]
        columns = [wide_ref[q] for q in range(z.cd + 4)]
        for q in range(z.cd + 2):
            energy = jnp.sqrt(1.0 + (columns[q] + columns[q + 1] + columns[q + 2]))
            inverse = (1.0 / energy).astype(bf16).astype(f32)
            row, col = row0 + i, col0 + q
            inside = (row >= 0) & (row < z.R * z.rd) & (col >= 0) & (col < z.C * z.cd)
            inverse_ref[i, q] = inverse * jnp.where(inside, 1.0, 0.0)
    for i in range(z.rd):
        columns = []
        for q in range(z.cd + 2):
            columns.append(inverse_ref[i, q] + inverse_ref[i + 1, q] + inverse_ref[i + 2, q])
        for q in range(z.cd):
            spread = columns[q] + columns[q + 1] + columns[q + 2]
            out_ref[i, q] = sparsity * hidden_ref[i, q].astype(f32) * spread


def grad_kernel(
    z, sum_ref, last_ref, window_ref, patch_ref, hidden_ref, pooled_ref, first_ref, wide_ref,
    out_hbm, resid_ref, flat_ref, dense_ref, resid_patch_ref, factor_ref, out_ref, sems,
):
    B, F = z.B, z.F
    from_left = jnp.logical_not(is_even())
    lane = lax.broadcasted_iota(jnp.int32, (1, z.lanes), 1) % z.stride
    x = lax.axis_index("col") * z.w - PAD + lane
    across = ((x >= 0) & (x < z.width)).astype(f32)
    first = lax.axis_index("row") * z.h - PAD
    for t in range(0, z.T, 2):
        came = unpack_side(z, from_left, last_ref[t // 2].astype(f32))
        for n in range(2):
            line = first + S * ((t + n) % z.YB)
            inside = jnp.where((line >= 0) & (line < z.height), across, 0.0)
            recon = sum_ref[t + n] + came[n]
            resid_ref[t + n] = ((recon - window_ref[t + n].astype(f32)) * inside).astype(bf16)

    turn_fields(z, lambda t: resid_ref[t], flat_ref)
    factor_ref[...] = jnp.zeros_like(factor_ref)
    copies = []
    for q in range(z.cd):
        for p in range(z.rd):
            weight = first_ref.at[p] if p < HELD else wide_ref.at[p - HELD]
            back = dot(field(z, p, resid_ref), weight[:, q * F : (q + 1) * F])
            group, inner = p // z.per, p % z.per
            columns = slice(inner * F, (inner + 1) * F)
            at = inner * B
            factor_ref[q, group, at : at + B, columns] = (pooled_ref[p, q] + back).astype(bf16)
            factor_ref[q, group, 128 + at : 128 + at + B, columns] = hidden_ref[p, q]
        for k in range(CH):
            place_fields(z, q, k, flat_ref, dense_ref, resid_patch_ref)
            rows = slice(k * FIELD * FIELD, (k + 1) * FIELD * FIELD)
            for group in range(z.groups):
                both = jnp.concatenate([patch_ref[q, group, rows, :], resid_patch_ref[q, group, rows, :]], axis=1)
                value = dot(both, factor_ref[q, group]) * (1.0 / B)
                for inner in range(z.per):
                    out_ref[group * z.per + inner, q, rows, :] = value[:, inner * F : (inner + 1) * F]
            copy = pltpu.make_async_copy(out_ref.at[:, q, rows, :], out_hbm.at[:, q, rows, :], sems.at[q, k])
            copy.start()
            copies.append(copy)
    for copy in copies:
        copy.wait()


def gradient(z, *args):
    B, F, L = z.B, z.F, z.lanes
    return pl.pallas_call(
        functools.partial(grad_kernel, z),
        out_shape=pltpu.HBM((z.rd, z.cd, K, F), f32),
        in_specs=[pl.BlockSpec(memory_space=pltpu.VMEM)] * len(args),
        out_specs=pl.BlockSpec(memory_space=pltpu.HBM),
        scratch_shapes=[
            pltpu.VMEM((z.T, B, L), bf16),
            pltpu.VMEM((z.groups, z.KW, 128), f32),
            pltpu.VMEM((K, 128), f32),
            pltpu.VMEM((z.cd, z.groups, K, 128), bf16),
            pltpu.VMEM((z.cd, z.groups, 256, z.per * F), bf16),
            pltpu.VMEM((z.rd, z.cd, K, F), f32),
            pltpu.SemaphoreType.DMA((z.cd, CH)),
        ],
        compiler_params=pltpu.CompilerParams(vmem_limit_bytes=40 * MIB),
    )(*args)


def exchange(z, value, partner):
    pairs = []
    for r in range(z.R):
        for c in range(z.C):
            to = partner(z, r, c)
            pairs.append((r * z.C + c, to[0] * z.C + to[1]))
    return lax.ppermute(value, ("row", "col"), pairs)


def cross_row(z, r, c):
    to = r + 1 if r % 2 else r - 1
    return (to, c) if 0 <= to < z.R else (r, c ^ 1)


def swap_col(z, r, c):
    return (r, c ^ 1)


def cross_col(z, r, c):
    to = c + 1 if c % 2 else c - 1
    return (r, to) if 0 <= to < z.C else (r ^ 1, c)


def body(z, images, weights):
    B, L = z.B, z.lanes
    tiles = ((z.T, B, L), f32)
    blocks = split(z, images)
    moved = lax.all_to_all(
        blocks.reshape(z.R * z.C, z.bd * z.T, L), ("row", "col"), split_axis=0, concat_axis=0, tiled=True
    ).reshape(B, z.T, L)
    turned = jnp.swapaxes(weights, 2, 3)
    wide_first = spread_weights(z, turned, 0, HELD, pltpu.VMEM)
    wide = spread_weights(z, turned, HELD, z.rd - HELD, pltpu.HBM)
    window, hidden, contrib, to_swap, to_cross, wide = encode(z, moved, wide_first, wide)
    crossed = exchange(z, to_cross, cross_row)
    swapped = exchange(z, to_swap, lambda z, r, c: (r ^ 1, c))
    tall = ((z.rd + 2, z.cd, B, z.F), f32)
    sent = ((z.T // 2 + 2 * (z.rd + 2), B, L), bf16)
    total, tall, send = vmem_call(
        functools.partial(rows_kernel, z), [tiles, tall, sent], [], contrib, hidden, swapped, crossed
    )
    near = exchange(z, send, swap_col)
    total, send = vmem_call(functools.partial(near_kernel, z), [tiles, sent], [], total, tall, near)
    (patch,) = vmem_call(
        functools.partial(patches_kernel, z),
        [((z.cd, z.groups, K, 128), bf16)],
        [((z.groups, z.KW, 128), f32), ((K, 128), f32)],
        window,
    )
    far, patch = lax.optimization_barrier((exchange(z, send, cross_col), patch))
    total, send = vmem_call(
        functools.partial(far_kernel, z), [tiles, ((z.T // 2, B, L), bf16)], [], total, far
    )
    last = exchange(z, send, swap_col)
    (pooled,) = vmem_call(
        functools.partial(pool_kernel, z),
        [((z.rd, z.cd, B, z.F), f32)],
        [((z.cd + 4, B, z.F), f32), ((z.rd + 2, z.cd + 2, B, z.F), f32)],
        hidden, tall, near, far,
    )
    return jnp.swapaxes(gradient(z, total, last, window, patch, hidden, pooled, wide_first, wide), 2, 3)


def solution(mesh):
    def run(images, weights):
        z = Sizes(
            (images.shape[0] // (mesh.shape["row"] * mesh.shape["col"]),) + images.shape[1:],
            (weights.shape[0] // mesh.shape["row"], weights.shape[1] // mesh.shape["col"]) + weights.shape[2:],
            mesh,
        )
        return jax.shard_map(
            functools.partial(body, z),
            mesh=mesh,
            in_specs=(P(("row", "col"), None, None, None), P("row", "col", None, None)),
            out_specs=P("row", "col", None, None),
            check_vma=False,
        )(images, weights)

    return run
```

```python
import functools

import jax
import jax.numpy as jnp
from jax import lax
from jax.experimental import pallas as pl
from jax.experimental.pallas import tpu as pltpu
from jax.sharding import PartitionSpec as P

CH = 3
S = 4
FIELD = 20
PAD = 8
K = 1200
MARGIN = 16
HELD = 2
GROUP = FIELD // S

sparsity = 0.5
f32 = jnp.float32
bf16 = jnp.bfloat16
NT = (((1,), (1,)), ((), ()))
NN = (((1,), (0,)), ((), ()))
TN = (((0,), (0,)), ((), ()))
MIB = 1024 * 1024


def dot(a, b, dims=NN):
    return lax.dot_general(a, b, dims, preferred_element_type=f32)


class Sizes:
    def __init__(self, images, weights, mesh):
        self.R, self.C = mesh.shape["row"], mesh.shape["col"]
        self.bd = images[0]
        self.height, self.width = images[2], images[3]
        self.rd, self.cd, self.F = weights[0], weights[1], weights[2]
        self.B = self.bd * self.R * self.C
        self.h, self.w = S * self.rd, S * self.cd
        self.ext = self.w + 2 * PAD
        self.stride = -(-self.ext // 32) * 32
        self.lanes = S * self.stride
        self.YB = self.rd + 2 * PAD // S
        self.T = CH * self.YB
        self.KW = CH * FIELD * self.stride
        self.per = 128 // self.B
        self.groups = self.rd // self.per
        assert self.B * self.per == 128 and self.groups * self.per == self.rd and self.F == 128
        assert self.C % 2 == 0 and self.R % 2 == 0 and self.rd >= 4 and self.cd >= 2 and self.lanes == 128
        assert self.height == self.R * self.h and self.width == self.C * self.w


def split_kernel(z, images_hbm, out_hbm, images_ref, rows_ref, pad_ref, pick_ref, out_ref, in_sem, out_sems):
    load = pltpu.make_async_copy(images_hbm, images_ref, in_sem)
    load.start()
    margin = PAD // S
    blocks = z.height // S
    n = lax.broadcasted_iota(jnp.int32, (1, z.C * z.lanes), 1)
    column = n // z.lanes
    inner = n % z.lanes
    lane_row = inner // z.stride
    across = inner % z.stride
    source = jnp.where(across < z.ext, z.w * column - PAD + across, -1)
    pixel = lax.broadcasted_iota(jnp.int32, (128, z.C * z.lanes), 0)
    chunks = rows_ref.shape[1]
    for k in range(chunks):
        for j in range(S):
            wanted = jnp.where(lane_row == j, source - 128 * k, -1)
            pick_ref[k, j] = (pixel == wanted).astype(f32).astype(bf16)
    rows_ref[...] = jnp.zeros_like(rows_ref)
    pad_ref[...] = jnp.zeros_like(pad_ref)
    inside = (source >= 0) & (source < z.width)
    load.wait()
    for i in range(z.bd):
        pixels = images_ref[i].astype(f32)
        for k in range(chunks):
            stop = min(128, z.width - 128 * k)
            rows_ref[:, k, :, :stop] = pixels[:, :, 128 * k : 128 * k + stop]
        total = jnp.zeros((CH * blocks, z.C * z.lanes), f32)
        for k in range(chunks):
            for j in range(S):
                line = jnp.concatenate(
                    [rows_ref[c, k, pl.ds(j, blocks, stride=S), :] for c in range(CH)], axis=0
                ).astype(bf16)
                total = total + dot(line, pick_ref[k, j])
        count = CH * z.height * z.width
        center = jnp.sum(pixels) / count
        variance = jnp.sum(jnp.square(pixels - center)) / count
        total = jnp.where(inside, (total - center) / jnp.sqrt(variance + 1e-05), 0.0)
        for c in range(CH):
            pad_ref[c, margin : margin + blocks, :] = total[c * blocks : (c + 1) * blocks]
        for r in range(z.R):
            for q in range(z.C):
                block = [
                    pad_ref[c, z.rd * r : z.rd * r + z.YB, q * z.lanes : (q + 1) * z.lanes]
                    for c in range(CH)
                ]
                out_ref[r * z.C + q, i] = jnp.concatenate(block, axis=0).astype(bf16)
            if i == z.bd - 1:
                part = pl.ds(r * z.C, z.C)
                pltpu.make_async_copy(out_ref.at[part], out_hbm.at[part], out_sems.at[r]).start()
    for r in range(z.R):
        part = pl.ds(r * z.C, z.C)
        pltpu.make_async_copy(out_ref.at[part], out_hbm.at[part], out_sems.at[r]).wait()


def split(z, images):
    shape = (z.R * z.C, z.bd, z.T, z.lanes)
    return pl.pallas_call(
        functools.partial(split_kernel, z),
        out_shape=pltpu.HBM(shape, bf16),
        in_specs=[pl.BlockSpec(memory_space=pltpu.HBM)],
        out_specs=pl.BlockSpec(memory_space=pltpu.HBM),
        scratch_shapes=[
            pltpu.VMEM((z.bd, CH, z.height, z.width), bf16),
            pltpu.VMEM((CH, -(-z.width // 128), z.height, 128), f32),
            pltpu.VMEM((CH, z.height // S + 2 * PAD // S, z.C * z.lanes), f32),
            pltpu.VMEM((-(-z.width // 128), S, 128, z.C * z.lanes), bf16),
            pltpu.VMEM(shape, bf16),
            pltpu.SemaphoreType.DMA,
            pltpu.SemaphoreType.DMA((z.R,)),
        ],
        compiler_params=pltpu.CompilerParams(vmem_limit_bytes=32 * MIB),
    )(pltpu.with_memory_space_constraint(images, pltpu.HBM))


def spread_kernel(z, weights_ref, out_ref, rows_ref):
    row = lax.broadcasted_iota(jnp.int32, (z.stride, z.F), 0)
    for q in range(z.cd):
        rows_ref[MARGIN : MARGIN + K, :] = weights_ref[0, q].astype(f32)
        inside = (row >= S * q) & (row < S * q + FIELD)
        for i in range(CH * FIELD):
            at = MARGIN + FIELD * i - S * q
            value = jnp.where(inside, rows_ref[at : at + z.stride, :], 0.0)
            out_ref[0, z.stride * i : z.stride * (i + 1), q * z.F : (q + 1) * z.F] = value.astype(bf16)


def spread_weights(z, weights, first, count, space):
    return pl.pallas_call(
        functools.partial(spread_kernel, z),
        grid=(count,),
        out_shape=space((count, z.KW, z.cd * z.F), bf16),
        in_specs=[pl.BlockSpec((1, z.cd, K, z.F), lambda p: (p + first, 0, 0, 0))],
        out_specs=pl.BlockSpec((1, z.KW, z.cd * z.F), lambda p: (p, 0, 0)),
        scratch_shapes=[pltpu.VMEM((K + 2 * MARGIN, z.F), f32)],
        compiler_params=pltpu.CompilerParams(vmem_limit_bytes=32 * MIB),
    )(weights)


def field(z, p, tiles_ref):
    return jnp.concatenate(
        [tiles_ref[c * z.YB + p + g] for c in range(CH) for g in range(GROUP)], axis=1
    )


def encode_kernel(
    z, moved_ref, first_ref, wide_hbm, window_ref, hidden_ref, contrib_ref, swap_ref, cross_ref, wide_ref, rows_ref, sems
):
    B = z.B
    copies = [pltpu.make_async_copy(wide_hbm.at[p], wide_ref.at[p], sems.at[p]) for p in range(z.rd - HELD)]
    for copy in copies[:2]:
        copy.start()
    rows_ref[...] = moved_ref[...].reshape(B * z.T, z.lanes).astype(f32)
    for t in range(z.T):
        window_ref[t] = rows_ref[pl.ds(t, B, stride=z.T), :].astype(bf16)
    contrib_ref[...] = jnp.zeros_like(contrib_ref)
    for first in range(0, z.rd, HELD):
        rows = range(first, min(first + HELD, z.rd))
        for p in rows:
            if p >= HELD:
                copies[p - HELD].wait()
                if p - HELD + 2 < len(copies):
                    copies[p - HELD + 2].start()
        weight = [first_ref.at[p] if p < HELD else wide_ref.at[p - HELD] for p in rows]
        hidden = [dot(field(z, p, window_ref), w[...]).astype(bf16) for p, w in zip(rows, weight)]
        terms = [dot(h, w[...], NT) for h, w in zip(hidden, weight)]
        for p, h, value in zip(rows, hidden, terms):
            for q in range(z.cd):
                hidden_ref[p, q] = h[:, q * z.F : (q + 1) * z.F]
            for c in range(CH):
                for g in range(GROUP):
                    at = (c * GROUP + g) * z.lanes
                    contrib_ref[c * z.YB + p + g] += value[:, at : at + z.lanes]
    half = z.YB // 2
    even = row_is_even()
    for ref, below in ((swap_ref, even), (cross_ref, jnp.logical_not(even))):
        first = jnp.where(below, z.YB - half, 0)
        row = jnp.where(below, z.rd - 2, 0)
        for c in range(CH):
            for y in range(half):
                ref[c * half + y] = contrib_ref[c * z.YB + first + y].astype(bf16)
        for i in range(2):
            for q in range(z.cd):
                ref[CH * half + i * z.cd + q] = hidden_ref[row + i, q]


def encode(z, moved, first, wide):
    B, L = z.B, z.lanes
    vmem = pl.BlockSpec(memory_space=pltpu.VMEM)
    sent = CH * (z.YB // 2) + 2 * z.cd
    shapes = [
        ((z.T, B, L), bf16),
        ((z.rd, z.cd, B, z.F), bf16),
        ((z.T, B, L), f32),
        ((sent, B, L), bf16),
        ((sent, B, L), bf16),
        ((z.rd - HELD, z.KW, z.cd * z.F), bf16),
    ]
    return pl.pallas_call(
        functools.partial(encode_kernel, z),
        out_shape=[pltpu.VMEM(*s) for s in shapes],
        in_specs=[vmem, vmem, pl.BlockSpec(memory_space=pltpu.HBM)],
        out_specs=[vmem] * len(shapes),
        scratch_shapes=[
            pltpu.VMEM((B * z.T, L), f32),
            pltpu.SemaphoreType.DMA((z.rd - HELD,)),
        ],
        compiler_params=pltpu.CompilerParams(vmem_limit_bytes=32 * MIB),
    )(moved, first, pltpu.with_memory_space_constraint(wide, pltpu.HBM))


def turn_fields(z, tile_of, flat_ref):
    for group in range(z.groups):
        for c in range(CH):
            for g in range(GROUP):
                first = c * z.YB + group * z.per + g
                stack = jnp.concatenate([tile_of(first + p) for p in range(z.per)], axis=0)
                at = (c * GROUP + g) * z.lanes
                flat_ref[group, at : at + z.lanes, :] = stack.astype(f32).T


def place_fields(z, q, c, flat_ref, dense_ref, out_ref):
    rows = slice(c * FIELD * FIELD, (c + 1) * FIELD * FIELD)
    for group in range(z.groups):
        for i in range(c * FIELD, (c + 1) * FIELD):
            at = z.stride * i + S * q
            dense_ref[FIELD * i : FIELD * (i + 1), :] = flat_ref[group, at : at + FIELD, :]
        out_ref[q, group, rows, :] = dense_ref[rows, :].astype(bf16)


def patches_kernel(z, window_ref, out_ref, flat_ref, dense_ref):
    turn_fields(z, lambda t: window_ref[t], flat_ref)
    for q in range(z.cd):
        for c in range(CH):
            place_fields(z, q, c, flat_ref, dense_ref, out_ref)


def vmem_call(kernel, shapes, scratch, *args):
    vmem = pl.BlockSpec(memory_space=pltpu.VMEM)
    return pl.pallas_call(
        kernel,
        out_shape=[pltpu.VMEM(*s) for s in shapes],
        in_specs=[vmem] * len(args),
        out_specs=[vmem] * len(shapes),
        scratch_shapes=[pltpu.VMEM(*s) for s in scratch],
        compiler_params=pltpu.CompilerParams(vmem_limit_bytes=32 * MIB),
    )(*args)


def is_even():
    return lax.rem(lax.axis_index("col"), 2) == 0


def row_is_even():
    return lax.rem(lax.axis_index("row"), 2) == 0


def pack_side(z, to_right, first, second):
    wide = 2 * PAD
    across = lax.broadcasted_iota(jnp.int32, first.shape, 1) % z.stride
    low = pltpu.roll(first, jnp.where(to_right, z.lanes - z.w, 0), 1)
    high = pltpu.roll(second, jnp.where(to_right, z.lanes - z.w + wide, wide) % z.lanes, 1)
    return jnp.where(across < wide, low, jnp.where(across < 2 * wide, high, 0.0))


def unpack_side(z, from_left, packed):
    wide = 2 * PAD
    across = lax.broadcasted_iota(jnp.int32, packed.shape, 1) % z.stride
    start = jnp.where(from_left, 0, z.w)
    inside = (across >= start) & (across < start + wide)
    first = pltpu.roll(packed, start, 1)
    second = pltpu.roll(packed, (start + z.lanes - wide) % z.lanes, 1)
    return jnp.where(inside, first, 0.0), jnp.where(inside, second, 0.0)


def rows_kernel(z, contrib_ref, hidden_ref, swap_ref, cross_ref, sum_ref, tall_ref, send_ref):
    half = z.YB // 2
    sum_ref[...] = contrib_ref[...]
    row = lax.axis_index("row")
    even_row = row_is_even()
    above_exists, below_exists = row > 0, row < z.R - 1
    for ref, below in ((swap_ref, even_row), (cross_ref, jnp.logical_not(even_row))):
        exists = jnp.where(below, below_exists, above_exists)
        first = jnp.where(below, z.YB - half, 0)
        for c in range(CH):
            for y in range(half):
                sum_ref[c * z.YB + first + y] += jnp.where(exists, ref[c * half + y].astype(f32), 0.0)
    even = is_even()
    for t in range(0, z.T, 2):
        send_ref[t // 2] = pack_side(z, even, sum_ref[t], sum_ref[t + 1]).astype(bf16)
    for q in range(z.cd):
        squares = [jnp.square(hidden_ref[i, q].astype(f32)) for i in range(z.rd)]
        above, below = [], []
        for i in range(2):
            swapped = swap_ref[CH * half + i * z.cd + q].astype(f32)
            crossed = cross_ref[CH * half + i * z.cd + q].astype(f32)
            upper = jnp.where(above_exists, jnp.where(even_row, crossed, swapped), 0.0)
            lower = jnp.where(below_exists, jnp.where(even_row, swapped, crossed), 0.0)
            above.append(jnp.square(upper))
            below.append(jnp.square(lower))
        squares = above + squares + below
        for i in range(z.rd + 2):
            tall_ref[i, q] = squares[i] + squares[i + 1] + squares[i + 2]
    first = jnp.where(even, z.cd - 2, 0)
    for i in range(z.rd + 2):
        for k in range(2):
            send_ref[z.T // 2 + 2 * i + k] = tall_ref[i, first + k].astype(bf16)


def near_kernel(z, sum_ref, tall_ref, near_ref, out_ref, send_ref):
    even = is_even()
    for t in range(0, z.T, 2):
        came = unpack_side(z, jnp.logical_not(even), near_ref[t // 2].astype(f32))
        total = [sum_ref[t + k] + came[k] for k in range(2)]
        for k in range(2):
            out_ref[t + k] = total[k]
        send_ref[t // 2] = pack_side(z, jnp.logical_not(even), *total).astype(bf16)
    first = jnp.where(even, 0, z.cd - 2)
    for i in range(z.rd + 2):
        for k in range(2):
            send_ref[z.T // 2 + 2 * i + k] = tall_ref[i, first + k].astype(bf16)


def far_kernel(z, sum_ref, far_ref, out_ref, send_ref):
    even = is_even()
    exists = jnp.where(even, lax.axis_index("col") > 0, lax.axis_index("col") < z.C - 1)
    for t in range(0, z.T, 2):
        came = unpack_side(z, even, jnp.where(exists, far_ref[t // 2].astype(f32), 0.0))
        for k in range(2):
            out_ref[t + k] = sum_ref[t + k] + came[k]
        send_ref[t // 2] = pack_side(z, even, *came).astype(bf16)


def pool_kernel(z, hidden_ref, tall_ref, near_ref, far_ref, out_ref, wide_ref, inverse_ref):
    even = is_even()
    row0 = lax.axis_index("row") * z.rd - 1
    col0 = lax.axis_index("col") * z.cd - 1
    near_at = jnp.where(even, z.cd + 2, 0)
    far_at = jnp.where(even, 0, z.cd + 2)
    exists = jnp.where(even, lax.axis_index("col") > 0, lax.axis_index("col") < z.C - 1)
    for i in range(z.rd + 2):
        for k in range(2):
            wide_ref[near_at + k] = near_ref[z.T // 2 + 2 * i + k].astype(f32)
            wide_ref[far_at + k] = jnp.where(exists, far_ref[z.T // 2 + 2 * i + k].astype(f32), 0.0)
        for q in range(z.cd):
            wide_ref[2 + q] = tall_ref[i, q]
        columns = [wide_ref[q] for q in range(z.cd + 4)]
        for q in range(z.cd + 2):
            energy = jnp.sqrt(1.0 + (columns[q] + columns[q + 1] + columns[q + 2]))
            inverse = (1.0 / energy).astype(bf16).astype(f32)
            row, col = row0 + i, col0 + q
            inside = (row >= 0) & (row < z.R * z.rd) & (col >= 0) & (col < z.C * z.cd)
            inverse_ref[i, q] = inverse * jnp.where(inside, 1.0, 0.0)
    for i in range(z.rd):
        columns = []
        for q in range(z.cd + 2):
            columns.append(inverse_ref[i, q] + inverse_ref[i + 1, q] + inverse_ref[i + 2, q])
        for q in range(z.cd):
            spread = columns[q] + columns[q + 1] + columns[q + 2]
            out_ref[i, q] = sparsity * hidden_ref[i, q].astype(f32) * spread


def grad_kernel(
    z, sum_ref, last_ref, window_ref, patch_ref, hidden_ref, pooled_ref, first_ref, wide_ref,
    out_hbm, resid_ref, flat_ref, dense_ref, resid_patch_ref, factor_ref, out_ref, sems,
):
    B, F = z.B, z.F
    from_left = jnp.logical_not(is_even())
    lane = lax.broadcasted_iota(jnp.int32, (1, z.lanes), 1) % z.stride
    x = lax.axis_index("col") * z.w - PAD + lane
    across = ((x >= 0) & (x < z.width)).astype(f32)
    first = lax.axis_index("row") * z.h - PAD
    for t in range(0, z.T, 2):
        came = unpack_side(z, from_left, last_ref[t // 2].astype(f32))
        for n in range(2):
            line = first + S * ((t + n) % z.YB)
            inside = jnp.where((line >= 0) & (line < z.height), across, 0.0)
            recon = sum_ref[t + n] + came[n]
            resid_ref[t + n] = ((recon - window_ref[t + n].astype(f32)) * inside).astype(bf16)

    turn_fields(z, lambda t: resid_ref[t], flat_ref)
    factor_ref[...] = jnp.zeros_like(factor_ref)
    copies = []
    for q in range(z.cd):
        for p in range(z.rd):
            weight = first_ref.at[p] if p < HELD else wide_ref.at[p - HELD]
            back = dot(field(z, p, resid_ref), weight[:, q * F : (q + 1) * F])
            group, inner = p // z.per, p % z.per
            columns = slice(inner * F, (inner + 1) * F)
            at = inner * B
            factor_ref[q, group, at : at + B, columns] = (pooled_ref[p, q] + back).astype(bf16)
            factor_ref[q, group, 128 + at : 128 + at + B, columns] = hidden_ref[p, q]
        for k in range(CH):
            place_fields(z, q, k, flat_ref, dense_ref, resid_patch_ref)
            rows = slice(k * FIELD * FIELD, (k + 1) * FIELD * FIELD)
            for group in range(z.groups):
                both = jnp.concatenate([patch_ref[q, group, rows, :], resid_patch_ref[q, group, rows, :]], axis=1)
                value = dot(both, factor_ref[q, group]) * (1.0 / B)
                for inner in range(z.per):
                    out_ref[group * z.per + inner, q, rows, :] = value[:, inner * F : (inner + 1) * F]
            copy = pltpu.make_async_copy(out_ref.at[:, q, rows, :], out_hbm.at[:, q, rows, :], sems.at[q, k])
            copy.start()
            copies.append(copy)
    for copy in copies:
        copy.wait()


def gradient(z, *args):
    B, F, L = z.B, z.F, z.lanes
    return pl.pallas_call(
        functools.partial(grad_kernel, z),
        out_shape=pltpu.HBM((z.rd, z.cd, K, F), f32),
        in_specs=[pl.BlockSpec(memory_space=pltpu.VMEM)] * len(args),
        out_specs=pl.BlockSpec(memory_space=pltpu.HBM),
        scratch_shapes=[
            pltpu.VMEM((z.T, B, L), bf16),
            pltpu.VMEM((z.groups, z.KW, 128), f32),
            pltpu.VMEM((K, 128), f32),
            pltpu.VMEM((z.cd, z.groups, K, 128), bf16),
            pltpu.VMEM((z.cd, z.groups, 256, z.per * F), bf16),
            pltpu.VMEM((z.rd, z.cd, K, F), f32),
            pltpu.SemaphoreType.DMA((z.cd, CH)),
        ],
        compiler_params=pltpu.CompilerParams(vmem_limit_bytes=40 * MIB),
    )(*args)


def exchange(z, value, partner):
    pairs = []
    for r in range(z.R):
        for c in range(z.C):
            to = partner(z, r, c)
            pairs.append((r * z.C + c, to[0] * z.C + to[1]))
    return lax.ppermute(value, ("row", "col"), pairs)


def cross_row(z, r, c):
    to = r + 1 if r % 2 else r - 1
    return (to, c) if 0 <= to < z.R else (r, c ^ 1)


def swap_col(z, r, c):
    return (r, c ^ 1)


def cross_col(z, r, c):
    to = c + 1 if c % 2 else c - 1
    return (r, to) if 0 <= to < z.C else (r ^ 1, c)


def body(z, images, weights):
    B, L = z.B, z.lanes
    tiles = ((z.T, B, L), f32)
    blocks = split(z, images)
    moved = lax.all_to_all(
        blocks.reshape(z.R * z.C, z.bd * z.T, L), ("row", "col"), split_axis=0, concat_axis=0, tiled=True
    ).reshape(B, z.T, L)
    turned = jnp.swapaxes(weights, 2, 3)
    wide_first = spread_weights(z, turned, 0, HELD, pltpu.VMEM)
    wide = spread_weights(z, turned, HELD, z.rd - HELD, pltpu.HBM)
    window, hidden, contrib, to_swap, to_cross, wide = encode(z, moved, wide_first, wide)
    crossed = exchange(z, to_cross, cross_row)
    swapped = exchange(z, to_swap, lambda z, r, c: (r ^ 1, c))
    tall = ((z.rd + 2, z.cd, B, z.F), f32)
    sent = ((z.T // 2 + 2 * (z.rd + 2), B, L), bf16)
    total, tall, send = vmem_call(
        functools.partial(rows_kernel, z), [tiles, tall, sent], [], contrib, hidden, swapped, crossed
    )
    near = exchange(z, send, swap_col)
    total, send = vmem_call(functools.partial(near_kernel, z), [tiles, sent], [], total, tall, near)
    (patch,) = vmem_call(
        functools.partial(patches_kernel, z),
        [((z.cd, z.groups, K, 128), bf16)],
        [((z.groups, z.KW, 128), f32), ((K, 128), f32)],
        window,
    )
    far, patch = lax.optimization_barrier((exchange(z, send, cross_col), patch))
    total, send = vmem_call(
        functools.partial(far_kernel, z), [tiles, ((z.T // 2, B, L), bf16)], [], total, far
    )
    last = exchange(z, send, swap_col)
    (pooled,) = vmem_call(
        functools.partial(pool_kernel, z),
        [((z.rd, z.cd, B, z.F), f32)],
        [((z.cd + 4, B, z.F), f32), ((z.rd + 2, z.cd + 2, B, z.F), f32)],
        hidden, tall, near, far,
    )
    return jnp.swapaxes(gradient(z, total, last, window, patch, hidden, pooled, wide_first, wide), 2, 3)


def solution(mesh):
    def run(images, weights):
        z = Sizes(
            (images.shape[0] // (mesh.shape["row"] * mesh.shape["col"]),) + images.shape[1:],
            (weights.shape[0] // mesh.shape["row"], weights.shape[1] // mesh.shape["col"]) + weights.shape[2:],
            mesh,
        )
        return jax.shard_map(
            functools.partial(body, z),
            mesh=mesh,
            in_specs=(P(("row", "col"), None, None, None), P("row", "col", None, None)),
            out_specs=P("row", "col", None, None),
            check_vma=False,
        )(images, weights)

    return run
```

```python
import functools

import jax
import jax.numpy as jnp
from jax import lax
from jax.experimental import pallas as pl
from jax.experimental.pallas import tpu as pltpu
from jax.sharding import PartitionSpec as P

CH = 3
S = 4
FIELD = 20
PAD = 8
K = 1200
MARGIN = 16
HELD = 2
GROUP = FIELD // S

sparsity = 0.5
f32 = jnp.float32
bf16 = jnp.bfloat16
NT = (((1,), (1,)), ((), ()))
NN = (((1,), (0,)), ((), ()))
TN = (((0,), (0,)), ((), ()))
MIB = 1024 * 1024


def dot(a, b, dims=NN):
    return lax.dot_general(a, b, dims, preferred_element_type=f32)


class Sizes:
    def __init__(self, images, weights, mesh):
        self.R, self.C = mesh.shape["row"], mesh.shape["col"]
        self.bd = images[0]
        self.height, self.width = images[2], images[3]
        self.rd, self.cd, self.F = weights[0], weights[1], weights[2]
        self.B = self.bd * self.R * self.C
        self.h, self.w = S * self.rd, S * self.cd
        self.ext = self.w + 2 * PAD
        self.stride = -(-self.ext // 32) * 32
        self.lanes = S * self.stride
        self.YB = self.rd + 2 * PAD // S
        self.T = CH * self.YB
        self.KW = CH * FIELD * self.stride
        self.per = 128 // self.B
        self.groups = self.rd // self.per
        assert self.B * self.per == 128 and self.groups * self.per == self.rd and self.F == 128
        assert self.C % 2 == 0 and self.R % 2 == 0 and self.rd >= 4 and self.cd >= 2 and self.lanes == 128
        assert self.height == self.R * self.h and self.width == self.C * self.w


def split_kernel(z, images_hbm, out_hbm, images_ref, rows_ref, pad_ref, pick_ref, out_ref, in_sem, out_sems):
    load = pltpu.make_async_copy(images_hbm, images_ref, in_sem)
    load.start()
    margin = PAD // S
    blocks = z.height // S
    n = lax.broadcasted_iota(jnp.int32, (1, z.C * z.lanes), 1)
    column = n // z.lanes
    inner = n % z.lanes
    lane_row = inner // z.stride
    across = inner % z.stride
    source = jnp.where(across < z.ext, z.w * column - PAD + across, -1)
    pixel = lax.broadcasted_iota(jnp.int32, (128, z.C * z.lanes), 0)
    chunks = rows_ref.shape[1]
    for k in range(chunks):
        for j in range(S):
            wanted = jnp.where(lane_row == j, source - 128 * k, -1)
            pick_ref[k, j] = (pixel == wanted).astype(f32).astype(bf16)
    rows_ref[...] = jnp.zeros_like(rows_ref)
    pad_ref[...] = jnp.zeros_like(pad_ref)
    inside = (source >= 0) & (source < z.width)
    load.wait()
    for i in range(z.bd):
        pixels = images_ref[i].astype(f32)
        for k in range(chunks):
            stop = min(128, z.width - 128 * k)
            rows_ref[:, k, :, :stop] = pixels[:, :, 128 * k : 128 * k + stop]
        total = jnp.zeros((CH * blocks, z.C * z.lanes), f32)
        for k in range(chunks):
            for j in range(S):
                line = jnp.concatenate(
                    [rows_ref[c, k, pl.ds(j, blocks, stride=S), :] for c in range(CH)], axis=0
                ).astype(bf16)
                total = total + dot(line, pick_ref[k, j])
        count = CH * z.height * z.width
        center = jnp.sum(pixels) / count
        variance = jnp.sum(jnp.square(pixels - center)) / count
        total = jnp.where(inside, (total - center) / jnp.sqrt(variance + 1e-05), 0.0)
        for c in range(CH):
            pad_ref[i, c, margin : margin + blocks, :] = total[c * blocks : (c + 1) * blocks]
    copies = []
    for r in range(z.R):
        parts = [
            pad_ref[i, c, z.rd * r : z.rd * r + z.YB, q * z.lanes : (q + 1) * z.lanes]
            for q in range(z.C)
            for i in range(z.bd)
            for c in range(CH)
        ]
        for k in range(0, len(parts), 2 * CH):
            pair = jnp.concatenate(parts[k : k + 2 * CH], axis=0)
            out_ref[r, k * z.YB : (k + 2 * CH) * z.YB, :] = pair.astype(bf16)
        copy = pltpu.make_async_copy(out_ref.at[r], out_hbm.at[r], out_sems.at[r])
        copy.start()
        copies.append(copy)
    for copy in copies:
        copy.wait()


def split(z, images):
    shape = (z.R, z.C * z.bd * z.T, z.lanes)
    return pl.pallas_call(
        functools.partial(split_kernel, z),
        out_shape=pltpu.HBM(shape, bf16),
        in_specs=[pl.BlockSpec(memory_space=pltpu.HBM)],
        out_specs=pl.BlockSpec(memory_space=pltpu.HBM),
        scratch_shapes=[
            pltpu.VMEM((z.bd, CH, z.height, z.width), bf16),
            pltpu.VMEM((CH, -(-z.width // 128), z.height, 128), f32),
            pltpu.VMEM((z.bd, CH, z.height // S + 2 * PAD // S, z.C * z.lanes), f32),
            pltpu.VMEM((-(-z.width // 128), S, 128, z.C * z.lanes), bf16),
            pltpu.VMEM(shape, bf16),
            pltpu.SemaphoreType.DMA,
            pltpu.SemaphoreType.DMA((z.R,)),
        ],
        compiler_params=pltpu.CompilerParams(vmem_limit_bytes=32 * MIB),
    )(pltpu.with_memory_space_constraint(images, pltpu.HBM))


def spread_kernel(z, weights_ref, out_ref, rows_ref):
    row = lax.broadcasted_iota(jnp.int32, (z.stride, z.F), 0)
    for q in range(z.cd):
        rows_ref[MARGIN : MARGIN + K, :] = weights_ref[0, q].astype(f32)
        inside = (row >= S * q) & (row < S * q + FIELD)
        for i in range(CH * FIELD):
            at = MARGIN + FIELD * i - S * q
            value = jnp.where(inside, rows_ref[at : at + z.stride, :], 0.0)
            out_ref[0, z.stride * i : z.stride * (i + 1), q * z.F : (q + 1) * z.F] = value.astype(bf16)


def spread_weights(z, weights, first, count, space):
    return pl.pallas_call(
        functools.partial(spread_kernel, z),
        grid=(count,),
        out_shape=space((count, z.KW, z.cd * z.F), bf16),
        in_specs=[pl.BlockSpec((1, z.cd, K, z.F), lambda p: (p + first, 0, 0, 0))],
        out_specs=pl.BlockSpec((1, z.KW, z.cd * z.F), lambda p: (p, 0, 0)),
        scratch_shapes=[pltpu.VMEM((K + 2 * MARGIN, z.F), f32)],
        compiler_params=pltpu.CompilerParams(vmem_limit_bytes=32 * MIB),
    )(weights)


def field(z, p, tiles_ref):
    return jnp.concatenate(
        [tiles_ref[c * z.YB + p + g] for c in range(CH) for g in range(GROUP)], axis=1
    )


def encode_kernel(
    z, moved_ref, first_ref, wide_hbm, window_ref, hidden_ref, contrib_ref, swap_ref, cross_ref, wide_ref, rows_ref, sems
):
    B = z.B
    copies = [pltpu.make_async_copy(wide_hbm.at[p], wide_ref.at[p], sems.at[p]) for p in range(z.rd - HELD)]
    for copy in copies[:2]:
        copy.start()
    rows_ref[...] = moved_ref[...].reshape(B * z.T, z.lanes).astype(f32)
    for t in range(z.T):
        window_ref[t] = rows_ref[pl.ds(t, B, stride=z.T), :].astype(bf16)
    contrib_ref[...] = jnp.zeros_like(contrib_ref)
    for first in range(0, z.rd, HELD):
        rows = range(first, min(first + HELD, z.rd))
        for p in rows:
            if p >= HELD:
                copies[p - HELD].wait()
                if p - HELD + 2 < len(copies):
                    copies[p - HELD + 2].start()
        weight = [first_ref.at[p] if p < HELD else wide_ref.at[p - HELD] for p in rows]
        hidden = [dot(field(z, p, window_ref), w[...]).astype(bf16) for p, w in zip(rows, weight)]
        terms = [dot(h, w[...], NT) for h, w in zip(hidden, weight)]
        for p, h, value in zip(rows, hidden, terms):
            for q in range(z.cd):
                hidden_ref[p, q] = h[:, q * z.F : (q + 1) * z.F]
            for c in range(CH):
                for g in range(GROUP):
                    at = (c * GROUP + g) * z.lanes
                    contrib_ref[c * z.YB + p + g] += value[:, at : at + z.lanes]
    half = z.YB // 2
    even = row_is_even()
    for ref, below in ((swap_ref, even), (cross_ref, jnp.logical_not(even))):
        first = jnp.where(below, z.YB - half, 0)
        row = jnp.where(below, z.rd - 2, 0)
        for c in range(CH):
            for y in range(half):
                ref[c * half + y] = contrib_ref[c * z.YB + first + y].astype(bf16)
        for i in range(2):
            for q in range(z.cd):
                ref[CH * half + i * z.cd + q] = hidden_ref[row + i, q]


def encode(z, moved, first, wide):
    B, L = z.B, z.lanes
    vmem = pl.BlockSpec(memory_space=pltpu.VMEM)
    sent = CH * (z.YB // 2) + 2 * z.cd
    shapes = [
        ((z.T, B, L), bf16),
        ((z.rd, z.cd, B, z.F), bf16),
        ((z.T, B, L), f32),
        ((sent, B, L), bf16),
        ((sent, B, L), bf16),
        ((z.rd - HELD, z.KW, z.cd * z.F), bf16),
    ]
    return pl.pallas_call(
        functools.partial(encode_kernel, z),
        out_shape=[pltpu.VMEM(*s) for s in shapes],
        in_specs=[vmem, vmem, pl.BlockSpec(memory_space=pltpu.HBM)],
        out_specs=[vmem] * len(shapes),
        scratch_shapes=[
            pltpu.VMEM((B * z.T, L), f32),
            pltpu.SemaphoreType.DMA((z.rd - HELD,)),
        ],
        compiler_params=pltpu.CompilerParams(vmem_limit_bytes=32 * MIB),
    )(moved, first, pltpu.with_memory_space_constraint(wide, pltpu.HBM))


def turn_fields(z, tile_of, flat_ref):
    for group in range(z.groups):
        for c in range(CH):
            for g in range(GROUP):
                first = c * z.YB + group * z.per + g
                stack = jnp.concatenate([tile_of(first + p) for p in range(z.per)], axis=0)
                at = (c * GROUP + g) * z.lanes
                flat_ref[group, at : at + z.lanes, :] = stack.astype(f32).T


def place_fields(z, q, c, flat_ref, dense_ref, out_ref):
    rows = slice(c * FIELD * FIELD, (c + 1) * FIELD * FIELD)
    for group in range(z.groups):
        for i in range(c * FIELD, (c + 1) * FIELD):
            at = z.stride * i + S * q
            dense_ref[FIELD * i : FIELD * (i + 1), :] = flat_ref[group, at : at + FIELD, :]
        out_ref[q, group, rows, :] = dense_ref[rows, :].astype(bf16)


def patches_kernel(z, window_ref, out_ref, flat_ref, dense_ref):
    turn_fields(z, lambda t: window_ref[t], flat_ref)
    for q in range(z.cd):
        for c in range(CH):
            place_fields(z, q, c, flat_ref, dense_ref, out_ref)


def vmem_call(kernel, shapes, scratch, *args):
    vmem = pl.BlockSpec(memory_space=pltpu.VMEM)
    return pl.pallas_call(
        kernel,
        out_shape=[pltpu.VMEM(*s) for s in shapes],
        in_specs=[vmem] * len(args),
        out_specs=[vmem] * len(shapes),
        scratch_shapes=[pltpu.VMEM(*s) for s in scratch],
        compiler_params=pltpu.CompilerParams(vmem_limit_bytes=32 * MIB),
    )(*args)


def is_even():
    return lax.rem(lax.axis_index("col"), 2) == 0


def row_is_even():
    return lax.rem(lax.axis_index("row"), 2) == 0


def pack_side(z, to_right, first, second):
    wide = 2 * PAD
    across = lax.broadcasted_iota(jnp.int32, first.shape, 1) % z.stride
    low = pltpu.roll(first, jnp.where(to_right, z.lanes - z.w, 0), 1)
    high = pltpu.roll(second, jnp.where(to_right, z.lanes - z.w + wide, wide) % z.lanes, 1)
    return jnp.where(across < wide, low, jnp.where(across < 2 * wide, high, 0.0))


def unpack_side(z, from_left, packed):
    wide = 2 * PAD
    across = lax.broadcasted_iota(jnp.int32, packed.shape, 1) % z.stride
    start = jnp.where(from_left, 0, z.w)
    inside = (across >= start) & (across < start + wide)
    first = pltpu.roll(packed, start, 1)
    second = pltpu.roll(packed, (start + z.lanes - wide) % z.lanes, 1)
    return jnp.where(inside, first, 0.0), jnp.where(inside, second, 0.0)


def rows_kernel(z, contrib_ref, hidden_ref, swap_ref, cross_ref, sum_ref, tall_ref, send_ref):
    half = z.YB // 2
    sum_ref[...] = contrib_ref[...]
    row = lax.axis_index("row")
    even_row = row_is_even()
    above_exists, below_exists = row > 0, row < z.R - 1
    for ref, below in ((swap_ref, even_row), (cross_ref, jnp.logical_not(even_row))):
        exists = jnp.where(below, below_exists, above_exists)
        first = jnp.where(below, z.YB - half, 0)
        for c in range(CH):
            for y in range(half):
                sum_ref[c * z.YB + first + y] += jnp.where(exists, ref[c * half + y].astype(f32), 0.0)
    even = is_even()
    for t in range(0, z.T, 2):
        send_ref[t // 2] = pack_side(z, even, sum_ref[t], sum_ref[t + 1]).astype(bf16)
    for q in range(z.cd):
        squares = [jnp.square(hidden_ref[i, q].astype(f32)) for i in range(z.rd)]
        above, below = [], []
        for i in range(2):
            swapped = swap_ref[CH * half + i * z.cd + q].astype(f32)
            crossed = cross_ref[CH * half + i * z.cd + q].astype(f32)
            upper = jnp.where(above_exists, jnp.where(even_row, crossed, swapped), 0.0)
            lower = jnp.where(below_exists, jnp.where(even_row, swapped, crossed), 0.0)
            above.append(jnp.square(upper))
            below.append(jnp.square(lower))
        squares = above + squares + below
        for i in range(z.rd + 2):
            tall_ref[i, q] = squares[i] + squares[i + 1] + squares[i + 2]
    first = jnp.where(even, z.cd - 2, 0)
    for i in range(z.rd + 2):
        for k in range(2):
            send_ref[z.T // 2 + 2 * i + k] = tall_ref[i, first + k].astype(bf16)


def near_kernel(z, sum_ref, tall_ref, near_ref, out_ref, send_ref):
    even = is_even()
    for t in range(0, z.T, 2):
        came = unpack_side(z, jnp.logical_not(even), near_ref[t // 2].astype(f32))
        total = [sum_ref[t + k] + came[k] for k in range(2)]
        for k in range(2):
            out_ref[t + k] = total[k]
        send_ref[t // 2] = pack_side(z, jnp.logical_not(even), *total).astype(bf16)
    first = jnp.where(even, 0, z.cd - 2)
    for i in range(z.rd + 2):
        for k in range(2):
            send_ref[z.T // 2 + 2 * i + k] = tall_ref[i, first + k].astype(bf16)


def far_kernel(z, sum_ref, far_ref, out_ref, send_ref):
    even = is_even()
    exists = jnp.where(even, lax.axis_index("col") > 0, lax.axis_index("col") < z.C - 1)
    for t in range(0, z.T, 2):
        came = unpack_side(z, even, jnp.where(exists, far_ref[t // 2].astype(f32), 0.0))
        for k in range(2):
            out_ref[t + k] = sum_ref[t + k] + came[k]
        send_ref[t // 2] = pack_side(z, even, *came).astype(bf16)


def pool_kernel(z, hidden_ref, tall_ref, near_ref, far_ref, out_ref, wide_ref, inverse_ref):
    even = is_even()
    row0 = lax.axis_index("row") * z.rd - 1
    col0 = lax.axis_index("col") * z.cd - 1
    near_at = jnp.where(even, z.cd + 2, 0)
    far_at = jnp.where(even, 0, z.cd + 2)
    exists = jnp.where(even, lax.axis_index("col") > 0, lax.axis_index("col") < z.C - 1)
    for i in range(z.rd + 2):
        for k in range(2):
            wide_ref[near_at + k] = near_ref[z.T // 2 + 2 * i + k].astype(f32)
            wide_ref[far_at + k] = jnp.where(exists, far_ref[z.T // 2 + 2 * i + k].astype(f32), 0.0)
        for q in range(z.cd):
            wide_ref[2 + q] = tall_ref[i, q]
        columns = [wide_ref[q] for q in range(z.cd + 4)]
        for q in range(z.cd + 2):
            energy = jnp.sqrt(1.0 + (columns[q] + columns[q + 1] + columns[q + 2]))
            inverse = (1.0 / energy).astype(bf16).astype(f32)
            row, col = row0 + i, col0 + q
            inside = (row >= 0) & (row < z.R * z.rd) & (col >= 0) & (col < z.C * z.cd)
            inverse_ref[i, q] = inverse * jnp.where(inside, 1.0, 0.0)
    for i in range(z.rd):
        columns = []
        for q in range(z.cd + 2):
            columns.append(inverse_ref[i, q] + inverse_ref[i + 1, q] + inverse_ref[i + 2, q])
        for q in range(z.cd):
            spread = columns[q] + columns[q + 1] + columns[q + 2]
            out_ref[i, q] = sparsity * hidden_ref[i, q].astype(f32) * spread


def grad_kernel(
    z, sum_ref, last_ref, window_ref, patch_ref, hidden_ref, pooled_ref, first_ref, wide_ref,
    out_hbm, resid_ref, flat_ref, dense_ref, resid_patch_ref, factor_ref, out_ref, sems,
):
    B, F = z.B, z.F
    from_left = jnp.logical_not(is_even())
    lane = lax.broadcasted_iota(jnp.int32, (1, z.lanes), 1) % z.stride
    x = lax.axis_index("col") * z.w - PAD + lane
    across = ((x >= 0) & (x < z.width)).astype(f32)
    first = lax.axis_index("row") * z.h - PAD
    for t in range(0, z.T, 2):
        came = unpack_side(z, from_left, last_ref[t // 2].astype(f32))
        for n in range(2):
            line = first + S * ((t + n) % z.YB)
            inside = jnp.where((line >= 0) & (line < z.height), across, 0.0)
            recon = sum_ref[t + n] + came[n]
            resid_ref[t + n] = ((recon - window_ref[t + n].astype(f32)) * inside).astype(bf16)

    turn_fields(z, lambda t: resid_ref[t], flat_ref)
    factor_ref[...] = jnp.zeros_like(factor_ref)
    copies = []
    for q in range(z.cd):
        for p in range(z.rd):
            weight = first_ref.at[p] if p < HELD else wide_ref.at[p - HELD]
            back = dot(field(z, p, resid_ref), weight[:, q * F : (q + 1) * F])
            group, inner = p // z.per, p % z.per
            columns = slice(inner * F, (inner + 1) * F)
            at = inner * B
            factor_ref[q, group, at : at + B, columns] = (pooled_ref[p, q] + back).astype(bf16)
            factor_ref[q, group, 128 + at : 128 + at + B, columns] = hidden_ref[p, q]
        for k in range(CH):
            place_fields(z, q, k, flat_ref, dense_ref, resid_patch_ref)
            rows = slice(k * FIELD * FIELD, (k + 1) * FIELD * FIELD)
            for group in range(z.groups):
                both = jnp.concatenate([patch_ref[q, group, rows, :], resid_patch_ref[q, group, rows, :]], axis=1)
                value = dot(both, factor_ref[q, group]) * (1.0 / B)
                for inner in range(z.per):
                    out_ref[group * z.per + inner, q, rows, :] = value[:, inner * F : (inner + 1) * F]
            copy = pltpu.make_async_copy(out_ref.at[:, q, rows, :], out_hbm.at[:, q, rows, :], sems.at[q, k])
            copy.start()
            copies.append(copy)
    for copy in copies:
        copy.wait()


def gradient(z, *args):
    B, F, L = z.B, z.F, z.lanes
    return pl.pallas_call(
        functools.partial(grad_kernel, z),
        out_shape=pltpu.HBM((z.rd, z.cd, K, F), f32),
        in_specs=[pl.BlockSpec(memory_space=pltpu.VMEM)] * len(args),
        out_specs=pl.BlockSpec(memory_space=pltpu.HBM),
        scratch_shapes=[
            pltpu.VMEM((z.T, B, L), bf16),
            pltpu.VMEM((z.groups, z.KW, 128), f32),
            pltpu.VMEM((K, 128), f32),
            pltpu.VMEM((z.cd, z.groups, K, 128), bf16),
            pltpu.VMEM((z.cd, z.groups, 256, z.per * F), bf16),
            pltpu.VMEM((z.rd, z.cd, K, F), f32),
            pltpu.SemaphoreType.DMA((z.cd, CH)),
        ],
        compiler_params=pltpu.CompilerParams(vmem_limit_bytes=40 * MIB),
    )(*args)


def exchange(z, value, partner):
    pairs = []
    for r in range(z.R):
        for c in range(z.C):
            to = partner(z, r, c)
            pairs.append((r * z.C + c, to[0] * z.C + to[1]))
    return lax.ppermute(value, ("row", "col"), pairs)


def cross_row(z, r, c):
    to = r + 1 if r % 2 else r - 1
    return (to, c) if 0 <= to < z.R else (r, c ^ 1)


def swap_col(z, r, c):
    return (r, c ^ 1)


def cross_col(z, r, c):
    to = c + 1 if c % 2 else c - 1
    return (r, to) if 0 <= to < z.C else (r ^ 1, c)


def body(z, images, weights):
    B, L = z.B, z.lanes
    tiles = ((z.T, B, L), f32)
    blocks = split(z, images)
    moved = lax.all_to_all(
        blocks.reshape(z.R * z.C, z.bd * z.T, L), ("row", "col"), split_axis=0, concat_axis=0, tiled=True
    ).reshape(B, z.T, L)
    turned = jnp.swapaxes(weights, 2, 3)
    wide_first = spread_weights(z, turned, 0, HELD, pltpu.VMEM)
    wide = spread_weights(z, turned, HELD, z.rd - HELD, pltpu.HBM)
    window, hidden, contrib, to_swap, to_cross, wide = encode(z, moved, wide_first, wide)
    crossed = exchange(z, to_cross, cross_row)
    swapped = exchange(z, to_swap, lambda z, r, c: (r ^ 1, c))
    tall = ((z.rd + 2, z.cd, B, z.F), f32)
    sent = ((z.T // 2 + 2 * (z.rd + 2), B, L), bf16)
    total, tall, send = vmem_call(
        functools.partial(rows_kernel, z), [tiles, tall, sent], [], contrib, hidden, swapped, crossed
    )
    near = exchange(z, send, swap_col)
    total, send = vmem_call(functools.partial(near_kernel, z), [tiles, sent], [], total, tall, near)
    (patch,) = vmem_call(
        functools.partial(patches_kernel, z),
        [((z.cd, z.groups, K, 128), bf16)],
        [((z.groups, z.KW, 128), f32), ((K, 128), f32)],
        window,
    )
    far, patch = lax.optimization_barrier((exchange(z, send, cross_col), patch))
    total, send = vmem_call(
        functools.partial(far_kernel, z), [tiles, ((z.T // 2, B, L), bf16)], [], total, far
    )
    last = exchange(z, send, swap_col)
    (pooled,) = vmem_call(
        functools.partial(pool_kernel, z),
        [((z.rd, z.cd, B, z.F), f32)],
        [((z.cd + 4, B, z.F), f32), ((z.rd + 2, z.cd + 2, B, z.F), f32)],
        hidden, tall, near, far,
    )
    return jnp.swapaxes(gradient(z, total, last, window, patch, hidden, pooled, wide_first, wide), 2, 3)


def solution(mesh):
    def run(images, weights):
        z = Sizes(
            (images.shape[0] // (mesh.shape["row"] * mesh.shape["col"]),) + images.shape[1:],
            (weights.shape[0] // mesh.shape["row"], weights.shape[1] // mesh.shape["col"]) + weights.shape[2:],
            mesh,
        )
        return jax.shard_map(
            functools.partial(body, z),
            mesh=mesh,
            in_specs=(P(("row", "col"), None, None, None), P("row", "col", None, None)),
            out_specs=P("row", "col", None, None),
            check_vma=False,
        )(images, weights)

    return run
```

```python
import functools

import jax
import jax.numpy as jnp
from jax import lax
from jax.experimental import pallas as pl
from jax.experimental.pallas import tpu as pltpu
from jax.sharding import PartitionSpec as P

CH = 3
S = 4
FIELD = 20
PAD = 8
K = 1200
MARGIN = 16
HELD = 2
GROUP = FIELD // S

sparsity = 0.5
f32 = jnp.float32
bf16 = jnp.bfloat16
NT = (((1,), (1,)), ((), ()))
NN = (((1,), (0,)), ((), ()))
TN = (((0,), (0,)), ((), ()))
MIB = 1024 * 1024


def dot(a, b, dims=NN):
    return lax.dot_general(a, b, dims, preferred_element_type=f32)


class Sizes:
    def __init__(self, images, weights, mesh):
        self.R, self.C = mesh.shape["row"], mesh.shape["col"]
        self.bd = images[0]
        self.height, self.width = images[2], images[3]
        self.rd, self.cd, self.F = weights[0], weights[1], weights[2]
        self.B = self.bd * self.R * self.C
        self.h, self.w = S * self.rd, S * self.cd
        self.ext = self.w + 2 * PAD
        self.stride = -(-self.ext // 32) * 32
        self.lanes = S * self.stride
        self.YB = self.rd + 2 * PAD // S
        self.T = CH * self.YB
        self.late = 2 * PAD - self.w
        self.KW = CH * FIELD * self.stride
        self.per = 128 // self.B
        self.groups = self.rd // self.per
        assert self.late > 0 and self.stride % self.late == 0 and self.T % (self.stride // self.late) == 0
        assert self.B * self.per == 128 and self.groups * self.per == self.rd and self.F == 128
        assert self.C % 2 == 0 and self.R % 2 == 0 and self.rd >= 4 and self.cd >= 2 and self.lanes == 128
        assert self.height == self.R * self.h and self.width == self.C * self.w


def split_kernel(z, images_hbm, out_hbm, images_ref, rows_ref, pad_ref, pick_ref, out_ref, in_sem, out_sems):
    load = pltpu.make_async_copy(images_hbm, images_ref, in_sem)
    load.start()
    margin = PAD // S
    blocks = z.height // S
    n = lax.broadcasted_iota(jnp.int32, (1, z.C * z.lanes), 1)
    column = n // z.lanes
    inner = n % z.lanes
    lane_row = inner // z.stride
    across = inner % z.stride
    source = jnp.where(across < z.ext, z.w * column - PAD + across, -1)
    pixel = lax.broadcasted_iota(jnp.int32, (128, z.C * z.lanes), 0)
    chunks = rows_ref.shape[1]
    for k in range(chunks):
        for j in range(S):
            wanted = jnp.where(lane_row == j, source - 128 * k, -1)
            pick_ref[k, j] = (pixel == wanted).astype(f32).astype(bf16)
    rows_ref[...] = jnp.zeros_like(rows_ref)
    pad_ref[...] = jnp.zeros_like(pad_ref)
    inside = (source >= 0) & (source < z.width)
    load.wait()
    for i in range(z.bd):
        pixels = images_ref[i].astype(f32)
        for k in range(chunks):
            stop = min(128, z.width - 128 * k)
            rows_ref[:, k, :, :stop] = pixels[:, :, 128 * k : 128 * k + stop]
        total = jnp.zeros((CH * blocks, z.C * z.lanes), f32)
        for k in range(chunks):
            for j in range(S):
                line = jnp.concatenate(
                    [rows_ref[c, k, pl.ds(j, blocks, stride=S), :] for c in range(CH)], axis=0
                ).astype(bf16)
                total = total + dot(line, pick_ref[k, j])
        count = CH * z.height * z.width
        center = jnp.sum(pixels) / count
        variance = jnp.sum(jnp.square(pixels - center)) / count
        total = jnp.where(inside, (total - center) / jnp.sqrt(variance + 1e-05), 0.0)
        for c in range(CH):
            pad_ref[i, c, margin : margin + blocks, :] = total[c * blocks : (c + 1) * blocks]
    copies = []
    for r in range(z.R):
        parts = [
            pad_ref[i, c, z.rd * r : z.rd * r + z.YB, q * z.lanes : (q + 1) * z.lanes]
            for q in range(z.C)
            for i in range(z.bd)
            for c in range(CH)
        ]
        for k in range(0, len(parts), 2 * CH):
            pair = jnp.concatenate(parts[k : k + 2 * CH], axis=0)
            out_ref[r, k * z.YB : (k + 2 * CH) * z.YB, :] = pair.astype(bf16)
        copy = pltpu.make_async_copy(out_ref.at[r], out_hbm.at[r], out_sems.at[r])
        copy.start()
        copies.append(copy)
    for copy in copies:
        copy.wait()


def split(z, images):
    shape = (z.R, z.C * z.bd * z.T, z.lanes)
    return pl.pallas_call(
        functools.partial(split_kernel, z),
        out_shape=pltpu.HBM(shape, bf16),
        in_specs=[pl.BlockSpec(memory_space=pltpu.HBM)],
        out_specs=pl.BlockSpec(memory_space=pltpu.HBM),
        scratch_shapes=[
            pltpu.VMEM((z.bd, CH, z.height, z.width), bf16),
            pltpu.VMEM((CH, -(-z.width // 128), z.height, 128), f32),
            pltpu.VMEM((z.bd, CH, z.height // S + 2 * PAD // S, z.C * z.lanes), f32),
            pltpu.VMEM((-(-z.width // 128), S, 128, z.C * z.lanes), bf16),
            pltpu.VMEM(shape, bf16),
            pltpu.SemaphoreType.DMA,
            pltpu.SemaphoreType.DMA((z.R,)),
        ],
        compiler_params=pltpu.CompilerParams(vmem_limit_bytes=32 * MIB),
    )(pltpu.with_memory_space_constraint(images, pltpu.HBM))


def spread_kernel(z, weights_ref, out_ref, rows_ref):
    row = lax.broadcasted_iota(jnp.int32, (z.stride, z.F), 0)
    for q in range(z.cd):
        rows_ref[MARGIN : MARGIN + K, :] = weights_ref[0, q].astype(f32)
        inside = (row >= S * q) & (row < S * q + FIELD)
        for i in range(CH * FIELD):
            at = MARGIN + FIELD * i - S * q
            value = jnp.where(inside, rows_ref[at : at + z.stride, :], 0.0)
            out_ref[0, z.stride * i : z.stride * (i + 1), q * z.F : (q + 1) * z.F] = value.astype(bf16)


def spread_weights(z, weights, first, count, space):
    return pl.pallas_call(
        functools.partial(spread_kernel, z),
        grid=(count,),
        out_shape=space((count, z.KW, z.cd * z.F), bf16),
        in_specs=[pl.BlockSpec((1, z.cd, K, z.F), lambda p: (p + first, 0, 0, 0))],
        out_specs=pl.BlockSpec((1, z.KW, z.cd * z.F), lambda p: (p, 0, 0)),
        scratch_shapes=[pltpu.VMEM((K + 2 * MARGIN, z.F), f32)],
        compiler_params=pltpu.CompilerParams(vmem_limit_bytes=32 * MIB),
    )(weights)


def field(z, p, tiles_ref):
    return jnp.concatenate(
        [tiles_ref[c * z.YB + p + g] for c in range(CH) for g in range(GROUP)], axis=1
    )


def encode_kernel(
    z, moved_ref, first_ref, wide_hbm, window_ref, hidden_ref, contrib_ref, swap_ref, cross_ref, wide_ref, rows_ref, sems
):
    B = z.B
    copies = [pltpu.make_async_copy(wide_hbm.at[p], wide_ref.at[p], sems.at[p]) for p in range(z.rd - HELD)]
    for copy in copies[:2]:
        copy.start()
    rows_ref[...] = moved_ref[...].reshape(B * z.T, z.lanes).astype(f32)
    for t in range(z.T):
        window_ref[t] = rows_ref[pl.ds(t, B, stride=z.T), :].astype(bf16)
    contrib_ref[...] = jnp.zeros_like(contrib_ref)
    for first in range(0, z.rd, HELD):
        rows = range(first, min(first + HELD, z.rd))
        for p in rows:
            if p >= HELD:
                copies[p - HELD].wait()
                if p - HELD + 2 < len(copies):
                    copies[p - HELD + 2].start()
        weight = [first_ref.at[p] if p < HELD else wide_ref.at[p - HELD] for p in rows]
        hidden = [dot(field(z, p, window_ref), w[...]).astype(bf16) for p, w in zip(rows, weight)]
        terms = [dot(h, w[...], NT) for h, w in zip(hidden, weight)]
        for p, h, value in zip(rows, hidden, terms):
            for q in range(z.cd):
                hidden_ref[p, q] = h[:, q * z.F : (q + 1) * z.F]
            for c in range(CH):
                for g in range(GROUP):
                    at = (c * GROUP + g) * z.lanes
                    contrib_ref[c * z.YB + p + g] += value[:, at : at + z.lanes]
    half = z.YB // 2
    even = row_is_even()
    for ref, below in ((swap_ref, even), (cross_ref, jnp.logical_not(even))):
        first = jnp.where(below, z.YB - half, 0)
        row = jnp.where(below, z.rd - 2, 0)
        for c in range(CH):
            for y in range(half):
                ref[c * half + y] = contrib_ref[c * z.YB + first + y].astype(bf16)
        for i in range(2):
            for q in range(z.cd):
                ref[CH * half + i * z.cd + q] = hidden_ref[row + i, q]


def encode(z, moved, first, wide):
    B, L = z.B, z.lanes
    vmem = pl.BlockSpec(memory_space=pltpu.VMEM)
    sent = CH * (z.YB // 2) + 2 * z.cd
    shapes = [
        ((z.T, B, L), bf16),
        ((z.rd, z.cd, B, z.F), bf16),
        ((z.T, B, L), f32),
        ((sent, B, L), bf16),
        ((sent, B, L), bf16),
        ((z.rd - HELD, z.KW, z.cd * z.F), bf16),
    ]
    return pl.pallas_call(
        functools.partial(encode_kernel, z),
        out_shape=[pltpu.VMEM(*s) for s in shapes],
        in_specs=[vmem, vmem, pl.BlockSpec(memory_space=pltpu.HBM)],
        out_specs=[vmem] * len(shapes),
        scratch_shapes=[
            pltpu.VMEM((B * z.T, L), f32),
            pltpu.SemaphoreType.DMA((z.rd - HELD,)),
        ],
        compiler_params=pltpu.CompilerParams(vmem_limit_bytes=32 * MIB),
    )(moved, first, pltpu.with_memory_space_constraint(wide, pltpu.HBM))


def turn_fields(z, tile_of, flat_ref):
    for group in range(z.groups):
        for c in range(CH):
            for g in range(GROUP):
                first = c * z.YB + group * z.per + g
                stack = jnp.concatenate([tile_of(first + p) for p in range(z.per)], axis=0)
                at = (c * GROUP + g) * z.lanes
                flat_ref[group, at : at + z.lanes, :] = stack.astype(f32).T


def place_fields(z, q, c, flat_ref, dense_ref, out_ref):
    rows = slice(c * FIELD * FIELD, (c + 1) * FIELD * FIELD)
    for group in range(z.groups):
        for i in range(c * FIELD, (c + 1) * FIELD):
            at = z.stride * i + S * q
            dense_ref[FIELD * i : FIELD * (i + 1), :] = flat_ref[group, at : at + FIELD, :]
        out_ref[q, group, rows, :] = dense_ref[rows, :].astype(bf16)


def patches_kernel(z, window_ref, out_ref, flat_ref, dense_ref):
    turn_fields(z, lambda t: window_ref[t], flat_ref)
    for q in range(z.cd):
        for c in range(CH):
            place_fields(z, q, c, flat_ref, dense_ref, out_ref)


def vmem_call(kernel, shapes, scratch, *args):
    vmem = pl.BlockSpec(memory_space=pltpu.VMEM)
    return pl.pallas_call(
        kernel,
        out_shape=[pltpu.VMEM(*s) for s in shapes],
        in_specs=[vmem] * len(args),
        out_specs=[vmem] * len(shapes),
        scratch_shapes=[pltpu.VMEM(*s) for s in scratch],
        compiler_params=pltpu.CompilerParams(vmem_limit_bytes=32 * MIB),
    )(*args)


def is_even():
    return lax.rem(lax.axis_index("col"), 2) == 0


def row_is_even():
    return lax.rem(lax.axis_index("row"), 2) == 0


def pack_side(z, to_right, first, second):
    wide = 2 * PAD
    across = lax.broadcasted_iota(jnp.int32, first.shape, 1) % z.stride
    low = pltpu.roll(first, jnp.where(to_right, z.lanes - z.w, 0), 1)
    high = pltpu.roll(second, jnp.where(to_right, z.lanes - z.w + wide, wide) % z.lanes, 1)
    return jnp.where(across < wide, low, jnp.where(across < 2 * wide, high, 0.0))


def unpack_side(z, from_left, packed):
    wide = 2 * PAD
    across = lax.broadcasted_iota(jnp.int32, packed.shape, 1) % z.stride
    start = jnp.where(from_left, 0, z.w)
    inside = (across >= start) & (across < start + wide)
    first = pltpu.roll(packed, start, 1)
    second = pltpu.roll(packed, (start + z.lanes - wide) % z.lanes, 1)
    return jnp.where(inside, first, 0.0), jnp.where(inside, second, 0.0)


def pack_late(z, to_right, tiles):
    across = lax.broadcasted_iota(jnp.int32, tiles[0].shape, 1) % z.stride
    start = jnp.where(to_right, 2 * z.w, 0)
    packed = jnp.zeros_like(tiles[0])
    for k, tile in enumerate(tiles):
        at = k * z.late
        turned = pltpu.roll(tile, (z.lanes + at - start) % z.lanes, 1)
        packed = jnp.where((across >= at) & (across < at + z.late), turned, packed)
    return packed


def unpack_late(z, from_left, packed, k):
    across = lax.broadcasted_iota(jnp.int32, packed.shape, 1) % z.stride
    start = jnp.where(from_left, 0, 2 * z.w)
    turned = pltpu.roll(packed, (z.lanes + start - k * z.late) % z.lanes, 1)
    return jnp.where((across >= start) & (across < start + z.late), turned, 0.0)


def rows_kernel(
    z, contrib_ref, hidden_ref, swap_ref, cross_ref, sum_ref, tall_ref, near_ref, far_ref, late_ref
):
    half = z.YB // 2
    sum_ref[...] = contrib_ref[...]
    row = lax.axis_index("row")
    even_row = row_is_even()
    above_exists, below_exists = row > 0, row < z.R - 1
    for ref, below in ((swap_ref, even_row), (cross_ref, jnp.logical_not(even_row))):
        exists = jnp.where(below, below_exists, above_exists)
        first = jnp.where(below, z.YB - half, 0)
        for c in range(CH):
            for y in range(half):
                sum_ref[c * z.YB + first + y] += jnp.where(exists, ref[c * half + y].astype(f32), 0.0)
    even = is_even()
    odd = jnp.logical_not(even)
    for t in range(0, z.T, 2):
        pair = sum_ref[t], sum_ref[t + 1]
        far_ref[t // 2] = pack_side(z, odd, *pair).astype(bf16)
        near_ref[t // 2] = pack_side(z, even, *pair).astype(bf16)
    slots = z.stride // z.late
    for t in range(0, z.T, slots):
        late_ref[t // slots] = pack_late(z, even, [sum_ref[t + k] for k in range(slots)]).astype(bf16)
    for q in range(z.cd):
        squares = [jnp.square(hidden_ref[i, q].astype(f32)) for i in range(z.rd)]
        above, below = [], []
        for i in range(2):
            swapped = swap_ref[CH * half + i * z.cd + q].astype(f32)
            crossed = cross_ref[CH * half + i * z.cd + q].astype(f32)
            upper = jnp.where(above_exists, jnp.where(even_row, crossed, swapped), 0.0)
            lower = jnp.where(below_exists, jnp.where(even_row, swapped, crossed), 0.0)
            above.append(jnp.square(upper))
            below.append(jnp.square(lower))
        squares = above + squares + below
        for i in range(z.rd + 2):
            tall_ref[i, q] = squares[i] + squares[i + 1] + squares[i + 2]
    for ref, right in ((near_ref, even), (far_ref, odd)):
        first = jnp.where(right, z.cd - 2, 0)
        for i in range(z.rd + 2):
            for k in range(2):
                ref[z.T // 2 + 2 * i + k] = tall_ref[i, first + k].astype(bf16)


def merge_kernel(z, sum_ref, near_ref, far_ref, late_ref, out_ref):
    even = is_even()
    col = lax.axis_index("col")
    exists = jnp.where(even, col > 0, col < z.C - 1)
    late_exists = jnp.where(even, col > 1, col < z.C - 2)
    slots = z.stride // z.late
    for t in range(0, z.T, 2):
        near = unpack_side(z, jnp.logical_not(even), near_ref[t // 2].astype(f32))
        came = unpack_side(z, even, jnp.where(exists, far_ref[t // 2].astype(f32), 0.0))
        late = jnp.where(late_exists, late_ref[t // slots].astype(f32), 0.0)
        for k in range(2):
            out_ref[t + k] = sum_ref[t + k] + near[k] + came[k] + unpack_late(z, even, late, t % slots + k)


def unpack_last(z, packed):
    even = is_even()
    col = lax.axis_index("col")
    exists = jnp.where(even, col + 1 < z.C - 1, col - 1 > 0)
    across = lax.broadcasted_iota(jnp.int32, packed.shape, 1) % z.stride
    start = jnp.where(even, 2 * z.w, 0)
    inside = (across >= start) & (across < start + z.late) & exists
    by = jnp.where(even, 2 * z.w, z.lanes - z.w)
    first = pltpu.roll(packed, by, 1)
    second = pltpu.roll(packed, (by + z.lanes - 2 * PAD) % z.lanes, 1)
    return jnp.where(inside, first, 0.0), jnp.where(inside, second, 0.0)


def pool_kernel(z, hidden_ref, tall_ref, near_ref, far_ref, out_ref, wide_ref, inverse_ref):
    even = is_even()
    row0 = lax.axis_index("row") * z.rd - 1
    col0 = lax.axis_index("col") * z.cd - 1
    near_at = jnp.where(even, z.cd + 2, 0)
    far_at = jnp.where(even, 0, z.cd + 2)
    exists = jnp.where(even, lax.axis_index("col") > 0, lax.axis_index("col") < z.C - 1)
    for i in range(z.rd + 2):
        for k in range(2):
            wide_ref[near_at + k] = near_ref[z.T // 2 + 2 * i + k].astype(f32)
            wide_ref[far_at + k] = jnp.where(exists, far_ref[z.T // 2 + 2 * i + k].astype(f32), 0.0)
        for q in range(z.cd):
            wide_ref[2 + q] = tall_ref[i, q]
        columns = [wide_ref[q] for q in range(z.cd + 4)]
        for q in range(z.cd + 2):
            energy = jnp.sqrt(1.0 + (columns[q] + columns[q + 1] + columns[q + 2]))
            inverse = (1.0 / energy).astype(bf16).astype(f32)
            row, col = row0 + i, col0 + q
            inside = (row >= 0) & (row < z.R * z.rd) & (col >= 0) & (col < z.C * z.cd)
            inverse_ref[i, q] = inverse * jnp.where(inside, 1.0, 0.0)
    for i in range(z.rd):
        columns = []
        for q in range(z.cd + 2):
            columns.append(inverse_ref[i, q] + inverse_ref[i + 1, q] + inverse_ref[i + 2, q])
        for q in range(z.cd):
            spread = columns[q] + columns[q + 1] + columns[q + 2]
            out_ref[i, q] = sparsity * hidden_ref[i, q].astype(f32) * spread


def grad_kernel(
    z, sum_ref, last_ref, window_ref, patch_ref, hidden_ref, pooled_ref, first_ref, wide_ref,
    out_hbm, resid_ref, flat_ref, dense_ref, resid_patch_ref, factor_ref, out_ref, sems,
):
    B, F = z.B, z.F
    lane = lax.broadcasted_iota(jnp.int32, (1, z.lanes), 1) % z.stride
    x = lax.axis_index("col") * z.w - PAD + lane
    across = ((x >= 0) & (x < z.width)).astype(f32)
    first = lax.axis_index("row") * z.h - PAD
    for t in range(0, z.T, 2):
        came = unpack_last(z, last_ref[t // 2].astype(f32))
        for n in range(2):
            line = first + S * ((t + n) % z.YB)
            inside = jnp.where((line >= 0) & (line < z.height), across, 0.0)
            recon = sum_ref[t + n] + came[n]
            resid_ref[t + n] = ((recon - window_ref[t + n].astype(f32)) * inside).astype(bf16)

    turn_fields(z, lambda t: resid_ref[t], flat_ref)
    factor_ref[...] = jnp.zeros_like(factor_ref)
    copies = []
    for q in range(z.cd):
        for p in range(z.rd):
            weight = first_ref.at[p] if p < HELD else wide_ref.at[p - HELD]
            back = dot(field(z, p, resid_ref), weight[:, q * F : (q + 1) * F])
            group, inner = p // z.per, p % z.per
            columns = slice(inner * F, (inner + 1) * F)
            at = inner * B
            factor_ref[q, group, at : at + B, columns] = (pooled_ref[p, q] + back).astype(bf16)
            factor_ref[q, group, 128 + at : 128 + at + B, columns] = hidden_ref[p, q]
        for k in range(CH):
            place_fields(z, q, k, flat_ref, dense_ref, resid_patch_ref)
            rows = slice(k * FIELD * FIELD, (k + 1) * FIELD * FIELD)
            for group in range(z.groups):
                both = jnp.concatenate([patch_ref[q, group, rows, :], resid_patch_ref[q, group, rows, :]], axis=1)
                value = dot(both, factor_ref[q, group]) * (1.0 / B)
                for inner in range(z.per):
                    out_ref[group * z.per + inner, q, rows, :] = value[:, inner * F : (inner + 1) * F]
            copy = pltpu.make_async_copy(out_ref.at[:, q, rows, :], out_hbm.at[:, q, rows, :], sems.at[q, k])
            copy.start()
            copies.append(copy)
    for copy in copies:
        copy.wait()


def gradient(z, *args):
    B, F, L = z.B, z.F, z.lanes
    return pl.pallas_call(
        functools.partial(grad_kernel, z),
        out_shape=pltpu.HBM((z.rd, z.cd, K, F), f32),
        in_specs=[pl.BlockSpec(memory_space=pltpu.VMEM)] * len(args),
        out_specs=pl.BlockSpec(memory_space=pltpu.HBM),
        scratch_shapes=[
            pltpu.VMEM((z.T, B, L), bf16),
            pltpu.VMEM((z.groups, z.KW, 128), f32),
            pltpu.VMEM((K, 128), f32),
            pltpu.VMEM((z.cd, z.groups, K, 128), bf16),
            pltpu.VMEM((z.cd, z.groups, 256, z.per * F), bf16),
            pltpu.VMEM((z.rd, z.cd, K, F), f32),
            pltpu.SemaphoreType.DMA((z.cd, CH)),
        ],
        compiler_params=pltpu.CompilerParams(vmem_limit_bytes=40 * MIB),
    )(*args)


def exchange(z, value, partner):
    pairs = []
    for r in range(z.R):
        for c in range(z.C):
            to = partner(z, r, c)
            pairs.append((r * z.C + c, to[0] * z.C + to[1]))
    return lax.ppermute(value, ("row", "col"), pairs)


def shift(z, value):
    pairs = []
    for r in range(z.R):
        for c in range(z.C):
            to = (c + (-2 if c % 2 else 2)) % z.C
            pairs.append((r * z.C + c, r * z.C + to))
    return lax.ppermute(value, ("row", "col"), pairs)


def cross_row(z, r, c):
    to = r + 1 if r % 2 else r - 1
    return (to, c) if 0 <= to < z.R else (r, c ^ 1)


def swap_col(z, r, c):
    return (r, c ^ 1)


def cross_col(z, r, c):
    to = c + 1 if c % 2 else c - 1
    return (r, to) if 0 <= to < z.C else (r ^ 1, c)


def body(z, images, weights):
    B, L = z.B, z.lanes
    tiles = ((z.T, B, L), f32)
    blocks = split(z, images)
    moved = lax.all_to_all(
        blocks.reshape(z.R * z.C, z.bd * z.T, L), ("row", "col"), split_axis=0, concat_axis=0, tiled=True
    ).reshape(B, z.T, L)
    turned = jnp.swapaxes(weights, 2, 3)
    wide_first = spread_weights(z, turned, 0, HELD, pltpu.VMEM)
    wide = spread_weights(z, turned, HELD, z.rd - HELD, pltpu.HBM)
    window, hidden, contrib, to_swap, to_cross, wide = encode(z, moved, wide_first, wide)
    crossed = exchange(z, to_cross, cross_row)
    swapped = exchange(z, to_swap, lambda z, r, c: (r ^ 1, c))
    tall = ((z.rd + 2, z.cd, B, z.F), f32)
    sent = ((z.T // 2 + 2 * (z.rd + 2), B, L), bf16)
    late = ((z.T * z.late // z.stride, B, L), bf16)
    total, tall, to_near, to_far, to_late = vmem_call(
        functools.partial(rows_kernel, z), [tiles, tall, sent, sent, late], [], contrib, hidden, swapped, crossed
    )
    far = exchange(z, to_far, cross_col)
    late = shift(z, to_late)
    near = exchange(z, to_near, swap_col)
    (patch,) = vmem_call(
        functools.partial(patches_kernel, z),
        [((z.cd, z.groups, K, 128), bf16)],
        [((z.groups, z.KW, 128), f32), ((K, 128), f32)],
        window,
    )
    far, near, late, patch = lax.optimization_barrier((far, near, late, patch))
    last = exchange(z, far, swap_col)
    (total,) = vmem_call(functools.partial(merge_kernel, z), [tiles], [], total, near, far, late)
    (pooled,) = vmem_call(
        functools.partial(pool_kernel, z),
        [((z.rd, z.cd, B, z.F), f32)],
        [((z.cd + 4, B, z.F), f32), ((z.rd + 2, z.cd + 2, B, z.F), f32)],
        hidden, tall, near, far,
    )
    return jnp.swapaxes(gradient(z, total, last, window, patch, hidden, pooled, wide_first, wide), 2, 3)


def solution(mesh):
    def run(images, weights):
        z = Sizes(
            (images.shape[0] // (mesh.shape["row"] * mesh.shape["col"]),) + images.shape[1:],
            (weights.shape[0] // mesh.shape["row"], weights.shape[1] // mesh.shape["col"]) + weights.shape[2:],
            mesh,
        )
        return jax.shard_map(
            functools.partial(body, z),
            mesh=mesh,
            in_specs=(P(("row", "col"), None, None, None), P("row", "col", None, None)),
            out_specs=P("row", "col", None, None),
            check_vma=False,
        )(images, weights)

    return run
```

```python
import functools

import jax
import jax.numpy as jnp
from jax import lax
from jax.experimental import pallas as pl
from jax.experimental.pallas import tpu as pltpu
from jax.sharding import PartitionSpec as P

CH = 3
S = 4
FIELD = 20
PAD = 8
K = 1200
MARGIN = 16
HELD = 2
GROUP = FIELD // S

sparsity = 0.5
f32 = jnp.float32
bf16 = jnp.bfloat16
NT = (((1,), (1,)), ((), ()))
NN = (((1,), (0,)), ((), ()))
TN = (((0,), (0,)), ((), ()))
MIB = 1024 * 1024


def dot(a, b, dims=NN):
    return lax.dot_general(a, b, dims, preferred_element_type=f32)


class Sizes:
    def __init__(self, images, weights, mesh):
        self.R, self.C = mesh.shape["row"], mesh.shape["col"]
        self.bd = images[0]
        self.height, self.width = images[2], images[3]
        self.rd, self.cd, self.F = weights[0], weights[1], weights[2]
        self.B = self.bd * self.R * self.C
        self.h, self.w = S * self.rd, S * self.cd
        self.ext = self.w + 2 * PAD
        self.stride = -(-self.ext // 32) * 32
        self.lanes = S * self.stride
        self.YB = self.rd + 2 * PAD // S
        self.T = CH * self.YB
        self.late = 2 * PAD - self.w
        late_even = [q for q in range(self.cd) if S * q + FIELD > 2 * self.w]
        late_odd = [q for q in range(self.cd) if S * q < self.late]
        self.early = next(q for q in range(self.cd) if q not in late_even + late_odd)
        self.KW = CH * FIELD * self.stride
        self.per = 128 // self.B
        self.groups = self.rd // self.per
        assert self.late > 0 and self.stride % self.late == 0 and self.T % (self.stride // self.late) == 0
        assert self.B * self.per == 128 and self.groups * self.per == self.rd and self.F == 128
        assert self.C % 2 == 0 and self.R % 2 == 0 and self.rd >= 4 and self.cd >= 2 and self.lanes == 128
        assert self.height == self.R * self.h and self.width == self.C * self.w


def split_kernel(z, images_hbm, out_hbm, images_ref, rows_ref, pad_ref, pick_ref, out_ref, in_sem, out_sems):
    load = pltpu.make_async_copy(images_hbm, images_ref, in_sem)
    load.start()
    margin = PAD // S
    blocks = z.height // S
    n = lax.broadcasted_iota(jnp.int32, (1, z.C * z.lanes), 1)
    column = n // z.lanes
    inner = n % z.lanes
    lane_row = inner // z.stride
    across = inner % z.stride
    source = jnp.where(across < z.ext, z.w * column - PAD + across, -1)
    pixel = lax.broadcasted_iota(jnp.int32, (128, z.C * z.lanes), 0)
    chunks = rows_ref.shape[1]
    for k in range(chunks):
        for j in range(S):
            wanted = jnp.where(lane_row == j, source - 128 * k, -1)
            pick_ref[k, j] = (pixel == wanted).astype(f32).astype(bf16)
    rows_ref[...] = jnp.zeros_like(rows_ref)
    pad_ref[...] = jnp.zeros_like(pad_ref)
    inside = (source >= 0) & (source < z.width)
    load.wait()
    for i in range(z.bd):
        pixels = images_ref[i].astype(f32)
        for k in range(chunks):
            stop = min(128, z.width - 128 * k)
            rows_ref[:, k, :, :stop] = pixels[:, :, 128 * k : 128 * k + stop]
        total = jnp.zeros((CH * blocks, z.C * z.lanes), f32)
        for k in range(chunks):
            for j in range(S):
                line = jnp.concatenate(
                    [rows_ref[c, k, pl.ds(j, blocks, stride=S), :] for c in range(CH)], axis=0
                ).astype(bf16)
                total = total + dot(line, pick_ref[k, j])
        count = CH * z.height * z.width
        center = jnp.sum(pixels) / count
        variance = jnp.sum(jnp.square(pixels - center)) / count
        total = jnp.where(inside, (total - center) / jnp.sqrt(variance + 1e-05), 0.0)
        for c in range(CH):
            pad_ref[i, c, margin : margin + blocks, :] = total[c * blocks : (c + 1) * blocks]
    copies = []
    for r in range(z.R):
        parts = [
            pad_ref[i, c, z.rd * r : z.rd * r + z.YB, q * z.lanes : (q + 1) * z.lanes]
            for q in range(z.C)
            for i in range(z.bd)
            for c in range(CH)
        ]
        for k in range(0, len(parts), 2 * CH):
            pair = jnp.concatenate(parts[k : k + 2 * CH], axis=0)
            out_ref[r, k * z.YB : (k + 2 * CH) * z.YB, :] = pair.astype(bf16)
        copy = pltpu.make_async_copy(out_ref.at[r], out_hbm.at[r], out_sems.at[r])
        copy.start()
        copies.append(copy)
    for copy in copies:
        copy.wait()


def split(z, images):
    shape = (z.R, z.C * z.bd * z.T, z.lanes)
    return pl.pallas_call(
        functools.partial(split_kernel, z),
        out_shape=pltpu.HBM(shape, bf16),
        in_specs=[pl.BlockSpec(memory_space=pltpu.HBM)],
        out_specs=pl.BlockSpec(memory_space=pltpu.HBM),
        scratch_shapes=[
            pltpu.VMEM((z.bd, CH, z.height, z.width), bf16),
            pltpu.VMEM((CH, -(-z.width // 128), z.height, 128), f32),
            pltpu.VMEM((z.bd, CH, z.height // S + 2 * PAD // S, z.C * z.lanes), f32),
            pltpu.VMEM((-(-z.width // 128), S, 128, z.C * z.lanes), bf16),
            pltpu.VMEM(shape, bf16),
            pltpu.SemaphoreType.DMA,
            pltpu.SemaphoreType.DMA((z.R,)),
        ],
        compiler_params=pltpu.CompilerParams(vmem_limit_bytes=32 * MIB),
    )(pltpu.with_memory_space_constraint(images, pltpu.HBM))


def spread_kernel(z, weights_ref, out_ref, rows_ref):
    row = lax.broadcasted_iota(jnp.int32, (z.stride, z.F), 0)
    for q in range(z.cd):
        rows_ref[MARGIN : MARGIN + K, :] = weights_ref[0, q].astype(f32)
        inside = (row >= S * q) & (row < S * q + FIELD)
        for i in range(CH * FIELD):
            at = MARGIN + FIELD * i - S * q
            value = jnp.where(inside, rows_ref[at : at + z.stride, :], 0.0)
            out_ref[0, z.stride * i : z.stride * (i + 1), q * z.F : (q + 1) * z.F] = value.astype(bf16)


def spread_weights(z, weights, first, count, space):
    return pl.pallas_call(
        functools.partial(spread_kernel, z),
        grid=(count,),
        out_shape=space((count, z.KW, z.cd * z.F), bf16),
        in_specs=[pl.BlockSpec((1, z.cd, K, z.F), lambda p: (p + first, 0, 0, 0))],
        out_specs=pl.BlockSpec((1, z.KW, z.cd * z.F), lambda p: (p, 0, 0)),
        scratch_shapes=[pltpu.VMEM((K + 2 * MARGIN, z.F), f32)],
        compiler_params=pltpu.CompilerParams(vmem_limit_bytes=32 * MIB),
    )(weights)


def field(z, p, tiles_ref):
    return jnp.concatenate(
        [tiles_ref[c * z.YB + p + g] for c in range(CH) for g in range(GROUP)], axis=1
    )


def encode_kernel(
    z, moved_ref, first_ref, wide_hbm, window_ref, hidden_ref, contrib_ref, swap_ref, cross_ref, wide_ref, rows_ref, sems
):
    B = z.B
    copies = [pltpu.make_async_copy(wide_hbm.at[p], wide_ref.at[p], sems.at[p]) for p in range(z.rd - HELD)]
    for copy in copies[:2]:
        copy.start()
    rows_ref[...] = moved_ref[...].reshape(B * z.T, z.lanes).astype(f32)
    for t in range(z.T):
        window_ref[t] = rows_ref[pl.ds(t, B, stride=z.T), :].astype(bf16)
    contrib_ref[...] = jnp.zeros_like(contrib_ref)
    for first in range(0, z.rd, HELD):
        rows = range(first, min(first + HELD, z.rd))
        for p in rows:
            if p >= HELD:
                copies[p - HELD].wait()
                if p - HELD + 2 < len(copies):
                    copies[p - HELD + 2].start()
        weight = [first_ref.at[p] if p < HELD else wide_ref.at[p - HELD] for p in rows]
        hidden = [dot(field(z, p, window_ref), w[...]).astype(bf16) for p, w in zip(rows, weight)]
        terms = [dot(h, w[...], NT) for h, w in zip(hidden, weight)]
        for p, h, value in zip(rows, hidden, terms):
            for q in range(z.cd):
                hidden_ref[p, q] = h[:, q * z.F : (q + 1) * z.F]
            for c in range(CH):
                for g in range(GROUP):
                    at = (c * GROUP + g) * z.lanes
                    contrib_ref[c * z.YB + p + g] += value[:, at : at + z.lanes]
    half = z.YB // 2
    even = row_is_even()
    for ref, below in ((swap_ref, even), (cross_ref, jnp.logical_not(even))):
        first = jnp.where(below, z.YB - half, 0)
        row = jnp.where(below, z.rd - 2, 0)
        for c in range(CH):
            for y in range(half):
                ref[c * half + y] = contrib_ref[c * z.YB + first + y].astype(bf16)
        for i in range(2):
            for q in range(z.cd):
                ref[CH * half + i * z.cd + q] = hidden_ref[row + i, q]


def encode(z, moved, first, wide):
    B, L = z.B, z.lanes
    vmem = pl.BlockSpec(memory_space=pltpu.VMEM)
    sent = CH * (z.YB // 2) + 2 * z.cd
    shapes = [
        ((z.T, B, L), bf16),
        ((z.rd, z.cd, B, z.F), bf16),
        ((z.T, B, L), f32),
        ((sent, B, L), bf16),
        ((sent, B, L), bf16),
        ((z.rd - HELD, z.KW, z.cd * z.F), bf16),
    ]
    return pl.pallas_call(
        functools.partial(encode_kernel, z),
        out_shape=[pltpu.VMEM(*s) for s in shapes],
        in_specs=[vmem, vmem, pl.BlockSpec(memory_space=pltpu.HBM)],
        out_specs=[vmem] * len(shapes),
        scratch_shapes=[
            pltpu.VMEM((B * z.T, L), f32),
            pltpu.SemaphoreType.DMA((z.rd - HELD,)),
        ],
        compiler_params=pltpu.CompilerParams(vmem_limit_bytes=32 * MIB),
    )(moved, first, pltpu.with_memory_space_constraint(wide, pltpu.HBM))


def turn_fields(z, tile_of, flat_ref):
    for group in range(z.groups):
        for c in range(CH):
            for g in range(GROUP):
                first = c * z.YB + group * z.per + g
                stack = jnp.concatenate([tile_of(first + p) for p in range(z.per)], axis=0)
                at = (c * GROUP + g) * z.lanes
                flat_ref[group, at : at + z.lanes, :] = stack.astype(f32).T


def place_fields(z, q, c, flat_ref, dense_ref, out_ref):
    rows = slice(c * FIELD * FIELD, (c + 1) * FIELD * FIELD)
    for group in range(z.groups):
        for i in range(c * FIELD, (c + 1) * FIELD):
            at = z.stride * i + S * q
            dense_ref[FIELD * i : FIELD * (i + 1), :] = flat_ref[group, at : at + FIELD, :]
        out_ref[group, rows, :] = dense_ref[rows, :].astype(bf16)


def patches_kernel(z, window_ref, out_ref, flat_ref, dense_ref):
    turn_fields(z, lambda t: window_ref[t], flat_ref)
    for q in range(z.cd):
        for c in range(CH):
            place_fields(z, q, c, flat_ref, dense_ref, out_ref.at[q])


def store_residual(z, recon_of, window_ref, resid_ref):
    lane = lax.broadcasted_iota(jnp.int32, (1, z.lanes), 1) % z.stride
    x = lax.axis_index("col") * z.w - PAD + lane
    across = ((x >= 0) & (x < z.width)).astype(f32)
    first = lax.axis_index("row") * z.h - PAD
    for t in range(0, z.T, 2):
        recon = recon_of(t)
        for n in range(2):
            line = first + S * ((t + n) % z.YB)
            inside = jnp.where((line >= 0) & (line < z.height), across, 0.0)
            resid_ref[t + n] = ((recon[n] - window_ref[t + n].astype(f32)) * inside).astype(bf16)


def fill_factor(z, q, resid_ref, pooled_ref, hidden_ref, first_ref, wide_ref, factor_ref):
    B, F = z.B, z.F
    factor_ref[...] = jnp.zeros_like(factor_ref)
    for p in range(z.rd):
        weight = first_ref.at[p] if p < HELD else wide_ref.at[p - HELD]
        back = dot(field(z, p, resid_ref), weight[:, q * F : (q + 1) * F])
        group, at = p // z.per, p % z.per * B
        columns = slice(p % z.per * F, (p % z.per + 1) * F)
        factor_ref[group, at : at + B, columns] = (pooled_ref[p, q] + back).astype(bf16)
        factor_ref[group, 128 + at : 128 + at + B, columns] = hidden_ref[p, q]


def vmem_call(kernel, shapes, scratch, *args):
    vmem = pl.BlockSpec(memory_space=pltpu.VMEM)
    return pl.pallas_call(
        kernel,
        out_shape=[pltpu.VMEM(*s) for s in shapes],
        in_specs=[vmem] * len(args),
        out_specs=[vmem] * len(shapes),
        scratch_shapes=[pltpu.VMEM(*s) for s in scratch],
        compiler_params=pltpu.CompilerParams(vmem_limit_bytes=32 * MIB),
    )(*args)


def is_even():
    return lax.rem(lax.axis_index("col"), 2) == 0


def row_is_even():
    return lax.rem(lax.axis_index("row"), 2) == 0


def pack_side(z, to_right, first, second):
    wide = 2 * PAD
    across = lax.broadcasted_iota(jnp.int32, first.shape, 1) % z.stride
    low = pltpu.roll(first, jnp.where(to_right, z.lanes - z.w, 0), 1)
    high = pltpu.roll(second, jnp.where(to_right, z.lanes - z.w + wide, wide) % z.lanes, 1)
    return jnp.where(across < wide, low, jnp.where(across < 2 * wide, high, 0.0))


def unpack_side(z, from_left, packed):
    wide = 2 * PAD
    across = lax.broadcasted_iota(jnp.int32, packed.shape, 1) % z.stride
    start = jnp.where(from_left, 0, z.w)
    inside = (across >= start) & (across < start + wide)
    first = pltpu.roll(packed, start, 1)
    second = pltpu.roll(packed, (start + z.lanes - wide) % z.lanes, 1)
    return jnp.where(inside, first, 0.0), jnp.where(inside, second, 0.0)


def pack_late(z, to_right, tiles):
    across = lax.broadcasted_iota(jnp.int32, tiles[0].shape, 1) % z.stride
    start = jnp.where(to_right, 2 * z.w, 0)
    packed = jnp.zeros_like(tiles[0])
    for k, tile in enumerate(tiles):
        at = k * z.late
        turned = pltpu.roll(tile, (z.lanes + at - start) % z.lanes, 1)
        packed = jnp.where((across >= at) & (across < at + z.late), turned, packed)
    return packed


def unpack_late(z, from_left, packed, k):
    across = lax.broadcasted_iota(jnp.int32, packed.shape, 1) % z.stride
    start = jnp.where(from_left, 0, 2 * z.w)
    turned = pltpu.roll(packed, (z.lanes + start - k * z.late) % z.lanes, 1)
    return jnp.where((across >= start) & (across < start + z.late), turned, 0.0)


def rows_kernel(
    z, contrib_ref, hidden_ref, swap_ref, cross_ref, sum_ref, tall_ref, near_ref, far_ref, late_ref
):
    half = z.YB // 2
    sum_ref[...] = contrib_ref[...]
    row = lax.axis_index("row")
    even_row = row_is_even()
    above_exists, below_exists = row > 0, row < z.R - 1
    for ref, below in ((swap_ref, even_row), (cross_ref, jnp.logical_not(even_row))):
        exists = jnp.where(below, below_exists, above_exists)
        first = jnp.where(below, z.YB - half, 0)
        for c in range(CH):
            for y in range(half):
                sum_ref[c * z.YB + first + y] += jnp.where(exists, ref[c * half + y].astype(f32), 0.0)
    even = is_even()
    odd = jnp.logical_not(even)
    for t in range(0, z.T, 2):
        pair = sum_ref[t], sum_ref[t + 1]
        far_ref[t // 2] = pack_side(z, odd, *pair).astype(bf16)
        near_ref[t // 2] = pack_side(z, even, *pair).astype(bf16)
    slots = z.stride // z.late
    for t in range(0, z.T, slots):
        late_ref[t // slots] = pack_late(z, even, [sum_ref[t + k] for k in range(slots)]).astype(bf16)
    for q in range(z.cd):
        squares = [jnp.square(hidden_ref[i, q].astype(f32)) for i in range(z.rd)]
        above, below = [], []
        for i in range(2):
            swapped = swap_ref[CH * half + i * z.cd + q].astype(f32)
            crossed = cross_ref[CH * half + i * z.cd + q].astype(f32)
            upper = jnp.where(above_exists, jnp.where(even_row, crossed, swapped), 0.0)
            lower = jnp.where(below_exists, jnp.where(even_row, swapped, crossed), 0.0)
            above.append(jnp.square(upper))
            below.append(jnp.square(lower))
        squares = above + squares + below
        for i in range(z.rd + 2):
            tall_ref[i, q] = squares[i] + squares[i + 1] + squares[i + 2]
    for ref, right in ((near_ref, even), (far_ref, odd)):
        first = jnp.where(right, z.cd - 2, 0)
        for i in range(z.rd + 2):
            for k in range(2):
                ref[z.T // 2 + 2 * i + k] = tall_ref[i, first + k].astype(bf16)


def merge_kernel(
    z, sum_ref, near_ref, far_ref, late_ref, window_ref, hidden_ref, pooled_ref, first_ref, wide_ref,
    out_ref, patch_ref, factor_ref, resid_ref, flat_ref, dense_ref,
):
    even = is_even()
    col = lax.axis_index("col")
    exists = jnp.where(even, col > 0, col < z.C - 1)
    late_exists = jnp.where(even, col > 1, col < z.C - 2)
    slots = z.stride // z.late

    def recon_of(t):
        near = unpack_side(z, jnp.logical_not(even), near_ref[t // 2].astype(f32))
        came = unpack_side(z, even, jnp.where(exists, far_ref[t // 2].astype(f32), 0.0))
        late = jnp.where(late_exists, late_ref[t // slots].astype(f32), 0.0)
        recon = []
        for k in range(2):
            recon.append(sum_ref[t + k] + near[k] + came[k] + unpack_late(z, even, late, t % slots + k))
            out_ref[t + k] = recon[k]
        return recon

    store_residual(z, recon_of, window_ref, resid_ref)
    turn_fields(z, lambda t: resid_ref[t], flat_ref)
    fill_factor(z, z.early, resid_ref, pooled_ref, hidden_ref, first_ref, wide_ref, factor_ref)
    for c in range(CH):
        place_fields(z, z.early, c, flat_ref, dense_ref, patch_ref)


def unpack_last(z, packed):
    even = is_even()
    col = lax.axis_index("col")
    exists = jnp.where(even, col + 1 < z.C - 1, col - 1 > 0)
    across = lax.broadcasted_iota(jnp.int32, packed.shape, 1) % z.stride
    start = jnp.where(even, 2 * z.w, 0)
    inside = (across >= start) & (across < start + z.late) & exists
    by = jnp.where(even, 2 * z.w, z.lanes - z.w)
    first = pltpu.roll(packed, by, 1)
    second = pltpu.roll(packed, (by + z.lanes - 2 * PAD) % z.lanes, 1)
    return jnp.where(inside, first, 0.0), jnp.where(inside, second, 0.0)


def pool_kernel(z, hidden_ref, tall_ref, near_ref, far_ref, out_ref, wide_ref, inverse_ref):
    even = is_even()
    row0 = lax.axis_index("row") * z.rd - 1
    col0 = lax.axis_index("col") * z.cd - 1
    near_at = jnp.where(even, z.cd + 2, 0)
    far_at = jnp.where(even, 0, z.cd + 2)
    exists = jnp.where(even, lax.axis_index("col") > 0, lax.axis_index("col") < z.C - 1)
    for i in range(z.rd + 2):
        for k in range(2):
            wide_ref[near_at + k] = near_ref[z.T // 2 + 2 * i + k].astype(f32)
            wide_ref[far_at + k] = jnp.where(exists, far_ref[z.T // 2 + 2 * i + k].astype(f32), 0.0)
        for q in range(z.cd):
            wide_ref[2 + q] = tall_ref[i, q]
        columns = [wide_ref[q] for q in range(z.cd + 4)]
        for q in range(z.cd + 2):
            energy = jnp.sqrt(1.0 + (columns[q] + columns[q + 1] + columns[q + 2]))
            inverse = (1.0 / energy).astype(bf16).astype(f32)
            row, col = row0 + i, col0 + q
            inside = (row >= 0) & (row < z.R * z.rd) & (col >= 0) & (col < z.C * z.cd)
            inverse_ref[i, q] = inverse * jnp.where(inside, 1.0, 0.0)
    for i in range(z.rd):
        columns = []
        for q in range(z.cd + 2):
            columns.append(inverse_ref[i, q] + inverse_ref[i + 1, q] + inverse_ref[i + 2, q])
        for q in range(z.cd):
            spread = columns[q] + columns[q + 1] + columns[q + 2]
            out_ref[i, q] = sparsity * hidden_ref[i, q].astype(f32) * spread


def grad_kernel(
    z, sum_ref, last_ref, window_ref, patch_ref, hidden_ref, pooled_ref, first_ref, wide_ref,
    early_patch_ref, early_factor_ref,
    out_hbm, resid_ref, flat_ref, dense_ref, resid_patch_ref, factor_ref, out_ref, sems,
):
    B, F = z.B, z.F
    copies = []

    def write(q, k, resid_patch, factor):
        rows = slice(k * FIELD * FIELD, (k + 1) * FIELD * FIELD)
        for group in range(z.groups):
            both = jnp.concatenate([patch_ref[q, group, rows, :], resid_patch[group, rows, :]], axis=1)
            value = dot(both, factor[group]) * (1.0 / B)
            for inner in range(z.per):
                out_ref[group * z.per + inner, q, rows, :] = value[:, inner * F : (inner + 1) * F]
        copy = pltpu.make_async_copy(out_ref.at[:, q, rows, :], out_hbm.at[:, q, rows, :], sems.at[q, k])
        copy.start()
        copies.append(copy)

    for k in range(CH):
        write(z.early, k, early_patch_ref, early_factor_ref)

    def recon_of(t):
        came = unpack_last(z, last_ref[t // 2].astype(f32))
        return [sum_ref[t + k] + came[k] for k in range(2)]

    store_residual(z, recon_of, window_ref, resid_ref)
    turn_fields(z, lambda t: resid_ref[t], flat_ref)
    for q in range(z.cd):
        if q == z.early:
            continue
        fill_factor(z, q, resid_ref, pooled_ref, hidden_ref, first_ref, wide_ref, factor_ref.at[q])
        for k in range(CH):
            place_fields(z, q, k, flat_ref, dense_ref, resid_patch_ref.at[q])
            write(q, k, resid_patch_ref.at[q], factor_ref.at[q])
    for copy in copies:
        copy.wait()


def gradient(z, *args):
    B, F, L = z.B, z.F, z.lanes
    return pl.pallas_call(
        functools.partial(grad_kernel, z),
        out_shape=pltpu.HBM((z.rd, z.cd, K, F), f32),
        in_specs=[pl.BlockSpec(memory_space=pltpu.VMEM)] * len(args),
        out_specs=pl.BlockSpec(memory_space=pltpu.HBM),
        scratch_shapes=[
            pltpu.VMEM((z.T, B, L), bf16),
            pltpu.VMEM((z.groups, z.KW, 128), f32),
            pltpu.VMEM((K, 128), f32),
            pltpu.VMEM((z.cd, z.groups, K, 128), bf16),
            pltpu.VMEM((z.cd, z.groups, 256, z.per * F), bf16),
            pltpu.VMEM((z.rd, z.cd, K, F), f32),
            pltpu.SemaphoreType.DMA((z.cd, CH)),
        ],
        compiler_params=pltpu.CompilerParams(vmem_limit_bytes=40 * MIB),
    )(*args)


def exchange(z, value, partner):
    pairs = []
    for r in range(z.R):
        for c in range(z.C):
            to = partner(z, r, c)
            pairs.append((r * z.C + c, to[0] * z.C + to[1]))
    return lax.ppermute(value, ("row", "col"), pairs)


def shift(z, value):
    pairs = []
    for r in range(z.R):
        for c in range(z.C):
            to = (c + (-2 if c % 2 else 2)) % z.C
            pairs.append((r * z.C + c, r * z.C + to))
    return lax.ppermute(value, ("row", "col"), pairs)


def cross_row(z, r, c):
    to = r + 1 if r % 2 else r - 1
    return (to, c) if 0 <= to < z.R else (r, c ^ 1)


def swap_col(z, r, c):
    return (r, c ^ 1)


def cross_col(z, r, c):
    to = c + 1 if c % 2 else c - 1
    return (r, to) if 0 <= to < z.C else (r ^ 1, c)


def body(z, images, weights):
    B, L = z.B, z.lanes
    tiles = ((z.T, B, L), f32)
    blocks = split(z, images)
    moved = lax.all_to_all(
        blocks.reshape(z.R * z.C, z.bd * z.T, L), ("row", "col"), split_axis=0, concat_axis=0, tiled=True
    ).reshape(B, z.T, L)
    turned = jnp.swapaxes(weights, 2, 3)
    wide_first = spread_weights(z, turned, 0, HELD, pltpu.VMEM)
    wide = spread_weights(z, turned, HELD, z.rd - HELD, pltpu.HBM)
    window, hidden, contrib, to_swap, to_cross, wide = encode(z, moved, wide_first, wide)
    crossed = exchange(z, to_cross, cross_row)
    swapped = exchange(z, to_swap, lambda z, r, c: (r ^ 1, c))
    tall = ((z.rd + 2, z.cd, B, z.F), f32)
    sent = ((z.T // 2 + 2 * (z.rd + 2), B, L), bf16)
    late = ((z.T * z.late // z.stride, B, L), bf16)
    total, tall, to_near, to_far, to_late = vmem_call(
        functools.partial(rows_kernel, z), [tiles, tall, sent, sent, late], [], contrib, hidden, swapped, crossed
    )
    far = exchange(z, to_far, cross_col)
    late = shift(z, to_late)
    near = exchange(z, to_near, swap_col)
    (patch,) = vmem_call(
        functools.partial(patches_kernel, z),
        [((z.cd, z.groups, K, 128), bf16)],
        [((z.groups, z.KW, 128), f32), ((K, 128), f32)],
        window,
    )
    far, near, late, patch = lax.optimization_barrier((far, near, late, patch))
    last = exchange(z, far, swap_col)
    (pooled,) = vmem_call(
        functools.partial(pool_kernel, z),
        [((z.rd, z.cd, B, z.F), f32)],
        [((z.cd + 4, B, z.F), f32), ((z.rd + 2, z.cd + 2, B, z.F), f32)],
        hidden, tall, near, far,
    )
    total, early_patch, early_factor = vmem_call(
        functools.partial(merge_kernel, z),
        [tiles, ((z.groups, K, 128), bf16), ((z.groups, 256, z.per * z.F), bf16)],
        [((z.T, B, L), bf16), ((z.groups, z.KW, 128), f32), ((K, 128), f32)],
        total, near, far, late, window, hidden, pooled, wide_first, wide,
    )
    out = gradient(
        z, total, last, window, patch, hidden, pooled, wide_first, wide, early_patch, early_factor
    )
    return jnp.swapaxes(out, 2, 3)


def solution(mesh):
    def run(images, weights):
        z = Sizes(
            (images.shape[0] // (mesh.shape["row"] * mesh.shape["col"]),) + images.shape[1:],
            (weights.shape[0] // mesh.shape["row"], weights.shape[1] // mesh.shape["col"]) + weights.shape[2:],
            mesh,
        )
        return jax.shard_map(
            functools.partial(body, z),
            mesh=mesh,
            in_specs=(P(("row", "col"), None, None, None), P("row", "col", None, None)),
            out_specs=P("row", "col", None, None),
            check_vma=False,
        )(images, weights)

    return run
```

```python
import functools

import jax
import jax.numpy as jnp
from jax import lax
from jax.experimental import pallas as pl
from jax.experimental.pallas import tpu as pltpu
from jax.sharding import PartitionSpec as P

CH = 3
S = 4
FIELD = 20
PAD = 8
K = 1200
MARGIN = 16
HELD = 2
GROUP = FIELD // S

sparsity = 0.5
f32 = jnp.float32
bf16 = jnp.bfloat16
NT = (((1,), (1,)), ((), ()))
NN = (((1,), (0,)), ((), ()))
TN = (((0,), (0,)), ((), ()))
MIB = 1024 * 1024


def dot(a, b, dims=NN):
    return lax.dot_general(a, b, dims, preferred_element_type=f32)


class Sizes:
    def __init__(self, images, weights, mesh):
        self.R, self.C = mesh.shape["row"], mesh.shape["col"]
        self.bd = images[0]
        self.height, self.width = images[2], images[3]
        self.rd, self.cd, self.F = weights[0], weights[1], weights[2]
        self.B = self.bd * self.R * self.C
        self.h, self.w = S * self.rd, S * self.cd
        self.ext = self.w + 2 * PAD
        self.stride = -(-self.ext // 32) * 32
        self.lanes = S * self.stride
        self.YB = self.rd + 2 * PAD // S
        self.T = CH * self.YB
        self.late = 2 * PAD - self.w
        late_even = [q for q in range(self.cd) if S * q + FIELD > 2 * self.w]
        late_odd = [q for q in range(self.cd) if S * q < self.late]
        self.early = next(q for q in range(self.cd) if q not in late_even + late_odd)
        self.KW = CH * FIELD * self.stride
        self.per = 128 // self.B
        self.groups = self.rd // self.per
        assert self.late > 0 and self.stride % self.late == 0 and self.T % (self.stride // self.late) == 0
        assert self.B * self.per == 128 and self.groups * self.per == self.rd and self.F == 128
        assert self.C % 2 == 0 and self.R % 2 == 0 and self.rd >= 4 and self.cd >= 2 and self.lanes == 128
        assert self.height == self.R * self.h and self.width == self.C * self.w


def split_kernel(z, images_hbm, out_hbm, images_ref, rows_ref, pad_ref, pick_ref, out_ref, in_sem, out_sems):
    load = pltpu.make_async_copy(images_hbm, images_ref, in_sem)
    load.start()
    margin = PAD // S
    blocks = z.height // S
    n = lax.broadcasted_iota(jnp.int32, (1, z.C * z.lanes), 1)
    column = n // z.lanes
    inner = n % z.lanes
    lane_row = inner // z.stride
    across = inner % z.stride
    source = jnp.where(across < z.ext, z.w * column - PAD + across, -1)
    pixel = lax.broadcasted_iota(jnp.int32, (128, z.C * z.lanes), 0)
    chunks = rows_ref.shape[1]
    for k in range(chunks):
        for j in range(S):
            wanted = jnp.where(lane_row == j, source - 128 * k, -1)
            pick_ref[k, j] = (pixel == wanted).astype(f32).astype(bf16)
    rows_ref[...] = jnp.zeros_like(rows_ref)
    pad_ref[...] = jnp.zeros_like(pad_ref)
    inside = (source >= 0) & (source < z.width)
    load.wait()
    for i in range(z.bd):
        pixels = images_ref[i].astype(f32)
        for k in range(chunks):
            stop = min(128, z.width - 128 * k)
            rows_ref[:, k, :, :stop] = pixels[:, :, 128 * k : 128 * k + stop]
        total = jnp.zeros((CH * blocks, z.C * z.lanes), f32)
        for k in range(chunks):
            for j in range(S):
                line = jnp.concatenate(
                    [rows_ref[c, k, pl.ds(j, blocks, stride=S), :] for c in range(CH)], axis=0
                ).astype(bf16)
                total = total + dot(line, pick_ref[k, j])
        count = CH * z.height * z.width
        center = jnp.sum(pixels) / count
        variance = jnp.sum(jnp.square(pixels - center)) / count
        total = jnp.where(inside, (total - center) / jnp.sqrt(variance + 1e-05), 0.0)
        for c in range(CH):
            pad_ref[i, c, margin : margin + blocks, :] = total[c * blocks : (c + 1) * blocks]
    copies = []
    for r in range(z.R):
        parts = [
            pad_ref[i, c, z.rd * r : z.rd * r + z.YB, q * z.lanes : (q + 1) * z.lanes]
            for q in range(z.C)
            for i in range(z.bd)
            for c in range(CH)
        ]
        for k in range(0, len(parts), 2 * CH):
            pair = jnp.concatenate(parts[k : k + 2 * CH], axis=0)
            out_ref[r, k * z.YB : (k + 2 * CH) * z.YB, :] = pair.astype(bf16)
        copy = pltpu.make_async_copy(out_ref.at[r], out_hbm.at[r], out_sems.at[r])
        copy.start()
        copies.append(copy)
    for copy in copies:
        copy.wait()


def split(z, images):
    shape = (z.R, z.C * z.bd * z.T, z.lanes)
    return pl.pallas_call(
        functools.partial(split_kernel, z),
        out_shape=pltpu.HBM(shape, bf16),
        in_specs=[pl.BlockSpec(memory_space=pltpu.HBM)],
        out_specs=pl.BlockSpec(memory_space=pltpu.HBM),
        scratch_shapes=[
            pltpu.VMEM((z.bd, CH, z.height, z.width), bf16),
            pltpu.VMEM((CH, -(-z.width // 128), z.height, 128), f32),
            pltpu.VMEM((z.bd, CH, z.height // S + 2 * PAD // S, z.C * z.lanes), f32),
            pltpu.VMEM((-(-z.width // 128), S, 128, z.C * z.lanes), bf16),
            pltpu.VMEM(shape, bf16),
            pltpu.SemaphoreType.DMA,
            pltpu.SemaphoreType.DMA((z.R,)),
        ],
        compiler_params=pltpu.CompilerParams(vmem_limit_bytes=32 * MIB),
    )(pltpu.with_memory_space_constraint(images, pltpu.HBM))


def spread_kernel(z, weights_ref, out_ref, rows_ref):
    row = lax.broadcasted_iota(jnp.int32, (z.stride, z.F), 0)
    for q in range(z.cd):
        rows_ref[MARGIN : MARGIN + K, :] = weights_ref[0, q].astype(f32)
        inside = (row >= S * q) & (row < S * q + FIELD)
        for i in range(CH * FIELD):
            at = MARGIN + FIELD * i - S * q
            value = jnp.where(inside, rows_ref[at : at + z.stride, :], 0.0)
            out_ref[0, z.stride * i : z.stride * (i + 1), q * z.F : (q + 1) * z.F] = value.astype(bf16)


def spread_weights(z, weights, first, count, space):
    return pl.pallas_call(
        functools.partial(spread_kernel, z),
        grid=(count,),
        out_shape=space((count, z.KW, z.cd * z.F), bf16),
        in_specs=[pl.BlockSpec((1, z.cd, K, z.F), lambda p: (p + first, 0, 0, 0))],
        out_specs=pl.BlockSpec((1, z.KW, z.cd * z.F), lambda p: (p, 0, 0)),
        scratch_shapes=[pltpu.VMEM((K + 2 * MARGIN, z.F), f32)],
        compiler_params=pltpu.CompilerParams(vmem_limit_bytes=32 * MIB),
    )(weights)


def field(z, p, tiles_ref):
    return jnp.concatenate(
        [tiles_ref[c * z.YB + p + g] for c in range(CH) for g in range(GROUP)], axis=1
    )


def encode_kernel(
    z, moved_ref, first_ref, wide_hbm, window_ref, hidden_ref, contrib_ref, swap_ref, cross_ref, wide_ref, rows_ref, sems
):
    B = z.B
    copies = [pltpu.make_async_copy(wide_hbm.at[p], wide_ref.at[p], sems.at[p]) for p in range(z.rd - HELD)]
    for copy in copies[:2]:
        copy.start()
    rows_ref[...] = moved_ref[...].reshape(B * z.T, z.lanes).astype(f32)
    for t in range(z.T):
        window_ref[t] = rows_ref[pl.ds(t, B, stride=z.T), :].astype(bf16)
    contrib_ref[...] = jnp.zeros_like(contrib_ref)
    for first in range(0, z.rd, HELD):
        rows = range(first, min(first + HELD, z.rd))
        for p in rows:
            if p >= HELD:
                copies[p - HELD].wait()
                if p - HELD + 2 < len(copies):
                    copies[p - HELD + 2].start()
        weight = [first_ref.at[p] if p < HELD else wide_ref.at[p - HELD] for p in rows]
        hidden = [dot(field(z, p, window_ref), w[...]).astype(bf16) for p, w in zip(rows, weight)]
        terms = [dot(h, w[...], NT) for h, w in zip(hidden, weight)]
        for p, h, value in zip(rows, hidden, terms):
            for q in range(z.cd):
                hidden_ref[p, q] = h[:, q * z.F : (q + 1) * z.F]
            for c in range(CH):
                for g in range(GROUP):
                    at = (c * GROUP + g) * z.lanes
                    contrib_ref[c * z.YB + p + g] += value[:, at : at + z.lanes]
    half = z.YB // 2
    even = row_is_even()
    for ref, below in ((swap_ref, even), (cross_ref, jnp.logical_not(even))):
        first = jnp.where(below, z.YB - half, 0)
        row = jnp.where(below, z.rd - 2, 0)
        for c in range(CH):
            for y in range(half):
                ref[c * half + y] = contrib_ref[c * z.YB + first + y].astype(bf16)
        for i in range(2):
            for q in range(z.cd):
                ref[CH * half + i * z.cd + q] = hidden_ref[row + i, q]


def encode(z, moved, first, wide):
    B, L = z.B, z.lanes
    vmem = pl.BlockSpec(memory_space=pltpu.VMEM)
    sent = CH * (z.YB // 2) + 2 * z.cd
    shapes = [
        ((z.T, B, L), bf16),
        ((z.rd, z.cd, B, z.F), bf16),
        ((z.T, B, L), f32),
        ((sent, B, L), bf16),
        ((sent, B, L), bf16),
        ((z.rd - HELD, z.KW, z.cd * z.F), bf16),
    ]
    return pl.pallas_call(
        functools.partial(encode_kernel, z),
        out_shape=[pltpu.VMEM(*s) for s in shapes],
        in_specs=[vmem, vmem, pl.BlockSpec(memory_space=pltpu.HBM)],
        out_specs=[vmem] * len(shapes),
        scratch_shapes=[
            pltpu.VMEM((B * z.T, L), f32),
            pltpu.SemaphoreType.DMA((z.rd - HELD,)),
        ],
        compiler_params=pltpu.CompilerParams(vmem_limit_bytes=32 * MIB),
    )(moved, first, pltpu.with_memory_space_constraint(wide, pltpu.HBM))


def turn_fields(z, tile_of, flat_ref):
    for group in range(z.groups):
        for c in range(CH):
            for g in range(GROUP):
                first = c * z.YB + group * z.per + g
                stack = jnp.concatenate([tile_of(first + p) for p in range(z.per)], axis=0)
                at = (c * GROUP + g) * z.lanes
                flat_ref[group, at : at + z.lanes, :] = stack.astype(f32).T


def place_fields(z, q, c, flat_ref, dense_ref, out_ref):
    rows = slice(c * FIELD * FIELD, (c + 1) * FIELD * FIELD)
    for group in range(z.groups):
        for i in range(c * FIELD, (c + 1) * FIELD):
            at = z.stride * i + S * q
            dense_ref[FIELD * i : FIELD * (i + 1), :] = flat_ref[group, at : at + FIELD, :]
        out_ref[group, rows, :] = dense_ref[rows, :].astype(bf16)


def patches_kernel(z, window_ref, out_ref, flat_ref, dense_ref):
    turn_fields(z, lambda t: window_ref[t], flat_ref)
    for q in range(z.cd):
        for c in range(CH):
            place_fields(z, q, c, flat_ref, dense_ref, out_ref.at[q])


def store_residual(z, recon_of, window_ref, resid_ref):
    lane = lax.broadcasted_iota(jnp.int32, (1, z.lanes), 1) % z.stride
    x = lax.axis_index("col") * z.w - PAD + lane
    across = ((x >= 0) & (x < z.width)).astype(f32)
    first = lax.axis_index("row") * z.h - PAD
    for t in range(0, z.T, 2):
        recon = recon_of(t)
        for n in range(2):
            line = first + S * ((t + n) % z.YB)
            inside = jnp.where((line >= 0) & (line < z.height), across, 0.0)
            resid_ref[t + n] = ((recon[n] - window_ref[t + n].astype(f32)) * inside).astype(bf16)


def fill_factor(z, q, resid_ref, pooled_ref, hidden_ref, first_ref, wide_ref, factor_ref):
    B, F = z.B, z.F
    factor_ref[...] = jnp.zeros_like(factor_ref)
    for p in range(z.rd):
        weight = first_ref.at[p] if p < HELD else wide_ref.at[p - HELD]
        back = dot(field(z, p, resid_ref), weight[:, q * F : (q + 1) * F])
        group, at = p // z.per, p % z.per * B
        columns = slice(p % z.per * F, (p % z.per + 1) * F)
        factor_ref[group, at : at + B, columns] = (pooled_ref[p, q] + back).astype(bf16)
        factor_ref[group, 128 + at : 128 + at + B, columns] = hidden_ref[p, q]


def vmem_call(kernel, shapes, scratch, *args):
    vmem = pl.BlockSpec(memory_space=pltpu.VMEM)
    return pl.pallas_call(
        kernel,
        out_shape=[pltpu.VMEM(*s) for s in shapes],
        in_specs=[vmem] * len(args),
        out_specs=[vmem] * len(shapes),
        scratch_shapes=[pltpu.VMEM(*s) for s in scratch],
        compiler_params=pltpu.CompilerParams(vmem_limit_bytes=32 * MIB),
    )(*args)


def is_even():
    return lax.rem(lax.axis_index("col"), 2) == 0


def row_is_even():
    return lax.rem(lax.axis_index("row"), 2) == 0


def pack_side(z, to_right, first, second):
    wide = 2 * PAD
    across = lax.broadcasted_iota(jnp.int32, first.shape, 1) % z.stride
    low = pltpu.roll(first, jnp.where(to_right, z.lanes - z.w, 0), 1)
    high = pltpu.roll(second, jnp.where(to_right, z.lanes - z.w + wide, wide) % z.lanes, 1)
    return jnp.where(across < wide, low, jnp.where(across < 2 * wide, high, 0.0))


def unpack_side(z, from_left, packed):
    wide = 2 * PAD
    across = lax.broadcasted_iota(jnp.int32, packed.shape, 1) % z.stride
    start = jnp.where(from_left, 0, z.w)
    inside = (across >= start) & (across < start + wide)
    first = pltpu.roll(packed, start, 1)
    second = pltpu.roll(packed, (start + z.lanes - wide) % z.lanes, 1)
    return jnp.where(inside, first, 0.0), jnp.where(inside, second, 0.0)


def pack_late(z, to_right, tiles):
    across = lax.broadcasted_iota(jnp.int32, tiles[0].shape, 1) % z.stride
    start = jnp.where(to_right, 2 * z.w, 0)
    packed = jnp.zeros_like(tiles[0])
    for k, tile in enumerate(tiles):
        at = k * z.late
        turned = pltpu.roll(tile, (z.lanes + at - start) % z.lanes, 1)
        packed = jnp.where((across >= at) & (across < at + z.late), turned, packed)
    return packed


def unpack_late(z, from_left, packed, k):
    across = lax.broadcasted_iota(jnp.int32, packed.shape, 1) % z.stride
    start = jnp.where(from_left, 0, 2 * z.w)
    turned = pltpu.roll(packed, (z.lanes + start - k * z.late) % z.lanes, 1)
    return jnp.where((across >= start) & (across < start + z.late), turned, 0.0)


def rows_kernel(
    z, contrib_ref, hidden_ref, swap_ref, cross_ref, sum_ref, tall_ref, near_ref, far_ref, late_ref
):
    half = z.YB // 2
    sum_ref[...] = contrib_ref[...]
    row = lax.axis_index("row")
    even_row = row_is_even()
    above_exists, below_exists = row > 0, row < z.R - 1
    for ref, below in ((swap_ref, even_row), (cross_ref, jnp.logical_not(even_row))):
        exists = jnp.where(below, below_exists, above_exists)
        first = jnp.where(below, z.YB - half, 0)
        for c in range(CH):
            for y in range(half):
                sum_ref[c * z.YB + first + y] += jnp.where(exists, ref[c * half + y].astype(f32), 0.0)
    even = is_even()
    odd = jnp.logical_not(even)
    for t in range(0, z.T, 2):
        pair = sum_ref[t], sum_ref[t + 1]
        far_ref[t // 2] = pack_side(z, odd, *pair).astype(bf16)
        near_ref[t // 2] = pack_side(z, even, *pair).astype(bf16)
    slots = z.stride // z.late
    for t in range(0, z.T, slots):
        late_ref[t // slots] = pack_late(z, even, [sum_ref[t + k] for k in range(slots)]).astype(bf16)
    for q in range(z.cd):
        squares = [jnp.square(hidden_ref[i, q].astype(f32)) for i in range(z.rd)]
        above, below = [], []
        for i in range(2):
            swapped = swap_ref[CH * half + i * z.cd + q].astype(f32)
            crossed = cross_ref[CH * half + i * z.cd + q].astype(f32)
            upper = jnp.where(above_exists, jnp.where(even_row, crossed, swapped), 0.0)
            lower = jnp.where(below_exists, jnp.where(even_row, swapped, crossed), 0.0)
            above.append(jnp.square(upper))
            below.append(jnp.square(lower))
        squares = above + squares + below
        for i in range(z.rd + 2):
            tall_ref[i, q] = squares[i] + squares[i + 1] + squares[i + 2]
    for ref, right in ((near_ref, even), (far_ref, odd)):
        first = jnp.where(right, z.cd - 2, 0)
        for i in range(z.rd + 2):
            for k in range(2):
                ref[z.T // 2 + 2 * i + k] = tall_ref[i, first + k].astype(bf16)


def merge_kernel(
    z, sum_ref, near_ref, far_ref, late_ref, window_ref, hidden_ref, pooled_ref, first_ref, wide_ref,
    out_ref, patch_ref, factor_ref, resid_ref, flat_ref, dense_ref,
):
    even = is_even()
    col = lax.axis_index("col")
    exists = jnp.where(even, col > 0, col < z.C - 1)
    late_exists = jnp.where(even, col > 1, col < z.C - 2)
    slots = z.stride // z.late

    def recon_of(t):
        near = unpack_side(z, jnp.logical_not(even), near_ref[t // 2].astype(f32))
        came = unpack_side(z, even, jnp.where(exists, far_ref[t // 2].astype(f32), 0.0))
        late = jnp.where(late_exists, late_ref[t // slots].astype(f32), 0.0)
        recon = []
        for k in range(2):
            recon.append(sum_ref[t + k] + near[k] + came[k] + unpack_late(z, even, late, t % slots + k))
            out_ref[t + k] = recon[k]
        return recon

    store_residual(z, recon_of, window_ref, resid_ref)
    turn_fields(z, lambda t: resid_ref[t], flat_ref)
    fill_factor(z, z.early, resid_ref, pooled_ref, hidden_ref, first_ref, wide_ref, factor_ref)
    for c in range(CH):
        place_fields(z, z.early, c, flat_ref, dense_ref, patch_ref)


def unpack_last(z, packed):
    even = is_even()
    col = lax.axis_index("col")
    exists = jnp.where(even, col + 1 < z.C - 1, col - 1 > 0)
    across = lax.broadcasted_iota(jnp.int32, packed.shape, 1) % z.stride
    start = jnp.where(even, 2 * z.w, 0)
    inside = (across >= start) & (across < start + z.late) & exists
    by = jnp.where(even, 2 * z.w, z.lanes - z.w)
    first = pltpu.roll(packed, by, 1)
    second = pltpu.roll(packed, (by + z.lanes - 2 * PAD) % z.lanes, 1)
    return jnp.where(inside, first, 0.0), jnp.where(inside, second, 0.0)


def pool_kernel(z, hidden_ref, tall_ref, near_ref, far_ref, out_ref, wide_ref, inverse_ref):
    even = is_even()
    row0 = lax.axis_index("row") * z.rd - 1
    col0 = lax.axis_index("col") * z.cd - 1
    near_at = jnp.where(even, z.cd + 2, 0)
    far_at = jnp.where(even, 0, z.cd + 2)
    exists = jnp.where(even, lax.axis_index("col") > 0, lax.axis_index("col") < z.C - 1)
    for i in range(z.rd + 2):
        for k in range(2):
            wide_ref[near_at + k] = near_ref[z.T // 2 + 2 * i + k].astype(f32)
            wide_ref[far_at + k] = jnp.where(exists, far_ref[z.T // 2 + 2 * i + k].astype(f32), 0.0)
        for q in range(z.cd):
            wide_ref[2 + q] = tall_ref[i, q]
        columns = [wide_ref[q] for q in range(z.cd + 4)]
        for q in range(z.cd + 2):
            energy = jnp.sqrt(1.0 + (columns[q] + columns[q + 1] + columns[q + 2]))
            inverse = (1.0 / energy).astype(bf16).astype(f32)
            row, col = row0 + i, col0 + q
            inside = (row >= 0) & (row < z.R * z.rd) & (col >= 0) & (col < z.C * z.cd)
            inverse_ref[i, q] = inverse * jnp.where(inside, 1.0, 0.0)
    for i in range(z.rd):
        columns = []
        for q in range(z.cd + 2):
            columns.append(inverse_ref[i, q] + inverse_ref[i + 1, q] + inverse_ref[i + 2, q])
        for q in range(z.cd):
            spread = columns[q] + columns[q + 1] + columns[q + 2]
            out_ref[i, q] = sparsity * hidden_ref[i, q].astype(f32) * spread


def grad_kernel(
    z, sum_ref, last_ref, window_ref, patch_ref, hidden_ref, pooled_ref, first_ref, wide_ref,
    early_patch_ref, early_factor_ref,
    out_hbm, resid_ref, flat_ref, dense_ref, resid_patch_ref, factor_ref, out_ref, sems,
):
    B, F = z.B, z.F
    copies = []

    def write(q, k, resid_patch, factor):
        rows = slice(k * FIELD * FIELD, (k + 1) * FIELD * FIELD)
        for group in range(z.groups):
            both = jnp.concatenate([patch_ref[q, group, rows, :], resid_patch[group, rows, :]], axis=1)
            value = dot(both, factor[group]) * (1.0 / B)
            for inner in range(z.per):
                out_ref[group * z.per + inner, q, rows, :] = value[:, inner * F : (inner + 1) * F]
        copy = pltpu.make_async_copy(out_ref.at[:, q, rows, :], out_hbm.at[:, q, rows, :], sems.at[q, k])
        copy.start()
        copies.append(copy)

    for k in range(CH):
        write(z.early, k, early_patch_ref, early_factor_ref)

    def recon_of(t):
        came = unpack_last(z, last_ref[t // 2].astype(f32))
        return [sum_ref[t + k] + came[k] for k in range(2)]

    store_residual(z, recon_of, window_ref, resid_ref)
    turn_fields(z, lambda t: resid_ref[t], flat_ref)
    for q in range(z.cd):
        if q == z.early:
            continue
        fill_factor(z, q, resid_ref, pooled_ref, hidden_ref, first_ref, wide_ref, factor_ref.at[q])
        for k in range(CH):
            place_fields(z, q, k, flat_ref, dense_ref, resid_patch_ref.at[q])
            write(q, k, resid_patch_ref.at[q], factor_ref.at[q])
    for copy in copies:
        copy.wait()


def gradient(z, *args):
    B, F, L = z.B, z.F, z.lanes
    return pl.pallas_call(
        functools.partial(grad_kernel, z),
        out_shape=pltpu.HBM((z.rd, z.cd, K, F), f32),
        in_specs=[pl.BlockSpec(memory_space=pltpu.VMEM)] * len(args),
        out_specs=pl.BlockSpec(memory_space=pltpu.HBM),
        scratch_shapes=[
            pltpu.VMEM((z.T, B, L), bf16),
            pltpu.VMEM((z.groups, z.KW, 128), f32),
            pltpu.VMEM((K, 128), f32),
            pltpu.VMEM((z.cd, z.groups, K, 128), bf16),
            pltpu.VMEM((z.cd, z.groups, 256, z.per * F), bf16),
            pltpu.VMEM((z.rd, z.cd, K, F), f32),
            pltpu.SemaphoreType.DMA((z.cd, CH)),
        ],
        compiler_params=pltpu.CompilerParams(vmem_limit_bytes=40 * MIB),
    )(*args)


def exchange(z, value, partner):
    pairs = []
    for r in range(z.R):
        for c in range(z.C):
            to = partner(z, r, c)
            pairs.append((r * z.C + c, to[0] * z.C + to[1]))
    return lax.ppermute(value, ("row", "col"), pairs)


def shift(z, value):
    pairs = []
    for r in range(z.R):
        for c in range(z.C):
            to = (c + (-2 if c % 2 else 2)) % z.C
            pairs.append((r * z.C + c, r * z.C + to))
    return lax.ppermute(value, ("row", "col"), pairs)


def cross_row(z, r, c):
    to = r + 1 if r % 2 else r - 1
    return (to, c) if 0 <= to < z.R else (r, c ^ 1)


def swap_col(z, r, c):
    return (r, c ^ 1)


def cross_col(z, r, c):
    to = c + 1 if c % 2 else c - 1
    return (r, to) if 0 <= to < z.C else (r ^ 1, c)


def body(z, images, weights):
    B, L = z.B, z.lanes
    tiles = ((z.T, B, L), f32)
    blocks = split(z, images)
    moved = lax.all_to_all(
        blocks.reshape(z.R * z.C, z.bd * z.T, L), ("row", "col"), split_axis=0, concat_axis=0, tiled=True
    ).reshape(B, z.T, L)
    turned = jnp.swapaxes(weights, 2, 3)
    wide_first = spread_weights(z, turned, 0, HELD, pltpu.VMEM)
    wide = spread_weights(z, turned, HELD, z.rd - HELD, pltpu.HBM)
    window, hidden, contrib, to_swap, to_cross, wide = encode(z, moved, wide_first, wide)
    crossed = exchange(z, to_cross, cross_row)
    swapped = exchange(z, to_swap, lambda z, r, c: (r ^ 1, c))
    tall = ((z.rd + 2, z.cd, B, z.F), f32)
    sent = ((z.T // 2 + 2 * (z.rd + 2), B, L), bf16)
    late = ((z.T * z.late // z.stride, B, L), bf16)
    total, tall, to_near, to_far, to_late = vmem_call(
        functools.partial(rows_kernel, z), [tiles, tall, sent, sent, late], [], contrib, hidden, swapped, crossed
    )
    far = exchange(z, to_far, cross_col)
    late = shift(z, to_late)
    near = exchange(z, to_near, swap_col)
    (patch,) = vmem_call(
        functools.partial(patches_kernel, z),
        [((z.cd, z.groups, K, 128), bf16)],
        [((z.groups, z.KW, 128), f32), ((K, 128), f32)],
        window,
    )
    far, near, late, patch = lax.optimization_barrier((far, near, late, patch))
    last = exchange(z, far[: z.T // 2], swap_col)
    (pooled,) = vmem_call(
        functools.partial(pool_kernel, z),
        [((z.rd, z.cd, B, z.F), f32)],
        [((z.cd + 4, B, z.F), f32), ((z.rd + 2, z.cd + 2, B, z.F), f32)],
        hidden, tall, near, far,
    )
    total, early_patch, early_factor = vmem_call(
        functools.partial(merge_kernel, z),
        [tiles, ((z.groups, K, 128), bf16), ((z.groups, 256, z.per * z.F), bf16)],
        [((z.T, B, L), bf16), ((z.groups, z.KW, 128), f32), ((K, 128), f32)],
        total, near, far, late, window, hidden, pooled, wide_first, wide,
    )
    out = gradient(
        z, total, last, window, patch, hidden, pooled, wide_first, wide, early_patch, early_factor
    )
    return jnp.swapaxes(out, 2, 3)


def solution(mesh):
    def run(images, weights):
        z = Sizes(
            (images.shape[0] // (mesh.shape["row"] * mesh.shape["col"]),) + images.shape[1:],
            (weights.shape[0] // mesh.shape["row"], weights.shape[1] // mesh.shape["col"]) + weights.shape[2:],
            mesh,
        )
        return jax.shard_map(
            functools.partial(body, z),
            mesh=mesh,
            in_specs=(P(("row", "col"), None, None, None), P("row", "col", None, None)),
            out_specs=P("row", "col", None, None),
            check_vma=False,
        )(images, weights)

    return run
```

```python
import functools

import jax
import jax.numpy as jnp
from jax import lax
from jax.experimental import pallas as pl
from jax.experimental.pallas import tpu as pltpu
from jax.sharding import PartitionSpec as P

CH = 3
S = 4
FIELD = 20
PAD = 8
K = 1200
MARGIN = 16
HELD = 2
GROUP = FIELD // S

sparsity = 0.5
f32 = jnp.float32
bf16 = jnp.bfloat16
NT = (((1,), (1,)), ((), ()))
NN = (((1,), (0,)), ((), ()))
TN = (((0,), (0,)), ((), ()))
MIB = 1024 * 1024


def dot(a, b, dims=NN):
    return lax.dot_general(a, b, dims, preferred_element_type=f32)


class Sizes:
    def __init__(self, images, weights, mesh):
        self.R, self.C = mesh.shape["row"], mesh.shape["col"]
        self.bd = images[0]
        self.height, self.width = images[2], images[3]
        self.rd, self.cd, self.F = weights[0], weights[1], weights[2]
        self.B = self.bd * self.R * self.C
        self.h, self.w = S * self.rd, S * self.cd
        self.ext = self.w + 2 * PAD
        self.stride = -(-self.ext // 32) * 32
        self.lanes = S * self.stride
        self.YB = self.rd + 2 * PAD // S
        self.T = CH * self.YB
        self.late = 2 * PAD - self.w
        late_even = [q for q in range(self.cd) if S * q + FIELD > 2 * self.w]
        late_odd = [q for q in range(self.cd) if S * q < self.late]
        self.early = next(q for q in range(self.cd) if q not in late_even + late_odd)
        self.KW = CH * FIELD * self.stride
        self.per = 128 // self.B
        self.groups = self.rd // self.per
        assert self.late > 0 and self.stride % self.late == 0 and self.T % (self.stride // self.late) == 0
        assert self.B * self.per == 128 and self.groups * self.per == self.rd and self.F == 128
        assert self.C % 2 == 0 and self.R % 2 == 0 and self.YB % 2 == 0 and self.rd >= 4 and self.cd >= 2 and self.lanes == 128
        assert self.height == self.R * self.h and self.width == self.C * self.w


def split_kernel(z, images_hbm, out_hbm, images_ref, rows_ref, pad_ref, pick_ref, out_ref, in_sem, out_sems):
    load = pltpu.make_async_copy(images_hbm, images_ref, in_sem)
    load.start()
    margin = PAD // S
    blocks = z.height // S
    n = lax.broadcasted_iota(jnp.int32, (1, z.C * z.lanes), 1)
    column = n // z.lanes
    inner = n % z.lanes
    lane_row = inner // z.stride
    across = inner % z.stride
    source = jnp.where(across < z.ext, z.w * column - PAD + across, -1)
    pixel = lax.broadcasted_iota(jnp.int32, (128, z.C * z.lanes), 0)
    chunks = rows_ref.shape[1]
    for k in range(chunks):
        for j in range(S):
            wanted = jnp.where(lane_row == j, source - 128 * k, -1)
            pick_ref[k, j] = (pixel == wanted).astype(f32).astype(bf16)
    rows_ref[...] = jnp.zeros_like(rows_ref)
    pad_ref[...] = jnp.zeros_like(pad_ref)
    inside = (source >= 0) & (source < z.width)
    load.wait()
    for i in range(z.bd):
        pixels = images_ref[i].astype(f32)
        for k in range(chunks):
            stop = min(128, z.width - 128 * k)
            rows_ref[:, k, :, :stop] = pixels[:, :, 128 * k : 128 * k + stop]
        total = jnp.zeros((CH * blocks, z.C * z.lanes), f32)
        for k in range(chunks):
            for j in range(S):
                line = jnp.concatenate(
                    [rows_ref[c, k, pl.ds(j, blocks, stride=S), :] for c in range(CH)], axis=0
                ).astype(bf16)
                total = total + dot(line, pick_ref[k, j])
        count = CH * z.height * z.width
        center = jnp.sum(pixels) / count
        variance = jnp.sum(jnp.square(pixels - center)) / count
        total = jnp.where(inside, (total - center) / jnp.sqrt(variance + 1e-05), 0.0)
        for c in range(CH):
            pad_ref[i, c, margin : margin + blocks, :] = total[c * blocks : (c + 1) * blocks]
    copies = []
    for r in range(z.R):
        parts = [
            pad_ref[i, c, z.rd * r : z.rd * r + z.YB, q * z.lanes : (q + 1) * z.lanes]
            for q in range(z.C)
            for i in range(z.bd)
            for c in range(CH)
        ]
        for k in range(0, len(parts), 2 * CH):
            pair = jnp.concatenate(parts[k : k + 2 * CH], axis=0)
            out_ref[r, k * z.YB : (k + 2 * CH) * z.YB, :] = pair.astype(bf16)
        copy = pltpu.make_async_copy(out_ref.at[r], out_hbm.at[r], out_sems.at[r])
        copy.start()
        copies.append(copy)
    for copy in copies:
        copy.wait()


def split(z, images):
    shape = (z.R, z.C * z.bd * z.T, z.lanes)
    return pl.pallas_call(
        functools.partial(split_kernel, z),
        out_shape=pltpu.HBM(shape, bf16),
        in_specs=[pl.BlockSpec(memory_space=pltpu.HBM)],
        out_specs=pl.BlockSpec(memory_space=pltpu.HBM),
        scratch_shapes=[
            pltpu.VMEM((z.bd, CH, z.height, z.width), bf16),
            pltpu.VMEM((CH, -(-z.width // 128), z.height, 128), f32),
            pltpu.VMEM((z.bd, CH, z.height // S + 2 * PAD // S, z.C * z.lanes), f32),
            pltpu.VMEM((-(-z.width // 128), S, 128, z.C * z.lanes), bf16),
            pltpu.VMEM(shape, bf16),
            pltpu.SemaphoreType.DMA,
            pltpu.SemaphoreType.DMA((z.R,)),
        ],
        compiler_params=pltpu.CompilerParams(vmem_limit_bytes=32 * MIB),
    )(pltpu.with_memory_space_constraint(images, pltpu.HBM))


def spread_kernel(z, weights_ref, out_ref, rows_ref):
    row = lax.broadcasted_iota(jnp.int32, (z.stride, z.F), 0)
    for q in range(z.cd):
        rows_ref[MARGIN : MARGIN + K, :] = weights_ref[0, q].astype(f32)
        inside = (row >= S * q) & (row < S * q + FIELD)
        for i in range(CH * FIELD):
            at = MARGIN + FIELD * i - S * q
            value = jnp.where(inside, rows_ref[at : at + z.stride, :], 0.0)
            out_ref[0, z.stride * i : z.stride * (i + 1), q * z.F : (q + 1) * z.F] = value.astype(bf16)


def spread_weights(z, weights, first, count, space):
    return pl.pallas_call(
        functools.partial(spread_kernel, z),
        grid=(count,),
        out_shape=space((count, z.KW, z.cd * z.F), bf16),
        in_specs=[pl.BlockSpec((1, z.cd, K, z.F), lambda p: (p + first, 0, 0, 0))],
        out_specs=pl.BlockSpec((1, z.KW, z.cd * z.F), lambda p: (p, 0, 0)),
        scratch_shapes=[pltpu.VMEM((K + 2 * MARGIN, z.F), f32)],
        compiler_params=pltpu.CompilerParams(vmem_limit_bytes=32 * MIB),
    )(weights)


def field(z, p, tiles_ref):
    return jnp.concatenate(
        [tiles_ref[c * z.YB + p + g] for c in range(CH) for g in range(GROUP)], axis=1
    )


def encode_kernel(
    z, moved_ref, first_ref, wide_hbm, window_ref, hidden_ref, contrib_ref, swap_ref, cross_ref, wide_ref, rows_ref, sems
):
    B = z.B
    copies = [pltpu.make_async_copy(wide_hbm.at[p], wide_ref.at[p], sems.at[p]) for p in range(z.rd - HELD)]
    for copy in copies[:2]:
        copy.start()
    rows_ref[...] = moved_ref[...].reshape(B * z.T, z.lanes).astype(f32)
    for t in range(z.T):
        window_ref[t] = rows_ref[pl.ds(t, B, stride=z.T), :].astype(bf16)
    contrib_ref[...] = jnp.zeros_like(contrib_ref)
    for first in range(0, z.rd, HELD):
        rows = range(first, min(first + HELD, z.rd))
        for p in rows:
            if p >= HELD:
                copies[p - HELD].wait()
                if p - HELD + 2 < len(copies):
                    copies[p - HELD + 2].start()
        weight = [first_ref.at[p] if p < HELD else wide_ref.at[p - HELD] for p in rows]
        hidden = [dot(field(z, p, window_ref), w[...]).astype(bf16) for p, w in zip(rows, weight)]
        terms = [dot(h, w[...], NT) for h, w in zip(hidden, weight)]
        for p, h, value in zip(rows, hidden, terms):
            for q in range(z.cd):
                hidden_ref[p, q] = h[:, q * z.F : (q + 1) * z.F]
            for c in range(CH):
                for g in range(GROUP):
                    at = (c * GROUP + g) * z.lanes
                    contrib_ref[c * z.YB + p + g] += value[:, at : at + z.lanes]
    half = z.YB // 2
    even = row_is_even()
    for ref, below in ((swap_ref, even), (cross_ref, jnp.logical_not(even))):
        first = jnp.where(below, z.YB - half, 0)
        row = jnp.where(below, z.rd - 2, 0)
        for c in range(CH):
            for y in range(half):
                ref[c * half + y] = contrib_ref[c * z.YB + first + y].astype(bf16)
        for i in range(2):
            for q in range(z.cd):
                ref[CH * half + i * z.cd + q] = hidden_ref[row + i, q]


def encode(z, moved, first, wide):
    B, L = z.B, z.lanes
    vmem = pl.BlockSpec(memory_space=pltpu.VMEM)
    sent = CH * (z.YB // 2) + 2 * z.cd
    shapes = [
        ((z.T, B, L), bf16),
        ((z.rd, z.cd, B, z.F), bf16),
        ((z.T, B, L), f32),
        ((sent, B, L), bf16),
        ((sent, B, L), bf16),
        ((z.rd - HELD, z.KW, z.cd * z.F), bf16),
    ]
    return pl.pallas_call(
        functools.partial(encode_kernel, z),
        out_shape=[pltpu.VMEM(*s) for s in shapes],
        in_specs=[vmem, vmem, pl.BlockSpec(memory_space=pltpu.HBM)],
        out_specs=[vmem] * len(shapes),
        scratch_shapes=[
            pltpu.VMEM((B * z.T, L), f32),
            pltpu.SemaphoreType.DMA((z.rd - HELD,)),
        ],
        compiler_params=pltpu.CompilerParams(vmem_limit_bytes=32 * MIB),
    )(moved, first, pltpu.with_memory_space_constraint(wide, pltpu.HBM))


def turn_fields(z, tile_of, flat_ref):
    for group in range(z.groups):
        for c in range(CH):
            for g in range(GROUP):
                first = c * z.YB + group * z.per + g
                stack = jnp.concatenate([tile_of(first + p) for p in range(z.per)], axis=0)
                at = (c * GROUP + g) * z.lanes
                flat_ref[group, at : at + z.lanes, :] = stack.astype(f32).T


def place_fields(z, q, c, flat_ref, dense_ref, out_ref):
    rows = slice(c * FIELD * FIELD, (c + 1) * FIELD * FIELD)
    for group in range(z.groups):
        for i in range(c * FIELD, (c + 1) * FIELD):
            at = z.stride * i + S * q
            dense_ref[FIELD * i : FIELD * (i + 1), :] = flat_ref[group, at : at + FIELD, :]
        out_ref[group, rows, :] = dense_ref[rows, :].astype(bf16)


def patches_kernel(z, window_ref, out_ref, flat_ref, dense_ref):
    turn_fields(z, lambda t: window_ref[t], flat_ref)
    for q in range(z.cd):
        for c in range(CH):
            place_fields(z, q, c, flat_ref, dense_ref, out_ref.at[q])


def store_residual(z, recon_of, window_ref, resid_ref):
    lane = lax.broadcasted_iota(jnp.int32, (1, z.lanes), 1) % z.stride
    x = lax.axis_index("col") * z.w - PAD + lane
    across = ((x >= 0) & (x < z.width)).astype(f32)
    first = lax.axis_index("row") * z.h - PAD
    for t in range(0, z.T, 2):
        recon = recon_of(t)
        for n in range(2):
            line = first + S * ((t + n) % z.YB)
            inside = jnp.where((line >= 0) & (line < z.height), across, 0.0)
            resid_ref[t + n] = ((recon[n] - window_ref[t + n].astype(f32)) * inside).astype(bf16)


def fill_factor(z, q, resid_ref, pooled_ref, hidden_ref, first_ref, wide_ref, factor_ref):
    B, F = z.B, z.F
    factor_ref[...] = jnp.zeros_like(factor_ref)
    for p in range(z.rd):
        weight = first_ref.at[p] if p < HELD else wide_ref.at[p - HELD]
        back = dot(field(z, p, resid_ref), weight[:, q * F : (q + 1) * F])
        group, at = p // z.per, p % z.per * B
        columns = slice(p % z.per * F, (p % z.per + 1) * F)
        factor_ref[group, at : at + B, columns] = (pooled_ref[p, q] + back).astype(bf16)
        factor_ref[group, 128 + at : 128 + at + B, columns] = hidden_ref[p, q]


def vmem_call(kernel, shapes, scratch, *args):
    vmem = pl.BlockSpec(memory_space=pltpu.VMEM)
    return pl.pallas_call(
        kernel,
        out_shape=[pltpu.VMEM(*s) for s in shapes],
        in_specs=[vmem] * len(args),
        out_specs=[vmem] * len(shapes),
        scratch_shapes=[pltpu.VMEM(*s) for s in scratch],
        compiler_params=pltpu.CompilerParams(vmem_limit_bytes=32 * MIB),
    )(*args)


def is_even():
    return lax.rem(lax.axis_index("col"), 2) == 0


def row_is_even():
    return lax.rem(lax.axis_index("row"), 2) == 0


def pack_side(z, to_right, first, second):
    wide = 2 * PAD
    across = lax.broadcasted_iota(jnp.int32, first.shape, 1) % z.stride
    low = pltpu.roll(first, jnp.where(to_right, z.lanes - z.w, 0), 1)
    high = pltpu.roll(second, jnp.where(to_right, z.lanes - z.w + wide, wide) % z.lanes, 1)
    return jnp.where(across < wide, low, jnp.where(across < 2 * wide, high, 0.0))


def unpack_side(z, from_left, packed):
    wide = 2 * PAD
    across = lax.broadcasted_iota(jnp.int32, packed.shape, 1) % z.stride
    start = jnp.where(from_left, 0, z.w)
    inside = (across >= start) & (across < start + wide)
    first = pltpu.roll(packed, start, 1)
    second = pltpu.roll(packed, (start + z.lanes - wide) % z.lanes, 1)
    return jnp.where(inside, first, 0.0), jnp.where(inside, second, 0.0)


def pack_late(z, to_right, tiles):
    across = lax.broadcasted_iota(jnp.int32, tiles[0].shape, 1) % z.stride
    start = jnp.where(to_right, 2 * z.w, 0)
    packed = jnp.zeros_like(tiles[0])
    for k, tile in enumerate(tiles):
        at = k * z.late
        turned = pltpu.roll(tile, (z.lanes + at - start) % z.lanes, 1)
        packed = jnp.where((across >= at) & (across < at + z.late), turned, packed)
    return packed


def unpack_late(z, from_left, packed, k):
    across = lax.broadcasted_iota(jnp.int32, packed.shape, 1) % z.stride
    start = jnp.where(from_left, 0, 2 * z.w)
    turned = pltpu.roll(packed, (z.lanes + start - k * z.late) % z.lanes, 1)
    return jnp.where((across >= start) & (across < start + z.late), turned, 0.0)


def rows_kernel(
    z, contrib_ref, hidden_ref, swap_ref, cross_ref, sum_ref, tall_ref, near_ref, far_ref, late_ref
):
    half = z.YB // 2
    row = lax.axis_index("row")
    even_row = row_is_even()
    above_exists, below_exists = row > 0, row < z.R - 1
    for ref, below in ((swap_ref, even_row), (cross_ref, jnp.logical_not(even_row))):
        exists = jnp.where(below, below_exists, above_exists)
        first = jnp.where(below, z.YB - half, 0)
        for c in range(CH):
            for y in range(half):
                t = c * z.YB + first + y
                sum_ref[t] = contrib_ref[t] + jnp.where(exists, ref[c * half + y].astype(f32), 0.0)
    even = is_even()
    odd = jnp.logical_not(even)
    for t in range(0, z.T, 2):
        pair = sum_ref[t], sum_ref[t + 1]
        far_ref[t // 2] = pack_side(z, odd, *pair).astype(bf16)
        near_ref[t // 2] = pack_side(z, even, *pair).astype(bf16)
    slots = z.stride // z.late
    for t in range(0, z.T, slots):
        late_ref[t // slots] = pack_late(z, even, [sum_ref[t + k] for k in range(slots)]).astype(bf16)
    for q in range(z.cd):
        squares = [jnp.square(hidden_ref[i, q].astype(f32)) for i in range(z.rd)]
        above, below = [], []
        for i in range(2):
            swapped = swap_ref[CH * half + i * z.cd + q].astype(f32)
            crossed = cross_ref[CH * half + i * z.cd + q].astype(f32)
            upper = jnp.where(above_exists, jnp.where(even_row, crossed, swapped), 0.0)
            lower = jnp.where(below_exists, jnp.where(even_row, swapped, crossed), 0.0)
            above.append(jnp.square(upper))
            below.append(jnp.square(lower))
        squares = above + squares + below
        for i in range(z.rd + 2):
            tall_ref[i, q] = squares[i] + squares[i + 1] + squares[i + 2]
    for ref, right in ((near_ref, even), (far_ref, odd)):
        first = jnp.where(right, z.cd - 2, 0)
        for i in range(z.rd + 2):
            for k in range(2):
                ref[z.T // 2 + 2 * i + k] = tall_ref[i, first + k].astype(bf16)


def merge_kernel(
    z, sum_ref, near_ref, far_ref, late_ref, window_ref, hidden_ref, pooled_ref, first_ref, wide_ref,
    out_ref, patch_ref, factor_ref, resid_ref, flat_ref, dense_ref,
):
    even = is_even()
    col = lax.axis_index("col")
    exists = jnp.where(even, col > 0, col < z.C - 1)
    late_exists = jnp.where(even, col > 1, col < z.C - 2)
    slots = z.stride // z.late

    def recon_of(t):
        near = unpack_side(z, jnp.logical_not(even), near_ref[t // 2].astype(f32))
        came = unpack_side(z, even, jnp.where(exists, far_ref[t // 2].astype(f32), 0.0))
        late = jnp.where(late_exists, late_ref[t // slots].astype(f32), 0.0)
        recon = []
        for k in range(2):
            recon.append(sum_ref[t + k] + near[k] + came[k] + unpack_late(z, even, late, t % slots + k))
            out_ref[t + k] = recon[k]
        return recon

    store_residual(z, recon_of, window_ref, resid_ref)
    turn_fields(z, lambda t: resid_ref[t], flat_ref)
    fill_factor(z, z.early, resid_ref, pooled_ref, hidden_ref, first_ref, wide_ref, factor_ref)
    for c in range(CH):
        place_fields(z, z.early, c, flat_ref, dense_ref, patch_ref)


def unpack_last(z, packed):
    even = is_even()
    col = lax.axis_index("col")
    exists = jnp.where(even, col + 1 < z.C - 1, col - 1 > 0)
    across = lax.broadcasted_iota(jnp.int32, packed.shape, 1) % z.stride
    start = jnp.where(even, 2 * z.w, 0)
    inside = (across >= start) & (across < start + z.late) & exists
    by = jnp.where(even, 2 * z.w, z.lanes - z.w)
    first = pltpu.roll(packed, by, 1)
    second = pltpu.roll(packed, (by + z.lanes - 2 * PAD) % z.lanes, 1)
    return jnp.where(inside, first, 0.0), jnp.where(inside, second, 0.0)


def pool_kernel(z, hidden_ref, tall_ref, near_ref, far_ref, out_ref, wide_ref, inverse_ref):
    even = is_even()
    row0 = lax.axis_index("row") * z.rd - 1
    col0 = lax.axis_index("col") * z.cd - 1
    near_at = jnp.where(even, z.cd + 2, 0)
    far_at = jnp.where(even, 0, z.cd + 2)
    exists = jnp.where(even, lax.axis_index("col") > 0, lax.axis_index("col") < z.C - 1)
    for i in range(z.rd + 2):
        for k in range(2):
            wide_ref[near_at + k] = near_ref[z.T // 2 + 2 * i + k].astype(f32)
            wide_ref[far_at + k] = jnp.where(exists, far_ref[z.T // 2 + 2 * i + k].astype(f32), 0.0)
        for q in range(z.cd):
            wide_ref[2 + q] = tall_ref[i, q]
        columns = [wide_ref[q] for q in range(z.cd + 4)]
        for q in range(z.cd + 2):
            energy = jnp.sqrt(1.0 + (columns[q] + columns[q + 1] + columns[q + 2]))
            inverse = (1.0 / energy).astype(bf16).astype(f32)
            row, col = row0 + i, col0 + q
            inside = (row >= 0) & (row < z.R * z.rd) & (col >= 0) & (col < z.C * z.cd)
            inverse_ref[i, q] = inverse * jnp.where(inside, 1.0, 0.0)
    for i in range(z.rd):
        columns = []
        for q in range(z.cd + 2):
            columns.append(inverse_ref[i, q] + inverse_ref[i + 1, q] + inverse_ref[i + 2, q])
        for q in range(z.cd):
            spread = columns[q] + columns[q + 1] + columns[q + 2]
            out_ref[i, q] = sparsity * hidden_ref[i, q].astype(f32) * spread


def grad_kernel(
    z, sum_ref, last_ref, window_ref, patch_ref, hidden_ref, pooled_ref, first_ref, wide_ref,
    early_patch_ref, early_factor_ref,
    out_hbm, resid_ref, flat_ref, dense_ref, resid_patch_ref, factor_ref, out_ref, sems,
):
    B, F = z.B, z.F
    copies = []

    def write(q, k, resid_patch, factor):
        rows = slice(k * FIELD * FIELD, (k + 1) * FIELD * FIELD)
        for group in range(z.groups):
            both = jnp.concatenate([patch_ref[q, group, rows, :], resid_patch[group, rows, :]], axis=1)
            value = dot(both, factor[group]) * (1.0 / B)
            for inner in range(z.per):
                out_ref[group * z.per + inner, q, rows, :] = value[:, inner * F : (inner + 1) * F]
        copy = pltpu.make_async_copy(out_ref.at[:, q, rows, :], out_hbm.at[:, q, rows, :], sems.at[q, k])
        copy.start()
        copies.append(copy)

    for k in range(CH):
        write(z.early, k, early_patch_ref, early_factor_ref)

    def recon_of(t):
        came = unpack_last(z, last_ref[t // 2].astype(f32))
        return [sum_ref[t + k] + came[k] for k in range(2)]

    store_residual(z, recon_of, window_ref, resid_ref)
    turn_fields(z, lambda t: resid_ref[t], flat_ref)
    for q in range(z.cd):
        if q == z.early:
            continue
        fill_factor(z, q, resid_ref, pooled_ref, hidden_ref, first_ref, wide_ref, factor_ref.at[q])
        for k in range(CH):
            place_fields(z, q, k, flat_ref, dense_ref, resid_patch_ref.at[q])
            write(q, k, resid_patch_ref.at[q], factor_ref.at[q])
    for copy in copies:
        copy.wait()


def gradient(z, *args):
    B, F, L = z.B, z.F, z.lanes
    return pl.pallas_call(
        functools.partial(grad_kernel, z),
        out_shape=pltpu.HBM((z.rd, z.cd, K, F), f32),
        in_specs=[pl.BlockSpec(memory_space=pltpu.VMEM)] * len(args),
        out_specs=pl.BlockSpec(memory_space=pltpu.HBM),
        scratch_shapes=[
            pltpu.VMEM((z.T, B, L), bf16),
            pltpu.VMEM((z.groups, z.KW, 128), f32),
            pltpu.VMEM((K, 128), f32),
            pltpu.VMEM((z.cd, z.groups, K, 128), bf16),
            pltpu.VMEM((z.cd, z.groups, 256, z.per * F), bf16),
            pltpu.VMEM((z.rd, z.cd, K, F), f32),
            pltpu.SemaphoreType.DMA((z.cd, CH)),
        ],
        compiler_params=pltpu.CompilerParams(vmem_limit_bytes=40 * MIB),
    )(*args)


def exchange(z, value, partner):
    pairs = []
    for r in range(z.R):
        for c in range(z.C):
            to = partner(z, r, c)
            pairs.append((r * z.C + c, to[0] * z.C + to[1]))
    return lax.ppermute(value, ("row", "col"), pairs)


def shift(z, value):
    pairs = []
    for r in range(z.R):
        for c in range(z.C):
            to = (c + (-2 if c % 2 else 2)) % z.C
            pairs.append((r * z.C + c, r * z.C + to))
    return lax.ppermute(value, ("row", "col"), pairs)


def cross_row(z, r, c):
    to = r + 1 if r % 2 else r - 1
    return (to, c) if 0 <= to < z.R else (r, c ^ 1)


def swap_col(z, r, c):
    return (r, c ^ 1)


def cross_col(z, r, c):
    to = c + 1 if c % 2 else c - 1
    return (r, to) if 0 <= to < z.C else (r ^ 1, c)


def body(z, images, weights):
    B, L = z.B, z.lanes
    tiles = ((z.T, B, L), f32)
    blocks = split(z, images)
    moved = lax.all_to_all(
        blocks.reshape(z.R * z.C, z.bd * z.T, L), ("row", "col"), split_axis=0, concat_axis=0, tiled=True
    ).reshape(B, z.T, L)
    turned = jnp.swapaxes(weights, 2, 3)
    wide_first = spread_weights(z, turned, 0, HELD, pltpu.VMEM)
    wide = spread_weights(z, turned, HELD, z.rd - HELD, pltpu.HBM)
    window, hidden, contrib, to_swap, to_cross, wide = encode(z, moved, wide_first, wide)
    crossed = exchange(z, to_cross, cross_row)
    swapped = exchange(z, to_swap, lambda z, r, c: (r ^ 1, c))
    tall = ((z.rd + 2, z.cd, B, z.F), f32)
    sent = ((z.T // 2 + 2 * (z.rd + 2), B, L), bf16)
    late = ((z.T * z.late // z.stride, B, L), bf16)
    total, tall, to_near, to_far, to_late = vmem_call(
        functools.partial(rows_kernel, z), [tiles, tall, sent, sent, late], [], contrib, hidden, swapped, crossed
    )
    far = exchange(z, to_far, cross_col)
    late = shift(z, to_late)
    near = exchange(z, to_near, swap_col)
    (patch,) = vmem_call(
        functools.partial(patches_kernel, z),
        [((z.cd, z.groups, K, 128), bf16)],
        [((z.groups, z.KW, 128), f32), ((K, 128), f32)],
        window,
    )
    far, near, late, patch = lax.optimization_barrier((far, near, late, patch))
    last = exchange(z, far[: z.T // 2], swap_col)
    (pooled,) = vmem_call(
        functools.partial(pool_kernel, z),
        [((z.rd, z.cd, B, z.F), f32)],
        [((z.cd + 4, B, z.F), f32), ((z.rd + 2, z.cd + 2, B, z.F), f32)],
        hidden, tall, near, far,
    )
    total, early_patch, early_factor = vmem_call(
        functools.partial(merge_kernel, z),
        [tiles, ((z.groups, K, 128), bf16), ((z.groups, 256, z.per * z.F), bf16)],
        [((z.T, B, L), bf16), ((z.groups, z.KW, 128), f32), ((K, 128), f32)],
        total, near, far, late, window, hidden, pooled, wide_first, wide,
    )
    out = gradient(
        z, total, last, window, patch, hidden, pooled, wide_first, wide, early_patch, early_factor
    )
    return jnp.swapaxes(out, 2, 3)


def solution(mesh):
    def run(images, weights):
        z = Sizes(
            (images.shape[0] // (mesh.shape["row"] * mesh.shape["col"]),) + images.shape[1:],
            (weights.shape[0] // mesh.shape["row"], weights.shape[1] // mesh.shape["col"]) + weights.shape[2:],
            mesh,
        )
        return jax.shard_map(
            functools.partial(body, z),
            mesh=mesh,
            in_specs=(P(("row", "col"), None, None, None), P("row", "col", None, None)),
            out_specs=P("row", "col", None, None),
            check_vma=False,
        )(images, weights)

    return run
```

```python
import functools

import jax
import jax.numpy as jnp
from jax import lax
from jax.experimental import pallas as pl
from jax.experimental.pallas import tpu as pltpu
from jax.sharding import PartitionSpec as P

CH = 3
S = 4
FIELD = 20
PAD = 8
K = 1200
MARGIN = 16
HELD = 2
GROUP = FIELD // S

sparsity = 0.5
f32 = jnp.float32
bf16 = jnp.bfloat16
NT = (((1,), (1,)), ((), ()))
NN = (((1,), (0,)), ((), ()))
TN = (((0,), (0,)), ((), ()))
MIB = 1024 * 1024


def dot(a, b, dims=NN):
    return lax.dot_general(a, b, dims, preferred_element_type=f32)


class Sizes:
    def __init__(self, images, weights, mesh):
        self.R, self.C = mesh.shape["row"], mesh.shape["col"]
        self.bd = images[0]
        self.height, self.width = images[2], images[3]
        self.rd, self.cd, self.F = weights[0], weights[1], weights[2]
        self.B = self.bd * self.R * self.C
        self.h, self.w = S * self.rd, S * self.cd
        self.ext = self.w + 2 * PAD
        self.stride = -(-self.ext // 32) * 32
        self.lanes = S * self.stride
        self.YB = self.rd + 2 * PAD // S
        self.T = CH * self.YB
        self.late = 2 * PAD - self.w
        late_even = [q for q in range(self.cd) if S * q + FIELD > 2 * self.w]
        late_odd = [q for q in range(self.cd) if S * q < self.late]
        self.early = next(q for q in range(self.cd) if q not in late_even + late_odd)
        self.KW = CH * FIELD * self.stride
        self.per = 128 // self.B
        self.groups = self.rd // self.per
        assert self.late > 0 and self.stride % self.late == 0 and self.T % (self.stride // self.late) == 0
        assert self.B * self.per == 128 and self.groups * self.per == self.rd and self.F == 128
        assert self.C % 2 == 0 and self.R % 2 == 0 and self.YB % 2 == 0 and self.rd >= 4 and self.cd >= 2 and self.lanes == 128
        assert self.height == self.R * self.h and self.width == self.C * self.w


def split_kernel(z, images_hbm, out_hbm, images_ref, rows_ref, pad_ref, pick_ref, out_ref, in_sem, out_sems):
    load = pltpu.make_async_copy(images_hbm, images_ref, in_sem)
    load.start()
    margin = PAD // S
    blocks = z.height // S
    n = lax.broadcasted_iota(jnp.int32, (1, z.C * z.lanes), 1)
    column = n // z.lanes
    inner = n % z.lanes
    lane_row = inner // z.stride
    across = inner % z.stride
    source = jnp.where(across < z.ext, z.w * column - PAD + across, -1)
    pixel = lax.broadcasted_iota(jnp.int32, (128, z.C * z.lanes), 0)
    chunks = rows_ref.shape[1]
    for k in range(chunks):
        for j in range(S):
            wanted = jnp.where(lane_row == j, source - 128 * k, -1)
            pick_ref[k, j] = (pixel == wanted).astype(f32).astype(bf16)
    rows_ref[...] = jnp.zeros_like(rows_ref)
    pad_ref[...] = jnp.zeros_like(pad_ref)
    inside = (source >= 0) & (source < z.width)
    load.wait()
    for i in range(z.bd):
        pixels = images_ref[i].astype(f32)
        for k in range(chunks):
            stop = min(128, z.width - 128 * k)
            rows_ref[:, k, :, :stop] = pixels[:, :, 128 * k : 128 * k + stop]
        total = jnp.zeros((CH * blocks, z.C * z.lanes), f32)
        for k in range(chunks):
            for j in range(S):
                line = jnp.concatenate(
                    [rows_ref[c, k, pl.ds(j, blocks, stride=S), :] for c in range(CH)], axis=0
                ).astype(bf16)
                total = total + dot(line, pick_ref[k, j])
        count = CH * z.height * z.width
        center = jnp.sum(pixels) / count
        variance = jnp.sum(jnp.square(pixels - center)) / count
        total = jnp.where(inside, (total - center) / jnp.sqrt(variance + 1e-05), 0.0)
        for c in range(CH):
            pad_ref[i, c, margin : margin + blocks, :] = total[c * blocks : (c + 1) * blocks]
    copies = []
    for r in range(z.R):
        parts = [
            pad_ref[i, c, z.rd * r : z.rd * r + z.YB, q * z.lanes : (q + 1) * z.lanes]
            for q in range(z.C)
            for i in range(z.bd)
            for c in range(CH)
        ]
        for k in range(0, len(parts), 2 * CH):
            pair = jnp.concatenate(parts[k : k + 2 * CH], axis=0)
            out_ref[r, k * z.YB : (k + 2 * CH) * z.YB, :] = pair.astype(bf16)
        copy = pltpu.make_async_copy(out_ref.at[r], out_hbm.at[r], out_sems.at[r])
        copy.start()
        copies.append(copy)
    for copy in copies:
        copy.wait()


def split(z, images):
    shape = (z.R, z.C * z.bd * z.T, z.lanes)
    return pl.pallas_call(
        functools.partial(split_kernel, z),
        out_shape=pltpu.HBM(shape, bf16),
        in_specs=[pl.BlockSpec(memory_space=pltpu.HBM)],
        out_specs=pl.BlockSpec(memory_space=pltpu.HBM),
        scratch_shapes=[
            pltpu.VMEM((z.bd, CH, z.height, z.width), bf16),
            pltpu.VMEM((CH, -(-z.width // 128), z.height, 128), f32),
            pltpu.VMEM((z.bd, CH, z.height // S + 2 * PAD // S, z.C * z.lanes), f32),
            pltpu.VMEM((-(-z.width // 128), S, 128, z.C * z.lanes), bf16),
            pltpu.VMEM(shape, bf16),
            pltpu.SemaphoreType.DMA,
            pltpu.SemaphoreType.DMA((z.R,)),
        ],
        compiler_params=pltpu.CompilerParams(vmem_limit_bytes=32 * MIB),
    )(pltpu.with_memory_space_constraint(images, pltpu.HBM))


def spread_kernel(z, weights_ref, out_ref, rows_ref):
    row = lax.broadcasted_iota(jnp.int32, (z.stride, z.F), 0)
    for q in range(z.cd):
        rows_ref[MARGIN : MARGIN + K, :] = weights_ref[0, q].astype(f32)
        inside = (row >= S * q) & (row < S * q + FIELD)
        for i in range(CH * FIELD):
            at = MARGIN + FIELD * i - S * q
            value = jnp.where(inside, rows_ref[at : at + z.stride, :], 0.0)
            out_ref[0, z.stride * i : z.stride * (i + 1), q * z.F : (q + 1) * z.F] = value.astype(bf16)


def spread_weights(z, weights, first, count, space):
    return pl.pallas_call(
        functools.partial(spread_kernel, z),
        grid=(count,),
        out_shape=space((count, z.KW, z.cd * z.F), bf16),
        in_specs=[pl.BlockSpec((1, z.cd, K, z.F), lambda p: (p + first, 0, 0, 0))],
        out_specs=pl.BlockSpec((1, z.KW, z.cd * z.F), lambda p: (p, 0, 0)),
        scratch_shapes=[pltpu.VMEM((K + 2 * MARGIN, z.F), f32)],
        compiler_params=pltpu.CompilerParams(vmem_limit_bytes=32 * MIB),
    )(weights)


def field(z, p, tiles_ref):
    return jnp.concatenate(
        [tiles_ref[c * z.YB + p + g] for c in range(CH) for g in range(GROUP)], axis=1
    )


def encode_kernel(
    z, moved_ref, first_ref, wide_hbm, window_ref, hidden_ref, contrib_ref, swap_ref, cross_ref, wide_ref, rows_ref, sems
):
    B = z.B
    copies = [pltpu.make_async_copy(wide_hbm.at[p], wide_ref.at[p], sems.at[p]) for p in range(z.rd - HELD)]
    for copy in copies[:2]:
        copy.start()
    rows_ref[...] = moved_ref[...].reshape(B * z.T, z.lanes).astype(f32)
    for t in range(z.T):
        window_ref[t] = rows_ref[pl.ds(t, B, stride=z.T), :].astype(bf16)
    contrib_ref[...] = jnp.zeros_like(contrib_ref)
    for first in range(0, z.rd, HELD):
        rows = range(first, min(first + HELD, z.rd))
        for p in rows:
            if p >= HELD:
                copies[p - HELD].wait()
                if p - HELD + 2 < len(copies):
                    copies[p - HELD + 2].start()
        weight = [first_ref.at[p] if p < HELD else wide_ref.at[p - HELD] for p in rows]
        hidden = [dot(field(z, p, window_ref), w[...]).astype(bf16) for p, w in zip(rows, weight)]
        terms = [dot(h, w[...], NT) for h, w in zip(hidden, weight)]
        for p, h, value in zip(rows, hidden, terms):
            for q in range(z.cd):
                hidden_ref[p, q] = h[:, q * z.F : (q + 1) * z.F]
            for c in range(CH):
                for g in range(GROUP):
                    at = (c * GROUP + g) * z.lanes
                    contrib_ref[c * z.YB + p + g] += value[:, at : at + z.lanes]
    half = z.YB // 2
    even = row_is_even()
    for ref, below in ((swap_ref, even), (cross_ref, jnp.logical_not(even))):
        first = jnp.where(below, z.YB - half, 0)
        row = jnp.where(below, z.rd - 2, 0)
        for c in range(CH):
            for y in range(half):
                ref[c * half + y] = contrib_ref[c * z.YB + first + y].astype(bf16)
        for i in range(2):
            for q in range(z.cd):
                ref[CH * half + i * z.cd + q] = hidden_ref[row + i, q]


def encode(z, moved, first, wide):
    B, L = z.B, z.lanes
    vmem = pl.BlockSpec(memory_space=pltpu.VMEM)
    sent = CH * (z.YB // 2) + 2 * z.cd
    shapes = [
        ((z.T, B, L), bf16),
        ((z.rd, z.cd, B, z.F), bf16),
        ((z.T, B, L), f32),
        ((sent, B, L), bf16),
        ((sent, B, L), bf16),
        ((z.rd - HELD, z.KW, z.cd * z.F), bf16),
    ]
    return pl.pallas_call(
        functools.partial(encode_kernel, z),
        out_shape=[pltpu.VMEM(*s) for s in shapes],
        in_specs=[vmem, vmem, pl.BlockSpec(memory_space=pltpu.HBM)],
        out_specs=[vmem] * len(shapes),
        scratch_shapes=[
            pltpu.VMEM((B * z.T, L), f32),
            pltpu.SemaphoreType.DMA((z.rd - HELD,)),
        ],
        compiler_params=pltpu.CompilerParams(vmem_limit_bytes=32 * MIB),
    )(moved, first, pltpu.with_memory_space_constraint(wide, pltpu.HBM))


def turn_fields(z, tile_of, flat_ref):
    for group in range(z.groups):
        for c in range(CH):
            for g in range(GROUP):
                first = c * z.YB + group * z.per + g
                stack = jnp.concatenate([tile_of(first + p) for p in range(z.per)], axis=0)
                at = (c * GROUP + g) * z.lanes
                flat_ref[group, at : at + z.lanes, :] = stack.astype(f32).T


def place_fields(z, q, c, flat_ref, dense_ref, out_ref):
    rows = slice(c * FIELD * FIELD, (c + 1) * FIELD * FIELD)
    for group in range(z.groups):
        for i in range(c * FIELD, (c + 1) * FIELD):
            at = z.stride * i + S * q
            dense_ref[FIELD * i : FIELD * (i + 1), :] = flat_ref[group, at : at + FIELD, :]
        out_ref[group, rows, :] = dense_ref[rows, :].astype(bf16)


def patches_kernel(z, window_ref, out_ref, flat_ref, dense_ref):
    turn_fields(z, lambda t: window_ref[t], flat_ref)
    for q in range(z.cd):
        for c in range(CH):
            place_fields(z, q, c, flat_ref, dense_ref, out_ref.at[q])


def store_residual(z, recon_of, window_ref, resid_ref):
    lane = lax.broadcasted_iota(jnp.int32, (1, z.lanes), 1) % z.stride
    x = lax.axis_index("col") * z.w - PAD + lane
    across = ((x >= 0) & (x < z.width)).astype(f32)
    first = lax.axis_index("row") * z.h - PAD
    for t in range(0, z.T, 2):
        recon = recon_of(t)
        for n in range(2):
            line = first + S * ((t + n) % z.YB)
            inside = jnp.where((line >= 0) & (line < z.height), across, 0.0)
            resid_ref[t + n] = ((recon[n] - window_ref[t + n].astype(f32)) * inside).astype(bf16)


def fill_factor(z, q, resid_ref, pooled_ref, hidden_ref, first_ref, wide_ref, factor_ref):
    B, F = z.B, z.F
    factor_ref[...] = jnp.zeros_like(factor_ref)
    for p in range(z.rd):
        weight = first_ref.at[p] if p < HELD else wide_ref.at[p - HELD]
        back = dot(field(z, p, resid_ref), weight[:, q * F : (q + 1) * F])
        group, at = p // z.per, p % z.per * B
        columns = slice(p % z.per * F, (p % z.per + 1) * F)
        factor_ref[group, at : at + B, columns] = (pooled_ref[p, q] + back).astype(bf16)
        factor_ref[group, 128 + at : 128 + at + B, columns] = hidden_ref[p, q]


def vmem_call(kernel, shapes, scratch, *args):
    vmem = pl.BlockSpec(memory_space=pltpu.VMEM)
    return pl.pallas_call(
        kernel,
        out_shape=[pltpu.VMEM(*s) for s in shapes],
        in_specs=[vmem] * len(args),
        out_specs=[vmem] * len(shapes),
        scratch_shapes=[pltpu.VMEM(*s) for s in scratch],
        compiler_params=pltpu.CompilerParams(vmem_limit_bytes=32 * MIB),
    )(*args)


def is_even():
    return lax.rem(lax.axis_index("col"), 2) == 0


def row_is_even():
    return lax.rem(lax.axis_index("row"), 2) == 0


def pack_side(z, to_right, first, second):
    wide = 2 * PAD
    across = lax.broadcasted_iota(jnp.int32, first.shape, 1) % z.stride
    low = pltpu.roll(first, jnp.where(to_right, z.lanes - z.w, 0), 1)
    high = pltpu.roll(second, jnp.where(to_right, z.lanes - z.w + wide, wide) % z.lanes, 1)
    return jnp.where(across < wide, low, jnp.where(across < 2 * wide, high, 0.0))


def unpack_side(z, from_left, packed):
    wide = 2 * PAD
    across = lax.broadcasted_iota(jnp.int32, packed.shape, 1) % z.stride
    start = jnp.where(from_left, 0, z.w)
    inside = (across >= start) & (across < start + wide)
    first = pltpu.roll(packed, start, 1)
    second = pltpu.roll(packed, (start + z.lanes - wide) % z.lanes, 1)
    return jnp.where(inside, first, 0.0), jnp.where(inside, second, 0.0)


def pack_late(z, to_right, tiles):
    across = lax.broadcasted_iota(jnp.int32, tiles[0].shape, 1) % z.stride
    start = jnp.where(to_right, 2 * z.w, 0)
    packed = jnp.zeros_like(tiles[0])
    for k, tile in enumerate(tiles):
        at = k * z.late
        turned = pltpu.roll(tile, (z.lanes + at - start) % z.lanes, 1)
        packed = jnp.where((across >= at) & (across < at + z.late), turned, packed)
    return packed


def unpack_late(z, from_left, packed, k):
    across = lax.broadcasted_iota(jnp.int32, packed.shape, 1) % z.stride
    start = jnp.where(from_left, 0, 2 * z.w)
    turned = pltpu.roll(packed, (z.lanes + start - k * z.late) % z.lanes, 1)
    return jnp.where((across >= start) & (across < start + z.late), turned, 0.0)


def rows_kernel(
    z, contrib_ref, hidden_ref, swap_ref, cross_ref, sum_ref, tall_ref, near_ref, far_ref, late_ref
):
    half = z.YB // 2
    row = lax.axis_index("row")
    even_row = row_is_even()
    above_exists, below_exists = row > 0, row < z.R - 1
    for ref, below in ((swap_ref, even_row), (cross_ref, jnp.logical_not(even_row))):
        exists = jnp.where(below, below_exists, above_exists)
        first = jnp.where(below, z.YB - half, 0)
        for c in range(CH):
            for y in range(half):
                t = c * z.YB + first + y
                sum_ref[t] = contrib_ref[t] + jnp.where(exists, ref[c * half + y].astype(f32), 0.0)
    even = is_even()
    odd = jnp.logical_not(even)
    for t in range(0, z.T, 2):
        pair = sum_ref[t], sum_ref[t + 1]
        far_ref[t // 2] = pack_side(z, odd, *pair).astype(bf16)
        near_ref[t // 2] = pack_side(z, even, *pair).astype(bf16)
    slots = z.stride // z.late
    for t in range(0, z.T, slots):
        late_ref[t // slots] = pack_late(z, even, [sum_ref[t + k] for k in range(slots)]).astype(bf16)
    for q in range(z.cd):
        squares = [jnp.square(hidden_ref[i, q].astype(f32)) for i in range(z.rd)]
        above, below = [], []
        for i in range(2):
            swapped = swap_ref[CH * half + i * z.cd + q].astype(f32)
            crossed = cross_ref[CH * half + i * z.cd + q].astype(f32)
            upper = jnp.where(above_exists, jnp.where(even_row, crossed, swapped), 0.0)
            lower = jnp.where(below_exists, jnp.where(even_row, swapped, crossed), 0.0)
            above.append(jnp.square(upper))
            below.append(jnp.square(lower))
        squares = above + squares + below
        for i in range(z.rd + 2):
            tall_ref[i, q] = squares[i] + squares[i + 1] + squares[i + 2]
    for ref, right in ((near_ref, even), (far_ref, odd)):
        first = jnp.where(right, z.cd - 2, 0)
        for i in range(z.rd + 2):
            for k in range(2):
                ref[z.T // 2 + 2 * i + k] = tall_ref[i, first + k].astype(bf16)


def merge_kernel(
    z, sum_ref, near_ref, far_ref, late_ref, window_ref, hidden_ref, tall_ref, first_ref, wide_ref,
    out_ref, patch_ref, factor_ref, pooled_ref, resid_ref, flat_ref, dense_ref, wide_edge_ref, inverse_ref,
):
    even = is_even()
    col = lax.axis_index("col")
    exists = jnp.where(even, col > 0, col < z.C - 1)
    late_exists = jnp.where(even, col > 1, col < z.C - 2)
    slots = z.stride // z.late

    def recon_of(t):
        near = unpack_side(z, jnp.logical_not(even), near_ref[t // 2].astype(f32))
        came = unpack_side(z, even, jnp.where(exists, far_ref[t // 2].astype(f32), 0.0))
        late = jnp.where(late_exists, late_ref[t // slots].astype(f32), 0.0)
        recon = []
        for k in range(2):
            recon.append(sum_ref[t + k] + near[k] + came[k] + unpack_late(z, even, late, t % slots + k))
            out_ref[t + k] = recon[k]
        return recon

    pool_kernel(z, hidden_ref, tall_ref, near_ref, far_ref, pooled_ref, wide_edge_ref, inverse_ref)
    store_residual(z, recon_of, window_ref, resid_ref)
    turn_fields(z, lambda t: resid_ref[t], flat_ref)
    fill_factor(z, z.early, resid_ref, pooled_ref, hidden_ref, first_ref, wide_ref, factor_ref)
    for c in range(CH):
        place_fields(z, z.early, c, flat_ref, dense_ref, patch_ref)


def unpack_last(z, packed):
    even = is_even()
    col = lax.axis_index("col")
    exists = jnp.where(even, col + 1 < z.C - 1, col - 1 > 0)
    across = lax.broadcasted_iota(jnp.int32, packed.shape, 1) % z.stride
    start = jnp.where(even, 2 * z.w, 0)
    inside = (across >= start) & (across < start + z.late) & exists
    by = jnp.where(even, 2 * z.w, z.lanes - z.w)
    first = pltpu.roll(packed, by, 1)
    second = pltpu.roll(packed, (by + z.lanes - 2 * PAD) % z.lanes, 1)
    return jnp.where(inside, first, 0.0), jnp.where(inside, second, 0.0)


def pool_kernel(z, hidden_ref, tall_ref, near_ref, far_ref, out_ref, wide_ref, inverse_ref):
    even = is_even()
    row0 = lax.axis_index("row") * z.rd - 1
    col0 = lax.axis_index("col") * z.cd - 1
    near_at = jnp.where(even, z.cd + 2, 0)
    far_at = jnp.where(even, 0, z.cd + 2)
    exists = jnp.where(even, lax.axis_index("col") > 0, lax.axis_index("col") < z.C - 1)
    for i in range(z.rd + 2):
        for k in range(2):
            wide_ref[near_at + k] = near_ref[z.T // 2 + 2 * i + k].astype(f32)
            wide_ref[far_at + k] = jnp.where(exists, far_ref[z.T // 2 + 2 * i + k].astype(f32), 0.0)
        for q in range(z.cd):
            wide_ref[2 + q] = tall_ref[i, q]
        columns = [wide_ref[q] for q in range(z.cd + 4)]
        for q in range(z.cd + 2):
            energy = jnp.sqrt(1.0 + (columns[q] + columns[q + 1] + columns[q + 2]))
            inverse = (1.0 / energy).astype(bf16).astype(f32)
            row, col = row0 + i, col0 + q
            inside = (row >= 0) & (row < z.R * z.rd) & (col >= 0) & (col < z.C * z.cd)
            inverse_ref[i, q] = inverse * jnp.where(inside, 1.0, 0.0)
    for i in range(z.rd):
        columns = []
        for q in range(z.cd + 2):
            columns.append(inverse_ref[i, q] + inverse_ref[i + 1, q] + inverse_ref[i + 2, q])
        for q in range(z.cd):
            spread = columns[q] + columns[q + 1] + columns[q + 2]
            out_ref[i, q] = sparsity * hidden_ref[i, q].astype(f32) * spread


def grad_kernel(
    z, sum_ref, last_ref, window_ref, patch_ref, hidden_ref, pooled_ref, first_ref, wide_ref,
    early_patch_ref, early_factor_ref,
    out_hbm, resid_ref, flat_ref, dense_ref, resid_patch_ref, factor_ref, out_ref, sems,
):
    B, F = z.B, z.F
    copies = []

    def write(q, k, resid_patch, factor):
        rows = slice(k * FIELD * FIELD, (k + 1) * FIELD * FIELD)
        for group in range(z.groups):
            both = jnp.concatenate([patch_ref[q, group, rows, :], resid_patch[group, rows, :]], axis=1)
            value = dot(both, factor[group]) * (1.0 / B)
            for inner in range(z.per):
                out_ref[group * z.per + inner, q, rows, :] = value[:, inner * F : (inner + 1) * F]
        copy = pltpu.make_async_copy(out_ref.at[:, q, rows, :], out_hbm.at[:, q, rows, :], sems.at[q, k])
        copy.start()
        copies.append(copy)

    for k in range(CH):
        write(z.early, k, early_patch_ref, early_factor_ref)

    def recon_of(t):
        came = unpack_last(z, last_ref[t // 2].astype(f32))
        return [sum_ref[t + k] + came[k] for k in range(2)]

    store_residual(z, recon_of, window_ref, resid_ref)
    turn_fields(z, lambda t: resid_ref[t], flat_ref)
    for q in range(z.cd):
        if q == z.early:
            continue
        fill_factor(z, q, resid_ref, pooled_ref, hidden_ref, first_ref, wide_ref, factor_ref.at[q])
        for k in range(CH):
            place_fields(z, q, k, flat_ref, dense_ref, resid_patch_ref.at[q])
            write(q, k, resid_patch_ref.at[q], factor_ref.at[q])
    for copy in copies:
        copy.wait()


def gradient(z, *args):
    B, F, L = z.B, z.F, z.lanes
    return pl.pallas_call(
        functools.partial(grad_kernel, z),
        out_shape=pltpu.HBM((z.rd, z.cd, K, F), f32),
        in_specs=[pl.BlockSpec(memory_space=pltpu.VMEM)] * len(args),
        out_specs=pl.BlockSpec(memory_space=pltpu.HBM),
        scratch_shapes=[
            pltpu.VMEM((z.T, B, L), bf16),
            pltpu.VMEM((z.groups, z.KW, 128), f32),
            pltpu.VMEM((K, 128), f32),
            pltpu.VMEM((z.cd, z.groups, K, 128), bf16),
            pltpu.VMEM((z.cd, z.groups, 256, z.per * F), bf16),
            pltpu.VMEM((z.rd, z.cd, K, F), f32),
            pltpu.SemaphoreType.DMA((z.cd, CH)),
        ],
        compiler_params=pltpu.CompilerParams(vmem_limit_bytes=40 * MIB),
    )(*args)


def exchange(z, value, partner):
    pairs = []
    for r in range(z.R):
        for c in range(z.C):
            to = partner(z, r, c)
            pairs.append((r * z.C + c, to[0] * z.C + to[1]))
    return lax.ppermute(value, ("row", "col"), pairs)


def shift(z, value):
    pairs = []
    for r in range(z.R):
        for c in range(z.C):
            to = (c + (-2 if c % 2 else 2)) % z.C
            pairs.append((r * z.C + c, r * z.C + to))
    return lax.ppermute(value, ("row", "col"), pairs)


def cross_row(z, r, c):
    to = r + 1 if r % 2 else r - 1
    return (to, c) if 0 <= to < z.R else (r, c ^ 1)


def swap_col(z, r, c):
    return (r, c ^ 1)


def cross_col(z, r, c):
    to = c + 1 if c % 2 else c - 1
    return (r, to) if 0 <= to < z.C else (r ^ 1, c)


def body(z, images, weights):
    B, L = z.B, z.lanes
    tiles = ((z.T, B, L), f32)
    blocks = split(z, images)
    moved = lax.all_to_all(
        blocks.reshape(z.R * z.C, z.bd * z.T, L), ("row", "col"), split_axis=0, concat_axis=0, tiled=True
    ).reshape(B, z.T, L)
    turned = jnp.swapaxes(weights, 2, 3)
    wide_first = spread_weights(z, turned, 0, HELD, pltpu.VMEM)
    wide = spread_weights(z, turned, HELD, z.rd - HELD, pltpu.HBM)
    window, hidden, contrib, to_swap, to_cross, wide = encode(z, moved, wide_first, wide)
    crossed = exchange(z, to_cross, cross_row)
    swapped = exchange(z, to_swap, lambda z, r, c: (r ^ 1, c))
    tall = ((z.rd + 2, z.cd, B, z.F), f32)
    sent = ((z.T // 2 + 2 * (z.rd + 2), B, L), bf16)
    late = ((z.T * z.late // z.stride, B, L), bf16)
    total, tall, to_near, to_far, to_late = vmem_call(
        functools.partial(rows_kernel, z), [tiles, tall, sent, sent, late], [], contrib, hidden, swapped, crossed
    )
    far = exchange(z, to_far, cross_col)
    late = shift(z, to_late)
    near = exchange(z, to_near, swap_col)
    (patch,) = vmem_call(
        functools.partial(patches_kernel, z),
        [((z.cd, z.groups, K, 128), bf16)],
        [((z.groups, z.KW, 128), f32), ((K, 128), f32)],
        window,
    )
    far, near, late, patch = lax.optimization_barrier((far, near, late, patch))
    last = exchange(z, far[: z.T // 2], swap_col)
    total, early_patch, early_factor, pooled = vmem_call(
        functools.partial(merge_kernel, z),
        [
            tiles,
            ((z.groups, K, 128), bf16),
            ((z.groups, 256, z.per * z.F), bf16),
            ((z.rd, z.cd, B, z.F), f32),
        ],
        [
            ((z.T, B, L), bf16),
            ((z.groups, z.KW, 128), f32),
            ((K, 128), f32),
            ((z.cd + 4, B, z.F), f32),
            ((z.rd + 2, z.cd + 2, B, z.F), f32),
        ],
        total, near, far, late, window, hidden, tall, wide_first, wide,
    )
    out = gradient(
        z, total, last, window, patch, hidden, pooled, wide_first, wide, early_patch, early_factor
    )
    return jnp.swapaxes(out, 2, 3)


def solution(mesh):
    def run(images, weights):
        z = Sizes(
            (images.shape[0] // (mesh.shape["row"] * mesh.shape["col"]),) + images.shape[1:],
            (weights.shape[0] // mesh.shape["row"], weights.shape[1] // mesh.shape["col"]) + weights.shape[2:],
            mesh,
        )
        return jax.shard_map(
            functools.partial(body, z),
            mesh=mesh,
            in_specs=(P(("row", "col"), None, None, None), P("row", "col", None, None)),
            out_specs=P("row", "col", None, None),
            check_vma=False,
        )(images, weights)

    return run
```
